256 devices in a mesh: gx: 8 (over x, core), gy: 32 (over y, z).
Axes of the slice: x: 4, y: 4, z: 8, core: 2. Of those that a mesh axis runs over, the one named last changes fastest.
Arguments:
- state: float32 [4, 2, 256, 4096], P(None, None, 'gx', 'gy'), may hold values from -3.5 to 3.5
- diffusivity: float32 [2, 256, 4096], P(None, 'gx', 'gy'), may hold values from 1 to 4
- sea_mask: int32 [256, 4096], P('gx', 'gy'), may hold values 0 or 1
- depth_index: int32 [256, 4096], P('gx', 'gy'), may hold values from 1 to 2
- closure_in: float32 [64, 9], replicated, may hold values from -2.5 to 2.5
- closure_out: float32 [64], replicated, may hold values from -0.75 to 0.75
- cotangent: float32 [4, 2, 256, 4096], P(None, None, 'gx', 'gy'), may hold values from -6 to 6
Outputs:
- final_state: float32 [4, 2, 256, 4096], P(None, None, 'gx', 'gy')
- state_grad: float32 [4, 2, 256, 4096], P(None, None, 'gx', 'gy')
- closure_grad: float32 [64, 10], replicated
The draws below stay inside these ranges and needn't reach their ends.
All inputs are finite; a program needn't handle non-finite values. No bound on the sum of `sea_mask` on one device may be relied on, other than what follows from the above.
Results may differ from the reference program's by a relative error of at most 0.0005.
Values sent between devices are 32-bit elements; how exact they have to be, the bound alone decides.
No kernel may reach another device: no remote copies, remote signals or barrier semaphores. Data moves between devices by JAX's collectives and lax.ppermute only.
A program may use at most 64 MiB of HBM per device.

```python
import math
import jax
import jax.numpy as jnp
from jax import lax

FIELDS = 4
LEVELS = 2
STEPS = 1
HID = 64
FEAT = 8
DIFFUSE = 2048
NX = 256
NY = 4096


def draw_state(key, part):
    key = jax.random.fold_in(key, 11)
    shape = (FIELDS, LEVELS, NX, NY)
    return jax.random.truncated_normal(key, -3.5, 3.5, shape, jnp.float32)


def set_ends(values, stream_key, smallest, high):
    spot = [jax.random.randint(jax.random.fold_in(stream_key, axis), (), 0, length) for axis, length in enumerate(values.shape)]
    main_axis = values.shape.index(max(values.shape))
    neighbour = spot[:main_axis] + [(spot[main_axis] + 1) % values.shape[main_axis]] + spot[main_axis + 1:]
    return values.at[tuple(spot)].set(smallest).at[tuple(neighbour)].set(high)


def block_levels(stream_key, extent, shards, smallest, high):
    loudness, own = 1.0, jax.random.fold_in(stream_key, 6)
    for dim, blocks in shards:
        steps = jnp.exp(jax.random.uniform(jax.random.fold_in(own, dim), (blocks,), jnp.float32, smallest / len(shards), high / len(shards)))
        loudness = loudness * jnp.repeat(steps, extent[dim] // blocks).reshape([-1 if axis == dim else 1 for axis in range(len(extent))])
    return loudness


def normal_values(stream_key, extent, scale, most, pieces=(), kind=jnp.bfloat16):
    loudness = block_levels(stream_key, extent, pieces, -0.22, 0.18) if pieces else 1.0
    values = jax.random.normal(stream_key, extent, jnp.float32) * scale * loudness
    return jnp.minimum(jnp.maximum(values, -most), most).astype(kind)


def setup_inputs(seed: int = 0) -> dict:
    keys = jax.random.split(jax.random.key(seed), 8)
    state = draw_state(jax.random.fold_in(keys[7], 71), 0)
    diffusivity = jnp.clip(jnp.exp(math.log(4.0) - 1.3862944 * jax.random.uniform(keys[1], (LEVELS, NX, NY), jnp.float32) ** block_levels(keys[1], (LEVELS, NX, NY), ((1, 8), (2, 32)), -0.2, 0.2)), 1.0, 4.0)
    sea_mask = set_ends((jax.random.randint(keys[2], (NX, NY), 0, 128) < 127).astype(jnp.int32), jax.random.fold_in(keys[2], 1), 0, 1)
    depth_index = set_ends(jax.random.randint(keys[3], (NX, NY), LEVELS // 2, LEVELS + 1), jax.random.fold_in(keys[3], 1), LEVELS // 2, LEVELS).astype(jnp.int32)
    closure_in = normal_values(keys[4], (HID, FEAT + 1), 0.4, 2.5, (), jnp.float32)
    closure_out = normal_values(keys[5], (HID,), HID ** -0.5, 0.75, (), jnp.float32)
    cotangent = normal_values(keys[6], (FIELDS, LEVELS, NX, NY), 1.0, 6.0, ((2, 8), (3, 32)), jnp.float32)
    return dict(state=state, diffusivity=diffusivity, sea_mask=sea_mask, depth_index=depth_index, closure_in=closure_in, closure_out=closure_out, cotangent=cotangent)


def wet_field(sea_mask, depth_index):
    levels = jnp.arange(LEVELS, dtype=jnp.int32)[:, None, None]
    wet_bool = (levels < depth_index[None]) & (sea_mask[None] > 0)
    return jnp.where(wet_bool, 1.0, 0.0).astype(jnp.float32)

def closure_level(grads, closure_in, closure_out):
    preact = jnp.einsum('hc,cxy->hxy', closure_in[:, :FEAT], grads, precision=lax.Precision.HIGHEST)
    hidden = jnp.tanh(preact + closure_in[:, FEAT][:, None, None])
    mixed = jnp.einsum('h,hxy->xy', closure_out, hidden, precision=lax.Precision.HIGHEST)
    return 0.24 * jax.nn.sigmoid(mixed)

def explicit(padded, closure_in, closure_out, wet, coriolis):
    center = padded[:, :, 1:-1, 1:-1]
    east = padded[:, :, 2:, 1:-1]
    west = padded[:, :, :-2, 1:-1]
    north = padded[:, :, 1:-1, 2:]
    south = padded[:, :, 1:-1, :-2]
    slope_x = 0.5 * (east - west)
    slope_y = 0.5 * (north - south)
    curve_x = east - 2.0 * center + west
    curve_y = north - 2.0 * center + south
    speed_u = center[0]
    speed_v = center[1]
    upwind = speed_u * slope_x + speed_v * slope_y - 0.5 * (jnp.sqrt(speed_u * speed_u + 0.01) * curve_x + jnp.sqrt(speed_v * speed_v + 0.01) * curve_y)
    features = jnp.moveaxis(jnp.concatenate([slope_x, slope_y], 0), 1, 0)

    def level_viscosity(grads):
        return closure_level(grads, closure_in, closure_out)
    viscosity = lax.map(jax.checkpoint(level_viscosity), features)
    mixing = curve_x + curve_y
    moment_u = speed_u - 0.3 * upwind[0] + viscosity * mixing[0] + 0.3 * coriolis * speed_v
    moment_v = speed_v - 0.3 * upwind[1] + viscosity * mixing[1] - 0.3 * coriolis * speed_u
    tracers = center[2:] - 0.3 * upwind[2:]
    return wet[None] * jnp.concatenate([moment_u[None], moment_v[None], tracers], 0)

def line_solve(cond, rhs):
    cond_x = jnp.moveaxis(cond, 2, 0)
    rhs_x = jnp.moveaxis(rhs, 2, 0)
    before_x = jnp.concatenate([jnp.zeros_like(cond_x[:1]), cond_x[:-1]], 0)
    main_x = 1.0 + before_x + cond_x

    def sweep(carry, items):
        prev_ratio, prev_value = carry
        before, here, main_term, value = items
        denom = main_term + before * prev_ratio
        ratio = -here / denom
        new_value = (value + before * prev_value) / denom
        return ((ratio, new_value), (ratio, new_value))
    start = jnp.zeros(rhs_x.shape[1:], jnp.float32)
    _, (ratios, values) = lax.scan(sweep, (start, start), (before_x, cond_x, main_x, rhs_x))

    def back(next_cell, items):
        ratio, value = items
        here_cell = value - ratio * next_cell
        return (here_cell, here_cell)
    _, solved = lax.scan(back, start, (ratios, values), reverse=True)
    return jnp.moveaxis(solved, 0, 2)

def reference(state, diffusivity, sea_mask, depth_index, closure_in, closure_out, cotangent):
    wet = wet_field(sea_mask, depth_index)
    wet_next = jnp.pad(wet[:, 1:], ((0, 0), (0, 1), (0, 0)))
    rates = jnp.array([DIFFUSE, DIFFUSE, 0.5, 0.5], dtype=jnp.float32)
    cond = rates[:, None, None, None] * (diffusivity * wet * wet_next)[None]
    coriolis = 0.5 + 0.5 * jnp.arange(NY, dtype=jnp.float32) / NY

    def run(start_state, weights_in, weights_out):
        fields = start_state
        for step in range(STEPS):
            padded = jnp.pad(fields, ((0, 0), (0, 0), (1, 1), (1, 1)))
            fields = line_solve(cond, explicit(padded, weights_in, weights_out, wet, coriolis))
        return fields
    final_state, backward = jax.vjp(run, state, closure_in, closure_out)
    state_grad, grad_in, grad_out = backward(cotangent)
    factor = 1.0 / math.sqrt(LEVELS * NX * NY)
    closure_grad = jnp.concatenate([grad_in, grad_out[:, None]], 1) * factor
    return (final_state, state_grad, closure_grad)
```

```python
import math

import jax
import jax.numpy as jnp
from jax import lax
from jax.experimental import pallas as pl
from jax.experimental.pallas import tpu as pltpu
from jax.sharding import PartitionSpec as P

F32 = jnp.float32
BF16 = jnp.bfloat16
DIFFUSE = 2048.0
FEAT = 8
HID = 64
NX = 32
NY = 128
ROWS = 8
XS = 4
RIM = 80


def iota(shape, dim):
    return lax.broadcasted_iota(jnp.int32, shape, dim)


def rows8():
    return iota((ROWS, NY), 0)


def lanes8():
    return iota((ROWS, NY), 1)


def wide(row):
    return jnp.broadcast_to(row, (ROWS, NY))


def by_level(first, second):
    return jnp.where((rows8() & 1) == 0, wide(first), wide(second))


def line(ref, x):
    return ref[pl.ds(x, ROWS, stride=NX), :]


def wet_line(sea_ref, depth_ref, x):
    sea = wide(sea_ref[x : x + 1, :])
    depth = wide(depth_ref[x : x + 1, :])
    return jnp.where(((rows8() & 1) < depth) & (sea > 0), 1.0, 0.0).astype(F32)


def rates8():
    return jnp.where(rows8() < 4, DIFFUSE, 0.5).astype(F32)


def split(values):
    high = values.astype(BF16)
    return high, (values - high.astype(F32)).astype(BF16)


def columns_kernel(state_ref, first_ref, last_ref):
    lanes = lanes8()
    first = jnp.zeros((ROWS, NY), F32)
    last = jnp.zeros((ROWS, NY), F32)
    for x in range(NX):
        here = line(state_ref, x)
        first = jnp.where(lanes == x, pltpu.roll(here, x, 1) if x else here, first)
        last = jnp.where(lanes == x, pltpu.roll(here, x + 1, 1), last)
    first_ref[...] = first
    last_ref[...] = last


def factor_kernel(
    state_ref, diff_ref, sea_ref, depth_ref, cot_ref, send_ref, right_ref, recip_ref, left_ref
):
    me = lax.axis_index("gx")
    count = send_ref.shape[0]
    row = rows8()
    wet = [wet_line(sea_ref, depth_ref, x) for x in range(NX)]
    rates = rates8()
    bare = [
        by_level(diff_ref[x : x + 1, :], diff_ref[NX + x : NX + x + 1, :]) * wet[x]
        for x in range(NX)
    ]
    cond = [rates * bare[x] * wet[x + 1] for x in range(NX - 1)]
    mass = jnp.ones((ROWS, NY), F32)
    carry = jnp.ones((ROWS, NY), F32)
    load = line(cot_ref, 0)
    mass_back = jnp.ones((ROWS, NY), F32)
    load_back = line(cot_ref, NX - 1)
    for i in range(NX - 1):
        recip = 1.0 / (mass + cond[i])
        ratio = cond[i] * recip
        right_ref[i] = ratio
        recip_ref[i] = recip
        mass = 1.0 + mass * ratio
        load = line(cot_ref, i + 1) + ratio * load
        carry = carry * ratio
        j = NX - 2 - i
        ratio_back = cond[j] / (mass_back + cond[j])
        left_ref[j] = ratio_back
        mass_back = 1.0 + mass_back * ratio_back
        load_back = line(cot_ref, j) + ratio_back * load_back
    last_self = 1.0 / mass
    first_self = 1.0 / mass_back
    right_ref[NX - 1] = jnp.zeros((ROWS, NY), F32)
    left_ref[NX - 1] = jnp.zeros((ROWS, NY), F32)
    recip_ref[NX - 1] = last_self
    across = carry * last_self
    upper = (row & 2) == 0
    tiles = [
        load_back * first_self,
        load * last_self,
        jnp.where(upper, first_self, across),
        jnp.where(upper, last_self, jnp.where(row < 4, bare[NX - 1], wet[0])),
    ]
    own_last = line(state_ref, NX - 1)
    own_first = line(state_ref, 0)
    for j in range(count):
        for n, tile in enumerate(tiles):
            send_ref[j, ROWS * n : ROWS * (n + 1), :] = tile
        send_ref[j, ROWS * 4 :, :] = jnp.where(j > me, own_last, own_first)


def reduced(got_ref):
    count = got_ref.shape[0]
    upper = (rows8() & 2) == 0
    first_self, across, last_self, bare, wet = [], [], [], [], []
    for j in range(count):
        tile = got_ref[j, 16:24, :]
        first_self.append(jnp.where(upper, tile, pltpu.roll(tile, 2, 0)))
        across.append(jnp.where(upper, pltpu.roll(tile, 6, 0), tile))
        tile = got_ref[j, 24:32, :]
        last_self.append(jnp.where(upper, tile, pltpu.roll(tile, 2, 0)))
        bare.append(by_level(got_ref[j, 26:27, :], got_ref[j, 27:28, :]))
        wet.append(by_level(got_ref[j, 30:31, :], got_ref[j, 31:32, :]))
    face = [rates8() * bare[j] * wet[j + 1] for j in range(count - 1)]
    return first_self, across, last_self, face


def end_fluxes(system, first, last, me):
    first_self, across, last_self, face = system
    count = len(first_self)
    zero = jnp.zeros((ROWS, NY), F32)
    give, value = last_self[0], last[0]
    gives, values, links = [give], [value], [zero]
    for j in range(1, count):
        link = face[j - 1] / (1.0 + face[j - 1] * (give + first_self[j]))
        pull = across[j] * link
        value = last[j] + pull * (value - first[j])
        give = last_self[j] - pull * across[j]
        gives.append(give)
        values.append(value)
        links.append(link)
    back_give, back_value = first_self[count - 1], first[count - 1]
    right_flux = [None] * count
    right_flux[count - 1] = zero
    for j in range(count - 2, -1, -1):
        right_flux[j] = (
            face[j] * (back_value - values[j]) / (1.0 + face[j] * (back_give + gives[j]))
        )
        link = face[j] / (1.0 + face[j] * (back_give + last_self[j]))
        pull = across[j] * link
        back_value = first[j] + pull * (back_value - last[j])
        back_give = first_self[j] - pull * across[j]
    left, right = zero, right_flux[0]
    for j in range(1, count):
        here = links[j] * (values[j - 1] - first[j] - across[j] * right_flux[j])
        left = jnp.where(me == j, here, left)
        right = jnp.where(me == j, right_flux[j], right)
    return left, right


def own_lines(read, right_ref, recip_ref, fluxes, write):
    left, right = fluxes
    load = read(0) + left
    loads = [load]
    for i in range(1, NX):
        load = read(i) + right_ref[i - 1] * load
        loads.append(load)
    value = (loads[NX - 1] + right) * recip_ref[NX - 1]
    write(NX - 1, value)
    for i in range(NX - 2, -1, -1):
        value = right_ref[i] * value + recip_ref[i] * loads[i]
        write(i, value)


def network(weights_ref, out_ref):
    weights = weights_ref[...]
    where_to = []
    for level in range(2):
        spread = (iota((FEAT + 1, 128), 1) == 2 * iota((FEAT + 1, 128), 0) + level) & (
            iota((FEAT + 1, 128), 0) < FEAT
        )
        where_to.append(
            jnp.dot(
                weights,
                spread.astype(F32),
                precision=lax.Precision.HIGHEST,
                preferred_element_type=F32,
            )
        )
    both = jnp.concatenate(where_to, 0)
    high = both.astype(BF16).astype(F32)
    low = both - high
    bias = weights[:, FEAT : FEAT + 1]
    bias = jnp.broadcast_to(jnp.concatenate([bias, bias], 0), (2 * HID, 128))
    bias_high = bias.astype(BF16).astype(F32)
    bias_mid = (bias - bias_high).astype(BF16).astype(F32)
    bias_low = bias - bias_high - bias_mid
    lane = iota((2 * HID, 128), 1)
    forward = high + pltpu.roll(high, 16, 1) + pltpu.roll(low, 48, 1) + pltpu.roll(low, 64, 1)
    forward = jnp.where(lane == 32, bias_high, forward)
    forward = jnp.where(lane == 33, bias_mid, forward)
    forward = jnp.where(lane == 34, bias_low, forward)
    turned = jnp.transpose(high + pltpu.roll(low, 16, 1))[:32]
    back = jnp.concatenate([turned, turned], 1)
    out = out_ref[...]
    out = jnp.broadcast_to(jnp.concatenate([out, out], 0), (2 * HID, 128))
    return forward.astype(BF16), back.astype(BF16), out


def main_kernel(
    got_ref,
    low_ref,
    high_ref,
    state_ref,
    sea_ref,
    depth_ref,
    cot_ref,
    right_ref,
    recip_ref,
    left_ref,
    weights_ref,
    out_ref,
    send_ref,
    grad_ref,
    rims_ref,
    rhs_ref,
    fields,
    wets,
    adj,
    slope_x,
    slope_y,
    curve_x,
    curve_y,
    feats,
    forward_ref,
    back_ref,
    outw_ref,
    sums_ref,
    out_sums_ref,
):
    me = lax.axis_index("gx")
    here_y = lax.axis_index("gy")
    count = got_ref.shape[0]
    total_y = NY * lax.axis_size("gy")
    lanes = lanes8()
    row = rows8()
    zero = jnp.zeros((ROWS, NY), F32)

    for x in range(NX):
        wets[x] = wet_line(sea_ref, depth_ref, x)
        fields[x + 1] = line(state_ref, x)
    below = got_ref[jnp.maximum(me - 1, 0), 32:40, :]
    above = got_ref[jnp.minimum(me + 1, count - 1), 32:40, :]
    fields[0] = jnp.where(me > 0, below, zero)
    fields[NX + 1] = jnp.where(me < count - 1, above, zero)

    system = reduced(got_ref)
    first = [got_ref[j, 0:8, :] for j in range(count)]
    last = [got_ref[j, 8:16, :] for j in range(count)]
    fluxes = end_fluxes(system, first, last, me)

    def keep(x, value):
        adj[x] = wets[x] * value

    own_lines(lambda x: line(cot_ref, x), right_ref, recip_ref, fluxes, keep)

    low = low_ref[...]
    high = high_ref[...]
    feats[32:48, :] = jnp.ones((16, NX * NY), BF16)
    for x in range(NX):
        center = fields[x + 1]
        east = fields[x + 2]
        west = fields[x]
        south = jnp.where(lanes == 0, pltpu.roll(low, (-x) % NY, 1) if x else low, pltpu.roll(center, 1, 1))
        north = jnp.where(
            lanes == NY - 1, pltpu.roll(high, NY - 1 - x, 1), pltpu.roll(center, NY - 1, 1)
        )
        sx = 0.5 * (east - west)
        sy = 0.5 * (north - south)
        slope_x[x] = sx
        slope_y[x] = sy
        curve_x[x] = east - 2.0 * center + west
        curve_y[x] = north - 2.0 * center + south
        part_high, part_low = split(jnp.concatenate([sx, sy], 0))
        place = slice(x * NY, (x + 1) * NY)
        feats[0:16, place] = part_high
        feats[16:32, place] = part_low
        feats[48:64, place] = part_high
        feats[64:80, place] = part_low

    forward, back, outw = network(weights_ref, out_ref)
    forward_ref[...] = forward
    back_ref[...] = back
    outw_ref[...] = outw
    sums_ref[...] = jnp.zeros(sums_ref.shape, F32)
    out_sums_ref[...] = jnp.zeros(out_sums_ref.shape, F32)
    grad_ref[...] = jnp.zeros(grad_ref.shape, F32)
    rims_ref[...] = jnp.zeros(rims_ref.shape, F32)
    places = (here_y * NY + lanes).astype(F32)
    turn = 0.3 * (0.5 + 0.5 * places / total_y)
    moment = row < 4

    @pl.loop(0, NX // XS)
    def _(step):
        base = step * XS
        place = pl.ds(pl.multiple_of(base * NY, XS * NY), XS * NY)
        hidden = jnp.tanh(
            jnp.dot(forward_ref[:, 0:80], feats[0:80, place], preferred_element_type=F32)
        )
        outw = outw_ref[...]
        sharp, keepers = [], []
        for i in range(XS):
            x = base + i
            unit = hidden[:, i * NY : (i + 1) * NY]
            weighed = unit * outw
            mixed = by_level(
                jnp.sum(weighed[:HID], 0, keepdims=True), jnp.sum(weighed[HID:], 0, keepdims=True)
            )
            gate = 1.0 / (1.0 + jnp.exp(-mixed))
            nu = jnp.where(moment, 0.24 * gate, 0.0)
            center = fields[x + 1]
            sx, sy, cx, cy = slope_x[x], slope_y[x], curve_x[x], curve_y[x]
            u = by_level(center[0:1], center[1:2])
            v = by_level(center[2:3], center[3:4])
            speed_u = jnp.sqrt(u * u + 0.01)
            speed_v = jnp.sqrt(v * v + 0.01)
            upwind = u * sx + v * sy - 0.5 * (speed_u * cx + speed_v * cy)
            twist = jnp.where(
                row < 2, pltpu.roll(center, 6, 0), jnp.where(moment, -pltpu.roll(center, 2, 0), 0.0)
            )
            rhs_ref[x] = wets[x] * (center - 0.3 * upwind + nu * (cx + cy) + turn * twist)
            g = adj[x]
            to_gate = jnp.where(moment, g * (cx + cy) * (0.24 * gate * (1.0 - gate)), 0.0)
            to_gate = to_gate + pltpu.roll(to_gate, 6, 0)
            gate_level = jnp.concatenate(
                [
                    jnp.broadcast_to(to_gate[0:1], (HID, NY)),
                    jnp.broadcast_to(to_gate[1:2], (HID, NY)),
                ],
                0,
            )
            out_sums_ref[...] += unit * gate_level
            sharp.append((1.0 - unit * unit) * (outw * gate_level))
            along_u = g * (-0.3 * sx + 0.15 * (u / speed_u) * cx)
            along_v = g * (-0.3 * sy + 0.15 * (v / speed_v) * cy)
            along_u = along_u + pltpu.roll(along_u, 4, 0)
            along_u = along_u + pltpu.roll(along_u, 2, 0)
            along_v = along_v + pltpu.roll(along_v, 4, 0)
            along_v = along_v + pltpu.roll(along_v, 2, 0)
            untwist = jnp.where(
                row < 2, along_u - turn * pltpu.roll(g, 6, 0), along_v + turn * pltpu.roll(g, 2, 0)
            )
            bend_x = g * (0.15 * speed_u + nu)
            bend_y = g * (0.15 * speed_v + nu)
            middle = g + jnp.where(moment, untwist, 0.0) - 2.0 * (bend_x + bend_y)
            keepers.append((-0.3 * u * g, -0.3 * v * g, bend_x, bend_y, middle))
        parts = split(jnp.concatenate(sharp, 1))
        stacked = jnp.concatenate(parts, 0)
        sums_ref[...] += lax.dot_general(
            stacked, feats[0:48, place], (((1,), (1,)), ((), ())), preferred_element_type=F32
        )
        to_feats = jnp.dot(back_ref[...], stacked, preferred_element_type=F32)
        to_feats = to_feats[0:16] + to_feats[16:32]
        for i in range(XS):
            x = base + i
            to_sx, to_sy, bend_x, bend_y, middle = keepers[i]
            mine = to_feats[:, i * NY : (i + 1) * NY]
            half_x = 0.5 * (to_sx + mine[0:8])
            half_y = 0.5 * (to_sy + mine[8:16])
            to_north = bend_y + half_y
            to_south = bend_y - half_y
            north = pltpu.roll(to_north, 1, 1)
            south = pltpu.roll(to_south, NY - 1, 1)
            rims_ref[0] = jnp.where(lanes == RIM + x, pltpu.roll(north, RIM + x, 1), rims_ref[0])
            rims_ref[1] = jnp.where(
                lanes == RIM + x, pltpu.roll(south, RIM + x + 1, 1), rims_ref[1]
            )
            grad_ref[x] += bend_x - half_x
            grad_ref[x + 1] += (
                middle + jnp.where(lanes == 0, 0.0, north) + jnp.where(lanes == NY - 1, 0.0, south)
            )
            grad_ref[x + 2] += bend_x + half_x

    load = rhs_ref[0]
    load_back = rhs_ref[NX - 1]
    for i in range(NX - 1):
        load = rhs_ref[i + 1] + right_ref[i] * load
        j = NX - 2 - i
        load_back = rhs_ref[j] + left_ref[j] * load_back
    first_own = load_back * jnp.where(
        (row & 2) == 0, got_ref[me, 16:24, :], pltpu.roll(got_ref[me, 16:24, :], 2, 0)
    )
    last_own = load * recip_ref[NX - 1]

    sums = sums_ref[0:128] + sums_ref[128:256]
    total = jnp.zeros((HID, 128), F32)
    for level in range(2):
        source = iota((48, 128), 0)
        target = iota((48, 128), 1)
        feature = (source < 32) & ((source & 15) == 2 * target + level) & (target < FEAT)
        gather = feature | ((source == 32) & (target == FEAT))
        total += jnp.dot(
            sums[level * HID : (level + 1) * HID],
            gather.astype(F32),
            precision=lax.Precision.HIGHEST,
            preferred_element_type=F32,
        )
    out_total = jnp.sum(out_sums_ref[0:HID] + out_sums_ref[HID:], 1, keepdims=True)
    total = jnp.where(iota((HID, 128), 1) == FEAT + 1, out_total, total)
    packed = zero
    for a in range(HID // 8):
        piece = total[8 * a : 8 * (a + 1)]
        piece = pltpu.roll(piece, 10 * a, 1) if a else piece
        packed = jnp.where((lanes >= 10 * a) & (lanes < 10 * a + 10), piece, packed)
    to_last = grad_ref[NX + 1]
    to_first = grad_ref[0]
    for j in range(count):
        send_ref[j, 0:8, :] = first_own
        send_ref[j, 8:16, :] = last_own
        send_ref[j, 16:24, :] = packed
        send_ref[j, 24:32, :] = jnp.where(j > me, to_last, to_first)


def share_kernel(second_ref, rims_ref, send_ref):
    me = lax.axis_index("gy")
    lanes = lanes8()
    total = second_ref[0, 16:24, :]
    for j in range(1, second_ref.shape[0]):
        total = total + second_ref[j, 16:24, :]
    upward = jnp.where(lanes < RIM, total, rims_ref[0])
    downward = jnp.where(lanes < RIM, total, rims_ref[1])
    for j in range(send_ref.shape[0]):
        send_ref[j] = jnp.where(j > me, upward, downward)


def final_kernel(got_ref, second_ref, rhs_ref, right_ref, recip_ref, final_ref):
    me = lax.axis_index("gx")
    count = got_ref.shape[0]
    system = reduced(got_ref)
    first = [second_ref[j, 0:8, :] for j in range(count)]
    last = [second_ref[j, 8:16, :] for j in range(count)]
    fluxes = end_fluxes(system, first, last, me)

    def keep(x, value):
        final_ref[pl.ds(x, ROWS, stride=NX), :] = value

    own_lines(lambda x: rhs_ref[x], right_ref, recip_ref, fluxes, keep)


def finish_kernel(factor, third_ref, second_ref, grad_ref, out_ref, closure_ref):
    me_x = lax.axis_index("gx")
    me_y = lax.axis_index("gy")
    count_x = second_ref.shape[0]
    count_y = third_ref.shape[0]
    lanes = lanes8()
    zero = jnp.zeros((ROWS, NY), F32)
    parts = [third_ref[j] for j in range(count_y)]
    while len(parts) > 1:
        parts = [a + b for a, b in zip(parts[::2], parts[1::2])]
    total = parts[0] * factor
    for a in range(HID // 8):
        piece = pltpu.roll(total, NY - 10 * a, 1) if a else total
        closure_ref[8 * a : 8 * (a + 1), :] = piece[:, 0:10]
    before = jnp.where(me_x > 0, second_ref[jnp.maximum(me_x - 1, 0), 24:32, :], zero)
    after = jnp.where(
        me_x < count_x - 1, second_ref[jnp.minimum(me_x + 1, count_x - 1), 24:32, :], zero
    )
    south = jnp.where(me_y > 0, third_ref[jnp.maximum(me_y - 1, 0)], zero)
    north = jnp.where(me_y < count_y - 1, third_ref[jnp.minimum(me_y + 1, count_y - 1)], zero)
    for x in range(NX):
        value = grad_ref[x + 1]
        if x == 0:
            value = value + before
        if x == NX - 1:
            value = value + after
        value = value + jnp.where(lanes == 0, pltpu.roll(south, NY - RIM - x, 1), 0.0)
        value = value + jnp.where(lanes == NY - 1, pltpu.roll(north, NY - 1 - RIM - x, 1), 0.0)
        out_ref[pl.ds(x, ROWS, stride=NX), :] = value


def tile(*shape):
    return jax.ShapeDtypeStruct(shape, F32)


def params():
    return pltpu.CompilerParams(vmem_limit_bytes=40 * 1024 * 1024)


def per_device(state, diffusivity, sea_mask, depth_index, closure_in, closure_out, cotangent):
    count_x = lax.axis_size("gx")
    count_y = lax.axis_size("gy")
    flat_state = state.reshape(ROWS * NX, NY)
    flat_cot = cotangent.reshape(ROWS * NX, NY)
    flat_diff = diffusivity.reshape(2 * NX, NY)
    first, last = pl.pallas_call(
        columns_kernel, out_shape=(tile(8, NY), tile(8, NY)), compiler_params=params()
    )(flat_state)
    upward = [(i, i + 1) for i in range(count_y - 1)]
    downward = [(i + 1, i) for i in range(count_y - 1)]
    low = lax.ppermute(last, "gy", upward)
    high = lax.ppermute(first, "gy", downward)
    lines = tile(NX, ROWS, NY)
    send, right, recip, left = pl.pallas_call(
        factor_kernel,
        out_shape=(tile(count_x, 40, NY), lines, lines, lines),
        compiler_params=params(),
    )(flat_state, flat_diff, sea_mask, depth_index, flat_cot)
    got = lax.all_to_all(send, "gx", 0, 0, tiled=True)
    scratch = (
        [pltpu.VMEM((NX + 2, ROWS, NY), F32)]
        + [pltpu.VMEM((NX, ROWS, NY), F32)] * 6
        + [
            pltpu.VMEM((80, NX * NY), BF16),
            pltpu.VMEM((2 * HID, 128), BF16),
            pltpu.VMEM((32, 256), BF16),
            pltpu.VMEM((2 * HID, 128), F32),
            pltpu.VMEM((4 * HID, 48), F32),
            pltpu.VMEM((2 * HID, 128), F32),
        ]
    )
    send, grad, rims, rhs = pl.pallas_call(
        main_kernel,
        out_shape=(tile(count_x, 32, NY), tile(NX + 2, ROWS, NY), tile(2, ROWS, NY), lines),
        scratch_shapes=scratch,
        compiler_params=params(),
    )(
        got,
        low,
        high,
        flat_state,
        sea_mask,
        depth_index,
        flat_cot,
        right,
        recip,
        left,
        closure_in,
        closure_out.reshape(HID, 1),
    )
    second = lax.all_to_all(send, "gx", 0, 0, tiled=True)
    send = pl.pallas_call(
        share_kernel, out_shape=tile(count_y, ROWS, NY), compiler_params=params()
    )(second, rims)
    third = lax.all_to_all(send, "gy", 0, 0, tiled=True)
    final = pl.pallas_call(
        final_kernel, out_shape=tile(ROWS * NX, NY), compiler_params=params()
    )(got, second, rhs, right, recip)
    factor = 1.0 / math.sqrt(2 * NX * count_x * NY * count_y)

    def finish(*refs):
        finish_kernel(factor, *refs)

    state_grad, closure_grad = pl.pallas_call(
        finish, out_shape=(tile(ROWS * NX, NY), tile(HID, 10)), compiler_params=params()
    )(third, second, grad)
    return (final.reshape(state.shape), state_grad.reshape(state.shape), closure_grad)


def solution(mesh):
    return jax.shard_map(
        per_device,
        mesh=mesh,
        in_specs=(
            P(None, None, "gx", "gy"),
            P(None, "gx", "gy"),
            P("gx", "gy"),
            P("gx", "gy"),
            P(),
            P(),
            P(None, None, "gx", "gy"),
        ),
        out_specs=(P(None, None, "gx", "gy"), P(None, None, "gx", "gy"), P()),
        check_vma=False,
    )
```

```python
import math

import jax
import jax.numpy as jnp
from jax import lax
from jax.experimental import pallas as pl
from jax.experimental.pallas import tpu as pltpu
from jax.sharding import PartitionSpec as P

F32 = jnp.float32
BF16 = jnp.bfloat16
DIFFUSE = 2048.0
FEAT = 8
HID = 64
NX = 32
NY = 128
ROWS = 8
XS = 4
RIM = 64


def iota(shape, dim):
    return lax.broadcasted_iota(jnp.int32, shape, dim)


def rows8():
    return iota((ROWS, NY), 0)


def lanes8():
    return iota((ROWS, NY), 1)


def wide(row):
    return jnp.broadcast_to(row, (ROWS, NY))


def by_level(first, second):
    return jnp.where((rows8() & 1) == 0, wide(first), wide(second))


def line(ref, x):
    return ref[pl.ds(x, ROWS, stride=NX), :]


def wet_line(sea_ref, depth_ref, x):
    sea = wide(sea_ref[x : x + 1, :])
    depth = wide(depth_ref[x : x + 1, :])
    return jnp.where(((rows8() & 1) < depth) & (sea > 0), 1.0, 0.0).astype(F32)


def rates8():
    return jnp.where(rows8() < 4, DIFFUSE, 0.5).astype(F32)


def split(values):
    high = values.astype(BF16)
    return high, (values - high.astype(F32)).astype(BF16)


def columns_kernel(fields_ref, first_ref, last_ref):
    lanes = lanes8()
    first = jnp.zeros((ROWS, NY), F32)
    last = jnp.zeros((ROWS, NY), F32)
    for x in range(NX):
        here = fields_ref[x]
        first = jnp.where(lanes == x, pltpu.roll(here, x, 1) if x else here, first)
        last = jnp.where(lanes == x, pltpu.roll(here, x + 1, 1), last)
    first_ref[...] = first
    last_ref[...] = last


def factor_kernel(
    state_hbm,
    diff_hbm,
    sea_hbm,
    depth_hbm,
    cot_hbm,
    send_ref,
    right_ref,
    recip_ref,
    left_ref,
    fields_ref,
    wets_ref,
    cots_ref,
    state_ref,
    diff_ref,
    sea_ref,
    depth_ref,
    cot_ref,
    sems,
):
    copies = [
        pltpu.make_async_copy(source, target, sems.at[n])
        for n, (source, target) in enumerate(
            (
                (sea_hbm, sea_ref),
                (depth_hbm, depth_ref),
                (diff_hbm, diff_ref),
                (cot_hbm, cot_ref),
                (state_hbm, state_ref),
            )
        )
    ]
    for copy in copies:
        copy.start()
    me = lax.axis_index("gx")
    count = send_ref.shape[0]
    row = rows8()
    for copy in copies[:3]:
        copy.wait()
    wet = [wet_line(sea_ref, depth_ref, x) for x in range(NX)]
    for x in range(NX):
        wets_ref[x] = wet[x]
    rates = rates8()
    bare = [
        by_level(diff_ref[x : x + 1, :], diff_ref[NX + x : NX + x + 1, :]) * wet[x]
        for x in range(NX)
    ]
    cond = [rates * bare[x] * wet[x + 1] for x in range(NX - 1)]
    copies[3].wait()
    mass = jnp.ones((ROWS, NY), F32)
    carry = jnp.ones((ROWS, NY), F32)
    mass_back = jnp.ones((ROWS, NY), F32)
    cots = [line(cot_ref, x) for x in range(NX)]
    for x in range(NX):
        cots_ref[x] = cots[x]
    load = cots[0]
    load_back = cots[NX - 1]
    for i in range(NX - 1):
        recip = 1.0 / (mass + cond[i])
        ratio = cond[i] * recip
        right_ref[i] = ratio
        recip_ref[i] = recip
        mass = 1.0 + mass * ratio
        load = cots[i + 1] + ratio * load
        carry = carry * ratio
        j = NX - 2 - i
        ratio_back = cond[j] / (mass_back + cond[j])
        left_ref[j] = ratio_back
        mass_back = 1.0 + mass_back * ratio_back
        load_back = cots[j] + ratio_back * load_back
    last_self = 1.0 / mass
    first_self = 1.0 / mass_back
    right_ref[NX - 1] = jnp.zeros((ROWS, NY), F32)
    left_ref[NX - 1] = jnp.zeros((ROWS, NY), F32)
    recip_ref[NX - 1] = last_self
    across = carry * last_self
    upper = (row & 2) == 0
    copies[4].wait()
    for x in range(NX):
        fields_ref[x] = line(state_ref, x)
    tiles = [
        load_back * first_self,
        load * last_self,
        jnp.where(upper, first_self, across),
        jnp.where(upper, last_self, jnp.where(row < 4, bare[NX - 1], wet[0])),
    ]
    own_last = line(state_ref, NX - 1)
    own_first = line(state_ref, 0)
    for j in range(count):
        for n, tile in enumerate(tiles):
            send_ref[j, ROWS * n : ROWS * (n + 1), :] = tile
        send_ref[j, ROWS * 4 :, :] = jnp.where(j > me, own_last, own_first)


def reduced(got_ref):
    count = got_ref.shape[0]
    upper = (rows8() & 2) == 0
    first_self, across, last_self, bare, wet = [], [], [], [], []
    for j in range(count):
        tile = got_ref[j, 16:24, :]
        first_self.append(jnp.where(upper, tile, pltpu.roll(tile, 2, 0)))
        across.append(jnp.where(upper, pltpu.roll(tile, 6, 0), tile))
        tile = got_ref[j, 24:32, :]
        last_self.append(jnp.where(upper, tile, pltpu.roll(tile, 2, 0)))
        bare.append(by_level(got_ref[j, 26:27, :], got_ref[j, 27:28, :]))
        wet.append(by_level(got_ref[j, 30:31, :], got_ref[j, 31:32, :]))
    face = [rates8() * bare[j] * wet[j + 1] for j in range(count - 1)]
    return first_self, across, last_self, face


def end_fluxes(system, first, last, me):
    first_self, across, last_self, face = system
    count = len(first_self)
    zero = jnp.zeros((ROWS, NY), F32)
    give, value = last_self[0], last[0]
    gives, values, links = [give], [value], [zero]
    for j in range(1, count):
        link = face[j - 1] / (1.0 + face[j - 1] * (give + first_self[j]))
        pull = across[j] * link
        value = last[j] + pull * (value - first[j])
        give = last_self[j] - pull * across[j]
        gives.append(give)
        values.append(value)
        links.append(link)
    back_give, back_value = first_self[count - 1], first[count - 1]
    right_flux = [None] * count
    right_flux[count - 1] = zero
    for j in range(count - 2, -1, -1):
        right_flux[j] = (
            face[j] * (back_value - values[j]) / (1.0 + face[j] * (back_give + gives[j]))
        )
        link = face[j] / (1.0 + face[j] * (back_give + last_self[j]))
        pull = across[j] * link
        back_value = first[j] + pull * (back_value - last[j])
        back_give = first_self[j] - pull * across[j]
    left, right = zero, right_flux[0]
    for j in range(1, count):
        here = links[j] * (values[j - 1] - first[j] - across[j] * right_flux[j])
        left = jnp.where(me == j, here, left)
        right = jnp.where(me == j, right_flux[j], right)
    return left, right


def own_lines(read, right_ref, recip_ref, fluxes, write):
    left, right = fluxes
    load = read(0) + left
    loads = [load]
    for i in range(1, NX):
        load = read(i) + right_ref[i - 1] * load
        loads.append(load)
    value = (loads[NX - 1] + right) * recip_ref[NX - 1]
    write(NX - 1, value)
    for i in range(NX - 2, -1, -1):
        value = right_ref[i] * value + recip_ref[i] * loads[i]
        write(i, value)


def network_kernel(weights_ref, out_ref, forward_ref, back_ref, outw_ref):
    weights = weights_ref[...]
    per_level = []
    for level in range(2):
        spread = iota((16, FEAT + 1), 0) == 2 * iota((16, FEAT + 1), 1) + level
        per_level.append(
            jnp.dot(
                spread.astype(F32),
                weights,
                precision=lax.Precision.HIGHEST,
                preferred_element_type=F32,
            )
        )
    both = jnp.concatenate(per_level, 1)
    high = both.astype(BF16).astype(F32)
    low = both - high
    bias = weights[FEAT : FEAT + 1, :]
    bias = jnp.broadcast_to(jnp.concatenate([bias, bias], 1), (16, 2 * HID))
    bias_high = bias.astype(BF16).astype(F32)
    bias_mid = (bias - bias_high).astype(BF16).astype(F32)
    bias_low = bias - bias_high - bias_mid
    row = iota((16, 2 * HID), 0)
    bias = jnp.where(
        row == 0, bias_high, jnp.where(row == 1, bias_mid, jnp.where(row == 2, bias_low, 0.0))
    )
    stack = jnp.concatenate([high, high, bias, low, low, jnp.zeros((48, 2 * HID), F32)], 0)
    forward_ref[...] = jnp.transpose(stack).astype(BF16)
    turned = jnp.concatenate([high, low], 0)
    back_ref[...] = jnp.concatenate([turned, turned], 1).astype(BF16)
    out = out_ref[...]
    out = jnp.broadcast_to(jnp.concatenate([out, out], 1), (2 * HID, 2 * HID))
    outw_ref[...] = jnp.transpose(out)


def pack(features, bias, out):
    blank = jnp.zeros((ROWS, HID), F32)
    row = iota((ROWS, 32), 0)
    ends = [
        jnp.broadcast_to(v, (ROWS, 32))
        for v in (bias[:, 0:32], bias[:, 32:64], out[:, 0:32], out[:, 32:64])
    ]
    tail = jnp.zeros((ROWS, 32), F32)
    for n, end in enumerate(ends):
        tail = jnp.where(row == n, end, tail)
    return jnp.concatenate([features, blank[:, :32], tail], 1)


def main_kernel(
    got_ref,
    low_ref,
    high_ref,
    lines_ref,
    wets,
    cots_ref,
    right_ref,
    recip_ref,
    left_ref,
    forward_ref,
    back_ref,
    outw_ref,
    send_ref,
    grad_ref,
    rims_ref,
    rhs_ref,
    fields,
    adj,
    slope_x,
    slope_y,
    curve_x,
    curve_y,
    feats,
    sums_ref,
    out_sums_ref,
):
    me = lax.axis_index("gx")
    here_y = lax.axis_index("gy")
    count = got_ref.shape[0]
    total_y = NY * lax.axis_size("gy")
    lanes = lanes8()
    row = rows8()
    zero = jnp.zeros((ROWS, NY), F32)

    for x in range(NX):
        fields[x + 1] = lines_ref[x]
    below = got_ref[jnp.maximum(me - 1, 0), 32:40, :]
    above = got_ref[jnp.minimum(me + 1, count - 1), 32:40, :]
    fields[0] = jnp.where(me > 0, below, zero)
    fields[NX + 1] = jnp.where(me < count - 1, above, zero)

    system = reduced(got_ref)
    first = [got_ref[j, 0:8, :] for j in range(count)]
    last = [got_ref[j, 8:16, :] for j in range(count)]
    fluxes = end_fluxes(system, first, last, me)

    def keep(x, value):
        adj[x] = wets[x] * value

    own_lines(lambda x: cots_ref[x], right_ref, recip_ref, fluxes, keep)

    low = jnp.where(here_y > 0, low_ref[...], zero)
    high = jnp.where(here_y < lax.axis_size("gy") - 1, high_ref[...], zero)
    feats[32:48, :] = jnp.ones((16, NX * NY), BF16)
    for x in range(NX):
        center = fields[x + 1]
        east = fields[x + 2]
        west = fields[x]
        south = jnp.where(lanes == 0, pltpu.roll(low, (-x) % NY, 1) if x else low, pltpu.roll(center, 1, 1))
        north = jnp.where(
            lanes == NY - 1, pltpu.roll(high, NY - 1 - x, 1), pltpu.roll(center, NY - 1, 1)
        )
        sx = 0.5 * (east - west)
        sy = 0.5 * (north - south)
        slope_x[x] = sx
        slope_y[x] = sy
        curve_x[x] = east - 2.0 * center + west
        curve_y[x] = north - 2.0 * center + south
        part_high, part_low = split(jnp.concatenate([sx, sy], 0))
        place = slice(x * NY, (x + 1) * NY)
        feats[0:16, place] = part_high
        feats[16:32, place] = part_low
        feats[48:64, place] = part_high
        feats[64:80, place] = part_low

    sums_ref[...] = jnp.zeros(sums_ref.shape, F32)
    out_sums_ref[...] = jnp.zeros(out_sums_ref.shape, F32)
    grad_ref[...] = jnp.zeros(grad_ref.shape, F32)
    rims_ref[...] = jnp.zeros(rims_ref.shape, F32)
    places = (here_y * NY + lanes).astype(F32)
    turn = 0.3 * (0.5 + 0.5 * places / total_y)
    moment = row < 4

    @pl.loop(0, NX // XS)
    def _(step):
        base = step * XS
        place = pl.ds(pl.multiple_of(base * NY, XS * NY), XS * NY)
        hidden = jnp.tanh(
            jnp.dot(forward_ref[:, 0:80], feats[0:80, place], preferred_element_type=F32)
        )
        outw = outw_ref[...]
        sharp, keepers = [], []
        for i in range(XS):
            x = base + i
            unit = hidden[:, i * NY : (i + 1) * NY]
            weighed = unit * outw
            mixed = by_level(
                jnp.sum(weighed[:HID], 0, keepdims=True), jnp.sum(weighed[HID:], 0, keepdims=True)
            )
            gate = 1.0 / (1.0 + jnp.exp(-mixed))
            nu = jnp.where(moment, 0.24 * gate, 0.0)
            center = fields[x + 1]
            sx, sy, cx, cy = slope_x[x], slope_y[x], curve_x[x], curve_y[x]
            u = by_level(center[0:1], center[1:2])
            v = by_level(center[2:3], center[3:4])
            speed_u = jnp.sqrt(u * u + 0.01)
            speed_v = jnp.sqrt(v * v + 0.01)
            upwind = u * sx + v * sy - 0.5 * (speed_u * cx + speed_v * cy)
            twist = jnp.where(
                row < 2, pltpu.roll(center, 6, 0), jnp.where(moment, -pltpu.roll(center, 2, 0), 0.0)
            )
            rhs_ref[x] = wets[x] * (center - 0.3 * upwind + nu * (cx + cy) + turn * twist)
            g = adj[x]
            to_gate = jnp.where(moment, g * (cx + cy) * (0.24 * gate * (1.0 - gate)), 0.0)
            to_gate = to_gate + pltpu.roll(to_gate, 6, 0)
            gate_level = jnp.concatenate(
                [
                    jnp.broadcast_to(to_gate[0:1], (HID, NY)),
                    jnp.broadcast_to(to_gate[1:2], (HID, NY)),
                ],
                0,
            )
            out_sums_ref[...] += unit * gate_level
            sharp.append((1.0 - unit * unit) * (outw * gate_level))
            along_u = g * (-0.3 * sx + 0.15 * (u / speed_u) * cx)
            along_v = g * (-0.3 * sy + 0.15 * (v / speed_v) * cy)
            along_u = along_u + pltpu.roll(along_u, 4, 0)
            along_u = along_u + pltpu.roll(along_u, 2, 0)
            along_v = along_v + pltpu.roll(along_v, 4, 0)
            along_v = along_v + pltpu.roll(along_v, 2, 0)
            untwist = jnp.where(
                row < 2, along_u - turn * pltpu.roll(g, 6, 0), along_v + turn * pltpu.roll(g, 2, 0)
            )
            bend_x = g * (0.15 * speed_u + nu)
            bend_y = g * (0.15 * speed_v + nu)
            middle = g + jnp.where(moment, untwist, 0.0) - 2.0 * (bend_x + bend_y)
            keepers.append((-0.3 * u * g, -0.3 * v * g, bend_x, bend_y, middle))
        parts = split(jnp.concatenate(sharp, 1))
        stacked = jnp.concatenate(parts, 0)
        sums_ref[...] += lax.dot_general(
            stacked, feats[0:48, place], (((1,), (1,)), ((), ())), preferred_element_type=F32
        )
        to_feats = jnp.dot(back_ref[...], stacked, preferred_element_type=F32)
        to_feats = to_feats[0:16] + to_feats[16:32]
        for i in range(XS):
            x = base + i
            to_sx, to_sy, bend_x, bend_y, middle = keepers[i]
            mine = to_feats[:, i * NY : (i + 1) * NY]
            half_x = 0.5 * (to_sx + mine[0:8])
            half_y = 0.5 * (to_sy + mine[8:16])
            to_north = bend_y + half_y
            to_south = bend_y - half_y
            north = pltpu.roll(to_north, 1, 1)
            south = pltpu.roll(to_south, NY - 1, 1)
            rims_ref[0] = jnp.where(lanes == RIM + x, pltpu.roll(north, RIM + x, 1), rims_ref[0])
            rims_ref[1] = jnp.where(
                lanes == RIM + x, pltpu.roll(south, RIM + x + 1, 1), rims_ref[1]
            )
            grad_ref[x] += bend_x - half_x
            grad_ref[x + 1] += (
                middle + jnp.where(lanes == 0, 0.0, north) + jnp.where(lanes == NY - 1, 0.0, south)
            )
            grad_ref[x + 2] += bend_x + half_x

    load = rhs_ref[0]
    load_back = rhs_ref[NX - 1]
    for i in range(NX - 1):
        load = rhs_ref[i + 1] + right_ref[i] * load
        j = NX - 2 - i
        load_back = rhs_ref[j] + left_ref[j] * load_back
    first_own = load_back * jnp.where(
        (row & 2) == 0, got_ref[me, 16:24, :], pltpu.roll(got_ref[me, 16:24, :], 2, 0)
    )
    last_own = load * recip_ref[NX - 1]

    sums = sums_ref[0:128] + sums_ref[128:256]
    total = jnp.zeros((16, HID), F32)
    for level in range(2):
        source = iota((16, 48), 1)
        target = iota((16, 48), 0)
        feature = (source < 32) & ((source & 15) == 2 * target + level) & (target < FEAT)
        gather = feature | ((source == 32) & (target == FEAT))
        total += lax.dot_general(
            gather.astype(F32),
            sums[level * HID : (level + 1) * HID],
            (((1,), (1,)), ((), ())),
            precision=lax.Precision.HIGHEST,
            preferred_element_type=F32,
        )
    out_total = lax.dot_general(
        jnp.ones((8, 128), F32),
        out_sums_ref[0:HID] + out_sums_ref[HID:],
        (((1,), (1,)), ((), ())),
        precision=lax.Precision.HIGHEST,
        preferred_element_type=F32,
    )
    packed = pack(total[0:8], total[8:9], out_total[0:1])
    to_last = grad_ref[NX + 1]
    to_first = grad_ref[0]
    for j in range(count):
        send_ref[j, 0:8, :] = first_own
        send_ref[j, 8:16, :] = last_own
        send_ref[j, 16:24, :] = packed
        send_ref[j, 24:32, :] = jnp.where(j > me, to_last, to_first)


def share_kernel(
    second_ref, rims_ref, got_ref, rhs_ref, right_ref, recip_ref, send_ref, final_ref
):
    me_y = lax.axis_index("gy")
    me = lax.axis_index("gx")
    count = got_ref.shape[0]
    lanes = lanes8()
    total = second_ref[0, 16:24, :]
    for j in range(1, count):
        total = total + second_ref[j, 16:24, :]
    rim = (lanes >= RIM) & (lanes < RIM + NX)
    upward = jnp.where(rim, rims_ref[0], total)
    downward = jnp.where(rim, rims_ref[1], total)
    for j in range(send_ref.shape[0]):
        send_ref[j] = jnp.where(j > me_y, upward, downward)
    system = reduced(got_ref)
    first = [second_ref[j, 0:8, :] for j in range(count)]
    last = [second_ref[j, 8:16, :] for j in range(count)]
    fluxes = end_fluxes(system, first, last, me)

    def keep(x, value):
        final_ref[pl.ds(x, ROWS, stride=NX), :] = value

    own_lines(lambda x: rhs_ref[x], right_ref, recip_ref, fluxes, keep)


def finish_kernel(
    factor, third_ref, second_ref, grad_ref, final_ref, final_hbm, out_hbm, closure_ref, out_ref, sems
):
    copy = pltpu.make_async_copy(final_ref, final_hbm, sems.at[0])
    copy.start()
    me_x = lax.axis_index("gx")
    me_y = lax.axis_index("gy")
    count_x = second_ref.shape[0]
    count_y = third_ref.shape[0]
    lanes = lanes8()
    zero = jnp.zeros((ROWS, NY), F32)
    before = jnp.where(me_x > 0, second_ref[jnp.maximum(me_x - 1, 0), 24:32, :], zero)
    after = jnp.where(
        me_x < count_x - 1, second_ref[jnp.minimum(me_x + 1, count_x - 1), 24:32, :], zero
    )
    south = jnp.where(me_y > 0, third_ref[jnp.maximum(me_y - 1, 0)], zero)
    north = jnp.where(me_y < count_y - 1, third_ref[jnp.minimum(me_y + 1, count_y - 1)], zero)
    for x in range(NX):
        value = grad_ref[x + 1]
        if x == 0:
            value = value + before
        if x == NX - 1:
            value = value + after
        value = value + jnp.where(lanes == 0, pltpu.roll(south, NY - RIM - x, 1), 0.0)
        value = value + jnp.where(lanes == NY - 1, pltpu.roll(north, NY - 1 - RIM - x, 1), 0.0)
        out_ref[pl.ds(x, ROWS, stride=NX), :] = value
    copy_out = pltpu.make_async_copy(out_ref, out_hbm, sems.at[1])
    copy_out.start()
    parts = [third_ref[j] for j in range(count_y)]
    while len(parts) > 1:
        parts = [a + b for a, b in zip(parts[::2], parts[1::2])]
    total = parts[0] * factor
    closure_ref[0:8, :] = total[:, 0:HID]
    for n in range(2):
        closure_ref[8 + n : 9 + n, :] = jnp.concatenate(
            [total[2 * n : 2 * n + 1, 96:], total[2 * n + 1 : 2 * n + 2, 96:]], 1
        )
    copy.wait()
    copy_out.wait()


def tile(*shape):
    return jax.ShapeDtypeStruct(shape, F32)


def params():
    return pltpu.CompilerParams(vmem_limit_bytes=40 * 1024 * 1024)


def per_device(state, diffusivity, sea_mask, depth_index, closure_in, closure_out, cotangent):
    count_x = lax.axis_size("gx")
    count_y = lax.axis_size("gy")
    lines = tile(NX, ROWS, NY)
    in_hbm = pl.BlockSpec(memory_space=pltpu.HBM)
    in_vmem = pl.BlockSpec(memory_space=pltpu.VMEM)
    send, right, recip, left, fields, wets, cots = pl.pallas_call(
        factor_kernel,
        in_specs=[in_hbm] * 5,
        out_shape=(tile(count_x, 40, NY),) + (lines,) * 6,
        scratch_shapes=[
            pltpu.VMEM((ROWS * NX, NY), F32),
            pltpu.VMEM((2 * NX, NY), F32),
            pltpu.VMEM((NX, NY), jnp.int32),
            pltpu.VMEM((NX, NY), jnp.int32),
            pltpu.VMEM((ROWS * NX, NY), F32),
            pltpu.SemaphoreType.DMA((5,)),
        ],
        compiler_params=params(),
    )(
        state.reshape(ROWS * NX, NY),
        diffusivity.reshape(2 * NX, NY),
        sea_mask,
        depth_index,
        cotangent.reshape(ROWS * NX, NY),
    )
    got = lax.all_to_all(send, "gx", 0, 0, tiled=True)
    first, last = pl.pallas_call(
        columns_kernel, out_shape=(tile(8, NY), tile(8, NY)), compiler_params=params()
    )(fields)
    low = lax.ppermute(last, "gy", [(i, (i + 1) % count_y) for i in range(count_y)])
    high = lax.ppermute(first, "gy", [((i + 1) % count_y, i) for i in range(count_y)])
    forward, back, outw = pl.pallas_call(
        network_kernel,
        out_shape=(
            jax.ShapeDtypeStruct((2 * HID, 128), BF16),
            jax.ShapeDtypeStruct((32, 256), BF16),
            tile(2 * HID, 128),
        ),
        compiler_params=params(),
    )(closure_in.T, closure_out.reshape(1, HID))
    scratch = (
        [pltpu.VMEM((NX + 2, ROWS, NY), F32)]
        + [pltpu.VMEM((NX, ROWS, NY), F32)] * 5
        + [
            pltpu.VMEM((80, NX * NY), BF16),
            pltpu.VMEM((4 * HID, 48), F32),
            pltpu.VMEM((2 * HID, 128), F32),
        ]
    )
    send, grad, rims, rhs = pl.pallas_call(
        main_kernel,
        out_shape=(tile(count_x, 32, NY), tile(NX + 2, ROWS, NY), tile(2, ROWS, NY), lines),
        scratch_shapes=scratch,
        compiler_params=params(),
    )(got, low, high, fields, wets, cots, right, recip, left, forward, back, outw)
    second = lax.all_to_all(send, "gx", 0, 0, tiled=True)
    send, final = pl.pallas_call(
        share_kernel,
        out_shape=(tile(count_y, ROWS, NY), tile(ROWS * NX, NY)),
        compiler_params=params(),
    )(second, rims, got, rhs, right, recip)
    third = lax.all_to_all(send, "gy", 0, 0, tiled=True)
    factor = 1.0 / math.sqrt(2 * NX * count_x * NY * count_y)

    def finish(*refs):
        finish_kernel(factor, *refs)

    final, state_grad, closure_grad = pl.pallas_call(
        finish,
        in_specs=[in_vmem] * 4,
        out_shape=(tile(ROWS * NX, NY), tile(ROWS * NX, NY), tile(10, HID)),
        out_specs=(in_hbm, in_hbm, in_vmem),
        scratch_shapes=[pltpu.VMEM((ROWS * NX, NY), F32), pltpu.SemaphoreType.DMA((2,))],
        compiler_params=params(),
    )(third, second, grad, final)
    return (final.reshape(state.shape), state_grad.reshape(state.shape), closure_grad.T)


def solution(mesh):
    return jax.shard_map(
        per_device,
        mesh=mesh,
        in_specs=(
            P(None, None, "gx", "gy"),
            P(None, "gx", "gy"),
            P("gx", "gy"),
            P("gx", "gy"),
            P(),
            P(),
            P(None, None, "gx", "gy"),
        ),
        out_specs=(P(None, None, "gx", "gy"), P(None, None, "gx", "gy"), P()),
        check_vma=False,
    )
```

```python
import math

import jax
import jax.numpy as jnp
from jax import lax
from jax.experimental import pallas as pl
from jax.experimental.pallas import tpu as pltpu
from jax.sharding import PartitionSpec as P

F32 = jnp.float32
BF16 = jnp.bfloat16
DIFFUSE = 2048.0
FEAT = 8
HID = 64
NX = 32
NY = 128
ROWS = 8
RIM = 64


def iota(shape, dim):
    return lax.broadcasted_iota(jnp.int32, shape, dim)


def rows8():
    return iota((ROWS, NY), 0)


def lanes8():
    return iota((ROWS, NY), 1)


def wide(row):
    return jnp.broadcast_to(row, (ROWS, NY))


def by_level(first, second):
    return jnp.where((rows8() & 1) == 0, wide(first), wide(second))


def line(ref, x):
    return ref[pl.ds(x, ROWS, stride=NX), :]


def wet_line(sea_ref, depth_ref, x):
    sea = wide(sea_ref[x : x + 1, :])
    depth = wide(depth_ref[x : x + 1, :])
    return jnp.where(((rows8() & 1) < depth) & (sea > 0), 1.0, 0.0).astype(F32)


def rates8():
    return jnp.where(rows8() < 4, DIFFUSE, 0.5).astype(F32)


def split(values):
    high = values.astype(BF16)
    return high, (values - high.astype(F32)).astype(BF16)


def load_kernel(
    state_hbm,
    diff_hbm,
    sea_hbm,
    depth_hbm,
    cot_hbm,
    fields_ref,
    first_ref,
    last_ref,
    diff_ref,
    sea_ref,
    depth_ref,
    cot_ref,
    state_ref,
    sems,
):
    copies = [
        pltpu.make_async_copy(source, target, sems.at[n])
        for n, (source, target) in enumerate(
            (
                (state_hbm, state_ref),
                (sea_hbm, sea_ref),
                (depth_hbm, depth_ref),
                (diff_hbm, diff_ref),
                (cot_hbm, cot_ref),
            )
        )
    ]
    for copy in copies:
        copy.start()
    copies[0].wait()
    lanes = lanes8()
    first = jnp.zeros((ROWS, NY), F32)
    last = jnp.zeros((ROWS, NY), F32)
    for x in range(NX):
        here = line(state_ref, x)
        fields_ref[x] = here
        first = jnp.where(lanes == x, pltpu.roll(here, x, 1) if x else here, first)
        last = jnp.where(lanes == x, pltpu.roll(here, x + 1, 1), last)
    first_ref[...] = first
    last_ref[...] = last
    for copy in copies[1:]:
        copy.wait()


def factor_kernel(
    fields_ref,
    diff_ref,
    sea_ref,
    depth_ref,
    cot_ref,
    send_ref,
    right_ref,
    recip_ref,
    left_ref,
    wets_ref,
):
    me = lax.axis_index("gx")
    count = send_ref.shape[0]
    row = rows8()
    wet = [wet_line(sea_ref, depth_ref, x) for x in range(NX)]
    for x in range(NX):
        wets_ref[x] = wet[x]
    rates = rates8()
    bare = [
        by_level(diff_ref[x : x + 1, :], diff_ref[NX + x : NX + x + 1, :]) * wet[x]
        for x in range(NX)
    ]
    cond = [rates * bare[x] * wet[x + 1] for x in range(NX - 1)]
    mass = jnp.ones((ROWS, NY), F32)
    carry = jnp.ones((ROWS, NY), F32)
    mass_back = jnp.ones((ROWS, NY), F32)
    cots = [line(cot_ref, x) for x in range(NX)]
    load = cots[0]
    load_back = cots[NX - 1]
    for i in range(NX - 1):
        recip = 1.0 / (mass + cond[i])
        ratio = cond[i] * recip
        right_ref[i] = ratio
        recip_ref[i] = recip
        mass = 1.0 + mass * ratio
        load = cots[i + 1] + ratio * load
        carry = carry * ratio
        j = NX - 2 - i
        ratio_back = cond[j] / (mass_back + cond[j])
        left_ref[j] = ratio_back
        mass_back = 1.0 + mass_back * ratio_back
        load_back = cots[j] + ratio_back * load_back
    last_self = 1.0 / mass
    first_self = 1.0 / mass_back
    right_ref[NX - 1] = jnp.zeros((ROWS, NY), F32)
    left_ref[NX - 1] = jnp.zeros((ROWS, NY), F32)
    recip_ref[NX - 1] = last_self
    across = carry * last_self
    upper = (row & 2) == 0
    tiles = [
        load_back * first_self,
        load * last_self,
        jnp.where(upper, first_self, across),
        jnp.where(upper, last_self, jnp.where(row < 4, bare[NX - 1], wet[0])),
    ]
    own_last = fields_ref[NX - 1]
    own_first = fields_ref[0]
    for j in range(count):
        for n, tile in enumerate(tiles):
            send_ref[j, ROWS * n : ROWS * (n + 1), :] = tile
        send_ref[j, ROWS * 4 :, :] = jnp.where(j > me, own_last, own_first)


def reduced(got_ref):
    count = got_ref.shape[0]
    upper = (rows8() & 2) == 0
    first_self, across, last_self, bare, wet = [], [], [], [], []
    for j in range(count):
        tile = got_ref[j, 16:24, :]
        first_self.append(jnp.where(upper, tile, pltpu.roll(tile, 2, 0)))
        across.append(jnp.where(upper, pltpu.roll(tile, 6, 0), tile))
        tile = got_ref[j, 24:32, :]
        last_self.append(jnp.where(upper, tile, pltpu.roll(tile, 2, 0)))
        bare.append(by_level(got_ref[j, 26:27, :], got_ref[j, 27:28, :]))
        wet.append(by_level(got_ref[j, 30:31, :], got_ref[j, 31:32, :]))
    face = [rates8() * bare[j] * wet[j + 1] for j in range(count - 1)]
    return first_self, across, last_self, face


def end_fluxes(system, first, last, me):
    first_self, across, last_self, face = system
    count = len(first_self)
    zero = jnp.zeros((ROWS, NY), F32)
    give, value = last_self[0], last[0]
    gives, values, links = [give], [value], [zero]
    for j in range(1, count):
        link = face[j - 1] / (1.0 + face[j - 1] * (give + first_self[j]))
        pull = across[j] * link
        value = last[j] + pull * (value - first[j])
        give = last_self[j] - pull * across[j]
        gives.append(give)
        values.append(value)
        links.append(link)
    back_give, back_value = first_self[count - 1], first[count - 1]
    right_flux = [None] * count
    right_flux[count - 1] = zero
    for j in range(count - 2, -1, -1):
        right_flux[j] = (
            face[j] * (back_value - values[j]) / (1.0 + face[j] * (back_give + gives[j]))
        )
        link = face[j] / (1.0 + face[j] * (back_give + last_self[j]))
        pull = across[j] * link
        back_value = first[j] + pull * (back_value - last[j])
        back_give = first_self[j] - pull * across[j]
    left, right = zero, right_flux[0]
    for j in range(1, count):
        here = links[j] * (values[j - 1] - first[j] - across[j] * right_flux[j])
        left = jnp.where(me == j, here, left)
        right = jnp.where(me == j, right_flux[j], right)
    return left, right


def own_lines(read, right_ref, recip_ref, fluxes, write):
    left, right = fluxes
    load = read(0) + left
    loads = [load]
    for i in range(1, NX):
        load = read(i) + right_ref[i - 1] * load
        loads.append(load)
    value = (loads[NX - 1] + right) * recip_ref[NX - 1]
    write(NX - 1, value)
    for i in range(NX - 2, -1, -1):
        value = right_ref[i] * value + recip_ref[i] * loads[i]
        write(i, value)


def network_kernel(weights_ref, out_ref, forward_ref, back_ref, outw_ref):
    weights = weights_ref[...]
    per_level = []
    for level in range(2):
        spread = iota((16, FEAT + 1), 0) == 2 * iota((16, FEAT + 1), 1) + level
        per_level.append(
            jnp.dot(
                spread.astype(F32),
                weights,
                precision=lax.Precision.HIGHEST,
                preferred_element_type=F32,
            )
        )
    both = jnp.concatenate(per_level, 1)
    high = both.astype(BF16).astype(F32)
    low = both - high
    bias = weights[FEAT : FEAT + 1, :]
    bias = jnp.broadcast_to(jnp.concatenate([bias, bias], 1), (16, 2 * HID))
    bias_high = bias.astype(BF16).astype(F32)
    bias_mid = (bias - bias_high).astype(BF16).astype(F32)
    bias_low = bias - bias_high - bias_mid
    row = iota((16, 2 * HID), 0)
    bias = jnp.where(
        row == 0, bias_high, jnp.where(row == 1, bias_mid, jnp.where(row == 2, bias_low, 0.0))
    )
    stack = jnp.concatenate([high, high, bias, low, low, jnp.zeros((48, 2 * HID), F32)], 0)
    forward_ref[...] = jnp.transpose(stack).astype(BF16)
    turned = jnp.concatenate([high, low], 0)
    back_ref[...] = jnp.concatenate([turned, turned], 1).astype(BF16)
    out = out_ref[...]
    out = jnp.broadcast_to(jnp.concatenate([out, out], 1), (2 * HID, 2 * HID))
    outw_ref[...] = jnp.transpose(out)


def pack(features, bias, out):
    blank = jnp.zeros((ROWS, HID), F32)
    row = iota((ROWS, 32), 0)
    ends = [
        jnp.broadcast_to(v, (ROWS, 32))
        for v in (bias[:, 0:32], bias[:, 32:64], out[:, 0:32], out[:, 32:64])
    ]
    tail = jnp.zeros((ROWS, 32), F32)
    for n, end in enumerate(ends):
        tail = jnp.where(row == n, end, tail)
    return jnp.concatenate([features, blank[:, :32], tail], 1)


def adjoint_kernel(got_ref, cot_ref, wets_ref, right_ref, recip_ref, adj_ref):
    me = lax.axis_index("gx")
    count = got_ref.shape[0]
    system = reduced(got_ref)
    first = [got_ref[j, 0:8, :] for j in range(count)]
    last = [got_ref[j, 8:16, :] for j in range(count)]
    fluxes = end_fluxes(system, first, last, me)

    def keep(x, value):
        adj_ref[x] = wets_ref[x] * value

    own_lines(lambda x: line(cot_ref, x), right_ref, recip_ref, fluxes, keep)


def stencil_kernel(
    got_ref, low_ref, high_ref, lines_ref, slope_x, slope_y, curve_x, curve_y, feats
):
    me = lax.axis_index("gx")
    here_y = lax.axis_index("gy")
    count = got_ref.shape[0]
    lanes = lanes8()
    zero = jnp.zeros((ROWS, NY), F32)
    below = got_ref[jnp.maximum(me - 1, 0), 32:40, :]
    above = got_ref[jnp.minimum(me + 1, count - 1), 32:40, :]
    below = jnp.where(me > 0, below, zero)
    above = jnp.where(me < count - 1, above, zero)
    low = jnp.where(here_y > 0, low_ref[...], zero)
    high = jnp.where(here_y < lax.axis_size("gy") - 1, high_ref[...], zero)
    feats[32:48, :] = jnp.ones((16, NX * NY), BF16)
    for x in range(NX):
        center = lines_ref[x]
        east = lines_ref[x + 1] if x < NX - 1 else above
        west = lines_ref[x - 1] if x else below
        south = jnp.where(
            lanes == 0, pltpu.roll(low, (-x) % NY, 1) if x else low, pltpu.roll(center, 1, 1)
        )
        north = jnp.where(
            lanes == NY - 1, pltpu.roll(high, NY - 1 - x, 1), pltpu.roll(center, NY - 1, 1)
        )
        sx = 0.5 * (east - west)
        sy = 0.5 * (north - south)
        slope_x[x] = sx
        slope_y[x] = sy
        curve_x[x] = east - 2.0 * center + west
        curve_y[x] = north - 2.0 * center + south
        part_high, part_low = split(jnp.concatenate([sx, sy], 0))
        place = slice(x * NY, (x + 1) * NY)
        feats[0:16, place] = part_high
        feats[16:32, place] = part_low
        feats[48:64, place] = part_high
        feats[64:80, place] = part_low


def closure_kernel(
    got_ref,
    lines_ref,
    wets,
    adj,
    slope_x,
    slope_y,
    curve_x,
    curve_y,
    feats,
    forward_ref,
    back_ref,
    outw_ref,
    right_ref,
    recip_ref,
    left_ref,
    send_ref,
    rhs_ref,
    grad_ref,
    rims_ref,
):
    me = lax.axis_index("gx")
    count = got_ref.shape[0]
    here_y = lax.axis_index("gy")
    total_y = NY * lax.axis_size("gy")
    lanes = lanes8()
    row = rows8()
    places = (here_y * NY + lanes).astype(F32)
    turn = 0.3 * (0.5 + 0.5 * places / total_y)
    moment = row < 4
    outw = outw_ref[...]
    hidden = jnp.tanh(jnp.dot(forward_ref[:, 0:80], feats[...], preferred_element_type=F32))
    sharp, keepers = [], []
    out_sums = jnp.zeros((2 * HID, NY), F32)
    for x in range(NX):
        unit = hidden[:, x * NY : (x + 1) * NY]
        weighed = unit * outw
        mixed = by_level(
            jnp.sum(weighed[:HID], 0, keepdims=True), jnp.sum(weighed[HID:], 0, keepdims=True)
        )
        gate = 1.0 / (1.0 + jnp.exp(-mixed))
        nu = jnp.where(moment, 0.24 * gate, 0.0)
        center = lines_ref[x]
        sx, sy, cx, cy = slope_x[x], slope_y[x], curve_x[x], curve_y[x]
        u = by_level(center[0:1], center[1:2])
        v = by_level(center[2:3], center[3:4])
        speed_u = jnp.sqrt(u * u + 0.01)
        speed_v = jnp.sqrt(v * v + 0.01)
        upwind = u * sx + v * sy - 0.5 * (speed_u * cx + speed_v * cy)
        twist = jnp.where(
            row < 2, pltpu.roll(center, 6, 0), jnp.where(moment, -pltpu.roll(center, 2, 0), 0.0)
        )
        rhs_ref[x] = wets[x] * (center - 0.3 * upwind + nu * (cx + cy) + turn * twist)
        g = adj[x]
        to_gate = jnp.where(moment, g * (cx + cy) * (0.24 * gate * (1.0 - gate)), 0.0)
        to_gate = to_gate + pltpu.roll(to_gate, 6, 0)
        gate_level = jnp.concatenate(
            [jnp.broadcast_to(to_gate[0:1], (HID, NY)), jnp.broadcast_to(to_gate[1:2], (HID, NY))],
            0,
        )
        out_sums = out_sums + unit * gate_level
        sharp.append((1.0 - unit * unit) * (outw * gate_level))
        along_u = g * (-0.3 * sx + 0.15 * (u / speed_u) * cx)
        along_v = g * (-0.3 * sy + 0.15 * (v / speed_v) * cy)
        along_u = along_u + pltpu.roll(along_u, 4, 0)
        along_u = along_u + pltpu.roll(along_u, 2, 0)
        along_v = along_v + pltpu.roll(along_v, 4, 0)
        along_v = along_v + pltpu.roll(along_v, 2, 0)
        untwist = jnp.where(
            row < 2, along_u - turn * pltpu.roll(g, 6, 0), along_v + turn * pltpu.roll(g, 2, 0)
        )
        bend_x = g * (0.15 * speed_u + nu)
        bend_y = g * (0.15 * speed_v + nu)
        middle = g + jnp.where(moment, untwist, 0.0) - 2.0 * (bend_x + bend_y)
        keepers.append((-0.3 * u * g, -0.3 * v * g, bend_x, bend_y, middle))
    stacked = jnp.concatenate(split(jnp.concatenate(sharp, 1)), 0)
    to_feats = jnp.dot(back_ref[...], stacked, preferred_element_type=F32)
    to_feats = to_feats[0:16] + to_feats[16:32]
    sums = lax.dot_general(
        stacked, feats[0:48, :], (((1,), (1,)), ((), ())), preferred_element_type=F32
    )

    load = rhs_ref[0]
    load_back = rhs_ref[NX - 1]
    for i in range(NX - 1):
        load = rhs_ref[i + 1] + right_ref[i] * load
        j = NX - 2 - i
        load_back = rhs_ref[j] + left_ref[j] * load_back
    first_own = load_back * jnp.where(
        (row & 2) == 0, got_ref[me, 16:24, :], pltpu.roll(got_ref[me, 16:24, :], 2, 0)
    )
    last_own = load * recip_ref[NX - 1]

    rim_north = jnp.zeros((ROWS, NY), F32)
    rim_south = jnp.zeros((ROWS, NY), F32)
    to_east, to_west, kept = [], [], []
    for x in range(NX):
        to_sx, to_sy, bend_x, bend_y, middle = keepers[x]
        mine = to_feats[:, x * NY : (x + 1) * NY]
        half_x = 0.5 * (to_sx + mine[0:8])
        half_y = 0.5 * (to_sy + mine[8:16])
        to_north = bend_y + half_y
        to_south = bend_y - half_y
        rim_north = jnp.where(lanes == RIM + x, pltpu.roll(to_north, RIM + x + 1, 1), rim_north)
        rim_south = jnp.where(lanes == RIM + x, pltpu.roll(to_south, RIM + x, 1), rim_south)
        to_east.append(bend_x + half_x)
        to_west.append(bend_x - half_x)
        kept.append(
            middle
            + jnp.where(lanes == 0, 0.0, pltpu.roll(to_north, 1, 1))
            + jnp.where(lanes == NY - 1, 0.0, pltpu.roll(to_south, NY - 1, 1))
        )
    for x in range(NX):
        total = kept[x]
        if x:
            total = total + to_east[x - 1]
        if x < NX - 1:
            total = total + to_west[x + 1]
        grad_ref[x] = total
    rims_ref[0] = rim_north
    rims_ref[1] = rim_south
    to_last = to_east[NX - 1]
    to_first = to_west[0]

    sums = sums[0:128] + sums[128:256]
    total = jnp.zeros((16, HID), F32)
    for level in range(2):
        source = iota((16, 48), 1)
        target = iota((16, 48), 0)
        feature = (source < 32) & ((source & 15) == 2 * target + level) & (target < FEAT)
        gather = feature | ((source == 32) & (target == FEAT))
        total += lax.dot_general(
            gather.astype(F32),
            sums[level * HID : (level + 1) * HID],
            (((1,), (1,)), ((), ())),
            precision=lax.Precision.HIGHEST,
            preferred_element_type=F32,
        )
    out_total = lax.dot_general(
        jnp.ones((8, 128), F32),
        out_sums[0:HID] + out_sums[HID:],
        (((1,), (1,)), ((), ())),
        precision=lax.Precision.HIGHEST,
        preferred_element_type=F32,
    )
    packed = pack(total[0:8], total[8:9], out_total[0:1])
    for j in range(count):
        send_ref[j, 0:8, :] = first_own
        send_ref[j, 8:16, :] = last_own
        send_ref[j, 16:24, :] = packed
        send_ref[j, 24:32, :] = jnp.where(j > me, to_last, to_first)


def share_kernel(
    second_ref, rims_ref, got_ref, rhs_ref, right_ref, recip_ref, send_ref, final_ref
):
    me_y = lax.axis_index("gy")
    me = lax.axis_index("gx")
    count = got_ref.shape[0]
    lanes = lanes8()
    total = second_ref[0, 16:24, :]
    for j in range(1, count):
        total = total + second_ref[j, 16:24, :]
    rim = (lanes >= RIM) & (lanes < RIM + NX)
    upward = jnp.where(rim, rims_ref[0], total)
    downward = jnp.where(rim, rims_ref[1], total)
    for j in range(send_ref.shape[0]):
        send_ref[j] = jnp.where(j > me_y, upward, downward)
    system = reduced(got_ref)
    first = [second_ref[j, 0:8, :] for j in range(count)]
    last = [second_ref[j, 8:16, :] for j in range(count)]
    fluxes = end_fluxes(system, first, last, me)

    def keep(x, value):
        final_ref[pl.ds(x, ROWS, stride=NX), :] = value

    own_lines(lambda x: rhs_ref[x], right_ref, recip_ref, fluxes, keep)


def finish_kernel(
    factor,
    third_ref,
    second_ref,
    grad_ref,
    final_ref,
    final_hbm,
    out_hbm,
    closure_hbm,
    closure_ref,
    out_ref,
    sems,
):
    copies = [pltpu.make_async_copy(final_ref, final_hbm, sems.at[0])]
    copies[0].start()
    me_x = lax.axis_index("gx")
    me_y = lax.axis_index("gy")
    count_x = second_ref.shape[0]
    count_y = third_ref.shape[0]
    lanes = lanes8()
    zero = jnp.zeros((ROWS, NY), F32)
    parts = [third_ref[j] for j in range(count_y)]
    while len(parts) > 1:
        parts = [a + b for a, b in zip(parts[::2], parts[1::2])]
    total = parts[0] * factor
    closure_ref[0:8, :] = total[:, 0:HID]
    for n in range(2):
        closure_ref[8 + n : 9 + n, :] = jnp.concatenate(
            [total[2 * n : 2 * n + 1, 96:], total[2 * n + 1 : 2 * n + 2, 96:]], 1
        )
    copies.append(pltpu.make_async_copy(closure_ref, closure_hbm, sems.at[1]))
    copies[1].start()
    before = jnp.where(me_x > 0, second_ref[jnp.maximum(me_x - 1, 0), 24:32, :], zero)
    after = jnp.where(
        me_x < count_x - 1, second_ref[jnp.minimum(me_x + 1, count_x - 1), 24:32, :], zero
    )
    south = jnp.where(me_y > 0, third_ref[jnp.maximum(me_y - 1, 0)], zero)
    north = jnp.where(me_y < count_y - 1, third_ref[jnp.minimum(me_y + 1, count_y - 1)], zero)
    for x in range(NX):
        value = grad_ref[x]
        if x == 0:
            value = value + before
        if x == NX - 1:
            value = value + after
        value = value + jnp.where(lanes == 0, pltpu.roll(south, NY - RIM - x, 1), 0.0)
        value = value + jnp.where(lanes == NY - 1, pltpu.roll(north, NY - 1 - RIM - x, 1), 0.0)
        out_ref[pl.ds(x, ROWS, stride=NX), :] = value
    copies.append(pltpu.make_async_copy(out_ref, out_hbm, sems.at[2]))
    copies[2].start()
    for copy in copies:
        copy.wait()


def tile(*shape):
    return jax.ShapeDtypeStruct(shape, F32)


def keep_in_hbm(values):
    return pltpu.with_memory_space_constraint(values, pltpu.HBM)


def params():
    return pltpu.CompilerParams(vmem_limit_bytes=40 * 1024 * 1024)


def per_device(state, diffusivity, sea_mask, depth_index, closure_in, closure_out, cotangent):
    count_x = lax.axis_size("gx")
    count_y = lax.axis_size("gy")
    lines = tile(NX, ROWS, NY)
    in_hbm = pl.BlockSpec(memory_space=pltpu.HBM)
    in_vmem = pl.BlockSpec(memory_space=pltpu.VMEM)
    ints = jax.ShapeDtypeStruct((NX, NY), jnp.int32)
    fields, first, last, diff, sea, depth, cot = pl.pallas_call(
        load_kernel,
        in_specs=[in_hbm] * 5,
        out_shape=(
            lines,
            tile(ROWS, NY),
            tile(ROWS, NY),
            tile(2 * NX, NY),
            ints,
            ints,
            tile(ROWS * NX, NY),
        ),
        scratch_shapes=[pltpu.VMEM((ROWS * NX, NY), F32), pltpu.SemaphoreType.DMA((5,))],
        compiler_params=params(),
    )(
        keep_in_hbm(state.reshape(ROWS * NX, NY)),
        keep_in_hbm(diffusivity.reshape(2 * NX, NY)),
        keep_in_hbm(sea_mask),
        keep_in_hbm(depth_index),
        keep_in_hbm(cotangent.reshape(ROWS * NX, NY)),
    )
    send, right, recip, left, wets = pl.pallas_call(
        factor_kernel,
        out_shape=(tile(count_x, 40, NY),) + (lines,) * 4,
        compiler_params=params(),
    )(fields, diff, sea, depth, cot)
    got = lax.all_to_all(send, "gx", 0, 0, tiled=True)
    low = lax.ppermute(last, "gy", [(i, (i + 1) % count_y) for i in range(count_y)])
    high = lax.ppermute(first, "gy", [((i + 1) % count_y, i) for i in range(count_y)])
    forward, back, outw = pl.pallas_call(
        network_kernel,
        out_shape=(
            jax.ShapeDtypeStruct((2 * HID, 128), BF16),
            jax.ShapeDtypeStruct((32, 256), BF16),
            tile(2 * HID, 128),
        ),
        compiler_params=params(),
    )(closure_in.T, closure_out.reshape(1, HID))
    adj = pl.pallas_call(adjoint_kernel, out_shape=lines, compiler_params=params())(
        got, cot, wets, right, recip
    )
    feats_shape = jax.ShapeDtypeStruct((80, NX * NY), BF16)
    stencil = pl.pallas_call(
        stencil_kernel, out_shape=(lines,) * 4 + (feats_shape,), compiler_params=params()
    )(got, low, high, fields)
    send, rhs, grad, rims = pl.pallas_call(
        closure_kernel,
        out_shape=(tile(count_x, 32, NY), lines, lines, tile(2, ROWS, NY)),
        compiler_params=params(),
    )(got, fields, wets, adj, *stencil, forward, back, outw, right, recip, left)
    second = lax.all_to_all(send, "gx", 0, 0, tiled=True)
    send, final = pl.pallas_call(
        share_kernel,
        out_shape=(tile(count_y, ROWS, NY), tile(ROWS * NX, NY)),
        compiler_params=params(),
    )(second, rims, got, rhs, right, recip)
    third = lax.all_to_all(send, "gy", 0, 0, tiled=True)
    factor = 1.0 / math.sqrt(2 * NX * count_x * NY * count_y)

    def finish(*refs):
        finish_kernel(factor, *refs)

    final, state_grad, closure_grad = pl.pallas_call(
        finish,
        in_specs=[in_vmem] * 4,
        out_shape=(tile(ROWS * NX, NY), tile(ROWS * NX, NY), tile(10, HID)),
        out_specs=(in_hbm,) * 3,
        scratch_shapes=[
            pltpu.VMEM((10, HID), F32),
            pltpu.VMEM((ROWS * NX, NY), F32),
            pltpu.SemaphoreType.DMA((3,)),
        ],
        compiler_params=params(),
    )(third, second, grad, final)
    return (final.reshape(state.shape), state_grad.reshape(state.shape), closure_grad.T)


def solution(mesh):
    return jax.shard_map(
        per_device,
        mesh=mesh,
        in_specs=(
            P(None, None, "gx", "gy"),
            P(None, "gx", "gy"),
            P("gx", "gy"),
            P("gx", "gy"),
            P(),
            P(),
            P(None, None, "gx", "gy"),
        ),
        out_specs=(P(None, None, "gx", "gy"), P(None, None, "gx", "gy"), P()),
        check_vma=False,
    )
```

```python
import math

import jax
import jax.numpy as jnp
from jax import lax
from jax.experimental import pallas as pl
from jax.experimental.pallas import tpu as pltpu
from jax.sharding import PartitionSpec as P

F32 = jnp.float32
BF16 = jnp.bfloat16
DIFFUSE = 2048.0
FEAT = 8
HID = 64
NX = 32
NY = 128
XS = 8
ROWS = 8
RIM = 64


def iota(shape, dim):
    return lax.broadcasted_iota(jnp.int32, shape, dim)


def rows8():
    return iota((ROWS, NY), 0)


def lanes8():
    return iota((ROWS, NY), 1)


def wide(row):
    return jnp.broadcast_to(row, (ROWS, NY))


def by_level(first, second):
    return jnp.where((rows8() & 1) == 0, wide(first), wide(second))


def line(ref, x):
    return ref[pl.ds(x, ROWS, stride=NX), :]


def wet_line(sea_ref, depth_ref, x):
    sea = wide(sea_ref[x : x + 1, :])
    depth = wide(depth_ref[x : x + 1, :])
    return jnp.where(((rows8() & 1) < depth) & (sea > 0), 1.0, 0.0).astype(F32)


def rates8():
    return jnp.where(rows8() < 4, DIFFUSE, 0.5).astype(F32)


def split(values):
    high = values.astype(BF16)
    return high, (values - high.astype(F32)).astype(BF16)


def load_kernel(
    state_hbm,
    diff_hbm,
    sea_hbm,
    depth_hbm,
    cot_hbm,
    fields_ref,
    first_ref,
    last_ref,
    diff_ref,
    sea_ref,
    depth_ref,
    cot_ref,
    state_ref,
    sems,
):
    copies = [
        pltpu.make_async_copy(source, target, sems.at[n])
        for n, (source, target) in enumerate(
            (
                (state_hbm, state_ref),
                (sea_hbm, sea_ref),
                (depth_hbm, depth_ref),
                (diff_hbm, diff_ref),
                (cot_hbm, cot_ref),
            )
        )
    ]
    for copy in copies:
        copy.start()
    copies[0].wait()
    lanes = lanes8()
    first = jnp.zeros((ROWS, NY), F32)
    last = jnp.zeros((ROWS, NY), F32)
    for x in range(NX):
        here = line(state_ref, x)
        fields_ref[x] = here
        first = jnp.where(lanes == x, pltpu.roll(here, x, 1) if x else here, first)
        last = jnp.where(lanes == x, pltpu.roll(here, x + 1, 1), last)
    first_ref[...] = first
    last_ref[...] = last
    for copy in copies[1:]:
        copy.wait()


def factor_kernel(
    fields_ref,
    diff_ref,
    sea_ref,
    depth_ref,
    cot_ref,
    send_ref,
    right_ref,
    recip_ref,
    left_ref,
    wets_ref,
):
    me = lax.axis_index("gx")
    count = send_ref.shape[0]
    row = rows8()
    wet = [wet_line(sea_ref, depth_ref, x) for x in range(NX)]
    for x in range(NX):
        wets_ref[x] = wet[x]
    rates = rates8()
    bare = [
        by_level(diff_ref[x : x + 1, :], diff_ref[NX + x : NX + x + 1, :]) * wet[x]
        for x in range(NX)
    ]
    cond = [rates * bare[x] * wet[x + 1] for x in range(NX - 1)]
    mass = jnp.ones((ROWS, NY), F32)
    carry = jnp.ones((ROWS, NY), F32)
    mass_back = jnp.ones((ROWS, NY), F32)
    cots = [line(cot_ref, x) for x in range(NX)]
    backs = []
    load = cots[0]
    load_back = cots[NX - 1]
    for i in range(NX - 1):
        recip = 1.0 / (mass + cond[i])
        ratio = cond[i] * recip
        right_ref[i] = ratio
        recip_ref[i] = recip
        mass = 1.0 + mass * ratio
        load = cots[i + 1] + ratio * load
        carry = carry * ratio
        j = NX - 2 - i
        ratio_back = cond[j] / (mass_back + cond[j])
        backs.append(ratio_back)
        mass_back = 1.0 + mass_back * ratio_back
        load_back = cots[j] + ratio_back * load_back
    last_self = 1.0 / mass
    first_self = 1.0 / mass_back
    right_ref[NX - 1] = jnp.zeros((ROWS, NY), F32)
    product = backs[NX - 2]
    for x in range(1, NX):
        left_ref[x] = product
        if x < NX - 1:
            product = product * backs[NX - 2 - x]
    recip_ref[NX - 1] = last_self
    across = carry * last_self
    upper = (row & 2) == 0
    tiles = [
        load_back * first_self,
        load * last_self,
        jnp.where(upper, first_self, across),
        jnp.where(upper, last_self, jnp.where(row < 4, bare[NX - 1], wet[0])),
    ]
    own_last = fields_ref[NX - 1]
    own_first = fields_ref[0]
    for j in range(count):
        for n, tile in enumerate(tiles):
            send_ref[j, ROWS * n : ROWS * (n + 1), :] = tile
        send_ref[j, ROWS * 4 :, :] = jnp.where(j > me, own_last, own_first)


def reduced(got_ref):
    count = got_ref.shape[0]
    upper = (rows8() & 2) == 0
    first_self, across, last_self, bare, wet = [], [], [], [], []
    for j in range(count):
        tile = got_ref[j, 16:24, :]
        first_self.append(jnp.where(upper, tile, pltpu.roll(tile, 2, 0)))
        across.append(jnp.where(upper, pltpu.roll(tile, 6, 0), tile))
        tile = got_ref[j, 24:32, :]
        last_self.append(jnp.where(upper, tile, pltpu.roll(tile, 2, 0)))
        bare.append(by_level(got_ref[j, 26:27, :], got_ref[j, 27:28, :]))
        wet.append(by_level(got_ref[j, 30:31, :], got_ref[j, 31:32, :]))
    face = [rates8() * bare[j] * wet[j + 1] for j in range(count - 1)]
    return first_self, across, last_self, face


def end_fluxes(system, first, last, me):
    first_self, across, last_self, face = system
    count = len(first_self)
    zero = jnp.zeros((ROWS, NY), F32)
    give, value = last_self[0], last[0]
    gives, values, links = [give], [value], [zero]
    for j in range(1, count):
        link = face[j - 1] / (1.0 + face[j - 1] * (give + first_self[j]))
        pull = across[j] * link
        value = last[j] + pull * (value - first[j])
        give = last_self[j] - pull * across[j]
        gives.append(give)
        values.append(value)
        links.append(link)
    back_give, back_value = first_self[count - 1], first[count - 1]
    right_flux = [None] * count
    right_flux[count - 1] = zero
    for j in range(count - 2, -1, -1):
        right_flux[j] = (
            face[j] * (back_value - values[j]) / (1.0 + face[j] * (back_give + gives[j]))
        )
        link = face[j] / (1.0 + face[j] * (back_give + last_self[j]))
        pull = across[j] * link
        back_value = first[j] + pull * (back_value - last[j])
        back_give = first_self[j] - pull * across[j]
    left, right = zero, right_flux[0]
    for j in range(1, count):
        here = links[j] * (values[j - 1] - first[j] - across[j] * right_flux[j])
        left = jnp.where(me == j, here, left)
        right = jnp.where(me == j, right_flux[j], right)
    return left, right


def own_lines(read, right_ref, recip_ref, fluxes, write):
    left, right = fluxes
    load = read(0) + left
    loads = [load]
    for i in range(1, NX):
        load = read(i) + right_ref[i - 1] * load
        loads.append(load)
    value = (loads[NX - 1] + right) * recip_ref[NX - 1]
    write(NX - 1, value)
    for i in range(NX - 2, -1, -1):
        value = right_ref[i] * value + recip_ref[i] * loads[i]
        write(i, value)


def network_kernel(weights_ref, out_ref, forward_ref, back_ref, outw_ref, outr_ref):
    weights = weights_ref[...]
    per_level = []
    for level in range(2):
        spread = iota((16, FEAT + 1), 0) == 2 * iota((16, FEAT + 1), 1) + level
        per_level.append(
            jnp.dot(
                spread.astype(F32),
                weights,
                precision=lax.Precision.HIGHEST,
                preferred_element_type=F32,
            )
        )
    both = jnp.concatenate(per_level, 1)
    high = both.astype(BF16).astype(F32)
    low = both - high
    bias = weights[FEAT : FEAT + 1, :]
    bias = jnp.broadcast_to(jnp.concatenate([bias, bias], 1), (16, 2 * HID))
    bias_high = bias.astype(BF16).astype(F32)
    bias_mid = (bias - bias_high).astype(BF16).astype(F32)
    bias_low = bias - bias_high - bias_mid
    row = iota((16, 2 * HID), 0)
    bias = jnp.where(
        row == 0, bias_high, jnp.where(row == 1, bias_mid, jnp.where(row == 2, bias_low, 0.0))
    )
    stack = jnp.concatenate([high, high, bias, low, low, jnp.zeros((48, 2 * HID), F32)], 0)
    forward_ref[...] = jnp.transpose(stack).astype(BF16)
    out = out_ref[...]
    out = jnp.broadcast_to(jnp.concatenate([out, out], 1), (2 * HID, 2 * HID))
    outw_ref[...] = jnp.transpose(out)
    outr_ref[...] = out[0:48]
    scaled = both * out[0:16]
    turned = jnp.concatenate(split(scaled), 0)
    back_ref[...] = jnp.concatenate([turned, turned], 1)


def pack(features, bias, out):
    blank = jnp.zeros((ROWS, HID), F32)
    row = iota((ROWS, 32), 0)
    ends = [
        jnp.broadcast_to(v, (ROWS, 32))
        for v in (bias[:, 0:32], bias[:, 32:64], out[:, 0:32], out[:, 32:64])
    ]
    tail = jnp.zeros((ROWS, 32), F32)
    for n, end in enumerate(ends):
        tail = jnp.where(row == n, end, tail)
    return jnp.concatenate([features, blank[:, :32], tail], 1)


def adjoint_kernel(
    got_ref, cot_ref, wets_ref, right_ref, recip_ref, lines_ref, adj_ref, slope_x, curve_x
):
    me = lax.axis_index("gx")
    count = got_ref.shape[0]
    zero = jnp.zeros((ROWS, NY), F32)
    below = got_ref[jnp.maximum(me - 1, 0), 32:40, :]
    above = got_ref[jnp.minimum(me + 1, count - 1), 32:40, :]
    below = jnp.where(me > 0, below, zero)
    above = jnp.where(me < count - 1, above, zero)
    for x in range(NX):
        east = lines_ref[x + 1] if x < NX - 1 else above
        west = lines_ref[x - 1] if x else below
        slope_x[x] = 0.5 * (east - west)
        curve_x[x] = east - 2.0 * lines_ref[x] + west
    system = reduced(got_ref)
    first = [got_ref[j, 0:8, :] for j in range(count)]
    last = [got_ref[j, 8:16, :] for j in range(count)]
    fluxes = end_fluxes(system, first, last, me)

    def keep(x, value):
        adj_ref[x] = wets_ref[x] * value

    own_lines(lambda x: line(cot_ref, x), right_ref, recip_ref, fluxes, keep)


def stencil_kernel(low_ref, high_ref, lines_ref, slope_x, slope_y, curve_y, feats):
    here_y = lax.axis_index("gy")
    lanes = lanes8()
    zero = jnp.zeros((ROWS, NY), F32)
    low = jnp.where(here_y > 0, low_ref[...], zero)
    high = jnp.where(here_y < lax.axis_size("gy") - 1, high_ref[...], zero)
    feats[32:48, :] = jnp.ones((16, NX * NY), BF16)
    for x in range(NX):
        center = lines_ref[x]
        south = jnp.where(
            lanes == 0, pltpu.roll(low, (-x) % NY, 1) if x else low, pltpu.roll(center, 1, 1)
        )
        north = jnp.where(
            lanes == NY - 1, pltpu.roll(high, NY - 1 - x, 1), pltpu.roll(center, NY - 1, 1)
        )
        sy = 0.5 * (north - south)
        slope_y[x] = sy
        curve_y[x] = north - 2.0 * center + south
        part_high, part_low = split(jnp.concatenate([slope_x[x], sy], 0))
        place = slice(x * NY, (x + 1) * NY)
        feats[0:16, place] = part_high
        feats[16:32, place] = part_low
        feats[48:64, place] = part_high
        feats[64:80, place] = part_low


def closure_kernel(
    got_ref,
    lines_ref,
    wets,
    adj,
    slope_x,
    slope_y,
    curve_x,
    curve_y,
    feats,
    forward_ref,
    back_ref,
    outw_ref,
    outr_ref,
    right_ref,
    recip_ref,
    left_ref,
    send_ref,
    rhs_ref,
    grad_ref,
    rims_ref,
    pairs_ref,
):
    me = lax.axis_index("gx")
    count = got_ref.shape[0]
    here_y = lax.axis_index("gy")
    total_y = NY * lax.axis_size("gy")
    lanes = lanes8()
    row = rows8()
    places = (here_y * NY + lanes).astype(F32)
    turn = 0.3 * (0.5 + 0.5 * places / total_y)
    moment = row < 4
    outw = outw_ref[...]
    sharp, keepers, to_feats = [], [], []
    sums = jnp.zeros((48, 256), F32)
    out_sums = jnp.zeros((2 * HID, NY), F32)
    load = load_back = jnp.zeros((ROWS, NY), F32)
    for x in range(NX):
        if x % XS == 0:
            place = slice(x * NY, (x + XS) * NY)
            hidden = jnp.tanh(
                jnp.dot(forward_ref[:, 0:80], feats[:, place], preferred_element_type=F32)
            )
        unit = hidden[:, (x % XS) * NY : (x % XS + 1) * NY]
        weighed = unit * outw
        mixed = by_level(
            jnp.sum(weighed[:HID], 0, keepdims=True), jnp.sum(weighed[HID:], 0, keepdims=True)
        )
        gate = 1.0 / (1.0 + jnp.exp(-mixed))
        nu = jnp.where(moment, 0.24 * gate, 0.0)
        center = lines_ref[x]
        sx, sy, cx, cy = slope_x[x], slope_y[x], curve_x[x], curve_y[x]
        u = by_level(center[0:1], center[1:2])
        v = by_level(center[2:3], center[3:4])
        speed_u = jnp.sqrt(u * u + 0.01)
        speed_v = jnp.sqrt(v * v + 0.01)
        upwind = u * sx + v * sy - 0.5 * (speed_u * cx + speed_v * cy)
        twist = jnp.where(
            row < 2, pltpu.roll(center, 6, 0), jnp.where(moment, -pltpu.roll(center, 2, 0), 0.0)
        )
        explicit = wets[x] * (center - 0.3 * upwind + nu * (cx + cy) + turn * twist)
        rhs_ref[x] = explicit
        load = explicit + right_ref[x - 1] * load if x else explicit
        load_back = load_back + left_ref[x] * explicit if x else explicit
        g = adj[x]
        to_gate = jnp.where(moment, g * (cx + cy) * (0.24 * gate * (1.0 - gate)), 0.0)
        to_gate = to_gate + pltpu.roll(to_gate, 6, 0)
        gate_level = jnp.concatenate(
            [jnp.broadcast_to(to_gate[0:1], (HID, NY)), jnp.broadcast_to(to_gate[1:2], (HID, NY))],
            0,
        )
        pulled = unit * gate_level
        out_sums = out_sums + pulled
        sharp.append(gate_level - unit * pulled)
        along_u = g * (-0.3 * sx + 0.15 * (u / speed_u) * cx)
        along_v = g * (-0.3 * sy + 0.15 * (v / speed_v) * cy)
        along_u = along_u + pltpu.roll(along_u, 4, 0)
        along_u = along_u + pltpu.roll(along_u, 2, 0)
        along_v = along_v + pltpu.roll(along_v, 4, 0)
        along_v = along_v + pltpu.roll(along_v, 2, 0)
        untwist = jnp.where(
            row < 2, along_u - turn * pltpu.roll(g, 6, 0), along_v + turn * pltpu.roll(g, 2, 0)
        )
        bend_x = g * (0.15 * speed_u + nu)
        bend_y = g * (0.15 * speed_v + nu)
        middle = g + jnp.where(moment, untwist, 0.0) - 2.0 * (bend_x + bend_y)
        keepers.append((-0.3 * u * g, -0.3 * v * g, bend_x, bend_y, middle))
        if x % XS == XS - 1:
            stacked = jnp.concatenate(split(jnp.concatenate(sharp, 1)), 0)
            sharp = []
            back = jnp.dot(back_ref[...], stacked, preferred_element_type=F32)
            to_feats.append(back[0:16] + back[16:32])
            sums = sums + lax.dot_general(
                feats[0:48, place], stacked, (((1,), (1,)), ((), ())), preferred_element_type=F32
            )

    first_own = load_back * jnp.where(
        (row & 2) == 0, got_ref[me, 16:24, :], pltpu.roll(got_ref[me, 16:24, :], 2, 0)
    )
    last_own = load * recip_ref[NX - 1]

    rim_north = jnp.zeros((ROWS, NY), F32)
    rim_south = jnp.zeros((ROWS, NY), F32)
    to_east, to_west, kept = [], [], []
    for x in range(NX):
        to_sx, to_sy, bend_x, bend_y, middle = keepers[x]
        mine = to_feats[x // XS][:, (x % XS) * NY : (x % XS + 1) * NY]
        half_x = 0.5 * (to_sx + mine[0:8])
        half_y = 0.5 * (to_sy + mine[8:16])
        to_north = bend_y + half_y
        to_south = bend_y - half_y
        rim_north = jnp.where(lanes == RIM + x, pltpu.roll(to_north, RIM + x + 1, 1), rim_north)
        rim_south = jnp.where(lanes == RIM + x, pltpu.roll(to_south, RIM + x, 1), rim_south)
        to_east.append(bend_x + half_x)
        to_west.append(bend_x - half_x)
        kept.append(
            middle
            + jnp.where(lanes == 0, 0.0, pltpu.roll(to_north, 1, 1))
            + jnp.where(lanes == NY - 1, 0.0, pltpu.roll(to_south, NY - 1, 1))
        )
    for x in range(NX):
        total = kept[x]
        if x:
            total = total + to_east[x - 1]
        if x < NX - 1:
            total = total + to_west[x + 1]
        grad_ref[x] = total
    rims_ref[0] = rim_north
    rims_ref[1] = rim_south
    to_last = to_east[NX - 1]
    to_first = to_west[0]

    sums = (sums[:, 0:128] + sums[:, 128:256]) * outr_ref[...]
    pairs_ref[...] = sums[0:16] + sums[16:32]
    features = pairs_ref[pl.ds(0, 8, stride=2), :] + pltpu.roll(
        pairs_ref[pl.ds(1, 8, stride=2), :], HID, 1
    )
    bias = sums[32:40] + pltpu.roll(sums[32:40], HID, 1)
    out_total = jnp.sum(jnp.transpose(out_sums[0:HID] + out_sums[HID:]), 0, keepdims=True)
    packed = pack(features[:, 0:HID], bias[0:1, 0:HID], out_total)
    for j in range(count):
        send_ref[j, 0:8, :] = first_own
        send_ref[j, 8:16, :] = last_own
        send_ref[j, 16:24, :] = packed
        send_ref[j, 24:32, :] = jnp.where(j > me, to_last, to_first)


def share_kernel(
    second_ref, rims_ref, got_ref, rhs_ref, right_ref, recip_ref, send_ref, final_ref
):
    me_y = lax.axis_index("gy")
    me = lax.axis_index("gx")
    count = got_ref.shape[0]
    lanes = lanes8()
    total = second_ref[0, 16:24, :]
    for j in range(1, count):
        total = total + second_ref[j, 16:24, :]
    rim = (lanes >= RIM) & (lanes < RIM + NX)
    upward = jnp.where(rim, rims_ref[0], total)
    downward = jnp.where(rim, rims_ref[1], total)
    for j in range(send_ref.shape[0]):
        send_ref[j] = jnp.where(j > me_y, upward, downward)
    system = reduced(got_ref)
    first = [second_ref[j, 0:8, :] for j in range(count)]
    last = [second_ref[j, 8:16, :] for j in range(count)]
    fluxes = end_fluxes(system, first, last, me)

    def keep(x, value):
        final_ref[pl.ds(x, ROWS, stride=NX), :] = value

    own_lines(lambda x: rhs_ref[x], right_ref, recip_ref, fluxes, keep)


def finish_kernel(
    factor,
    third_ref,
    second_ref,
    grad_ref,
    final_ref,
    final_hbm,
    out_hbm,
    closure_hbm,
    closure_ref,
    out_ref,
    sems,
):
    copies = [pltpu.make_async_copy(final_ref, final_hbm, sems.at[0])]
    copies[0].start()
    me_x = lax.axis_index("gx")
    me_y = lax.axis_index("gy")
    count_x = second_ref.shape[0]
    count_y = third_ref.shape[0]
    lanes = lanes8()
    zero = jnp.zeros((ROWS, NY), F32)
    parts = [third_ref[j] for j in range(count_y)]
    while len(parts) > 1:
        parts = [a + b for a, b in zip(parts[::2], parts[1::2])]
    total = parts[0] * factor
    closure_ref[0:8, :] = total[:, 0:HID]
    for n in range(2):
        closure_ref[8 + n : 9 + n, :] = jnp.concatenate(
            [total[2 * n : 2 * n + 1, 96:], total[2 * n + 1 : 2 * n + 2, 96:]], 1
        )
    copies.append(pltpu.make_async_copy(closure_ref, closure_hbm, sems.at[1]))
    copies[1].start()
    before = jnp.where(me_x > 0, second_ref[jnp.maximum(me_x - 1, 0), 24:32, :], zero)
    after = jnp.where(
        me_x < count_x - 1, second_ref[jnp.minimum(me_x + 1, count_x - 1), 24:32, :], zero
    )
    south = jnp.where(me_y > 0, third_ref[jnp.maximum(me_y - 1, 0)], zero)
    north = jnp.where(me_y < count_y - 1, third_ref[jnp.minimum(me_y + 1, count_y - 1)], zero)
    for x in range(NX):
        value = grad_ref[x]
        if x == 0:
            value = value + before
        if x == NX - 1:
            value = value + after
        value = value + jnp.where(lanes == 0, pltpu.roll(south, NY - RIM - x, 1), 0.0)
        value = value + jnp.where(lanes == NY - 1, pltpu.roll(north, NY - 1 - RIM - x, 1), 0.0)
        out_ref[pl.ds(x, ROWS, stride=NX), :] = value
    copies.append(pltpu.make_async_copy(out_ref, out_hbm, sems.at[2]))
    copies[2].start()
    for copy in copies:
        copy.wait()


def tile(*shape):
    return jax.ShapeDtypeStruct(shape, F32)


def keep_in_hbm(values):
    return pltpu.with_memory_space_constraint(values, pltpu.HBM)


def params():
    return pltpu.CompilerParams(vmem_limit_bytes=40 * 1024 * 1024)


def per_device(state, diffusivity, sea_mask, depth_index, closure_in, closure_out, cotangent):
    count_x = lax.axis_size("gx")
    count_y = lax.axis_size("gy")
    lines = tile(NX, ROWS, NY)
    in_hbm = pl.BlockSpec(memory_space=pltpu.HBM)
    in_vmem = pl.BlockSpec(memory_space=pltpu.VMEM)
    ints = jax.ShapeDtypeStruct((NX, NY), jnp.int32)
    fields, first, last, diff, sea, depth, cot = pl.pallas_call(
        load_kernel,
        in_specs=[in_hbm] * 5,
        out_shape=(
            lines,
            tile(ROWS, NY),
            tile(ROWS, NY),
            tile(2 * NX, NY),
            ints,
            ints,
            tile(ROWS * NX, NY),
        ),
        scratch_shapes=[pltpu.VMEM((ROWS * NX, NY), F32), pltpu.SemaphoreType.DMA((5,))],
        compiler_params=params(),
    )(
        keep_in_hbm(state.reshape(ROWS * NX, NY)),
        keep_in_hbm(diffusivity.reshape(2 * NX, NY)),
        keep_in_hbm(sea_mask),
        keep_in_hbm(depth_index),
        keep_in_hbm(cotangent.reshape(ROWS * NX, NY)),
    )
    send, right, recip, left, wets = pl.pallas_call(
        factor_kernel,
        out_shape=(tile(count_x, 40, NY),) + (lines,) * 4,
        compiler_params=params(),
    )(fields, diff, sea, depth, cot)
    got = lax.all_to_all(send, "gx", 0, 0, tiled=True)
    low = lax.ppermute(last, "gy", [(i, (i + 1) % count_y) for i in range(count_y)])
    high = lax.ppermute(first, "gy", [((i + 1) % count_y, i) for i in range(count_y)])
    forward, back, outw, outr = pl.pallas_call(
        network_kernel,
        out_shape=(
            jax.ShapeDtypeStruct((2 * HID, 128), BF16),
            jax.ShapeDtypeStruct((32, 256), BF16),
            tile(2 * HID, 128),
            tile(48, 128),
        ),
        compiler_params=params(),
    )(closure_in.T, closure_out.reshape(1, HID))
    adj, slope_x, curve_x = pl.pallas_call(
        adjoint_kernel, out_shape=(lines,) * 3, compiler_params=params()
    )(got, cot, wets, right, recip, fields)
    feats_shape = jax.ShapeDtypeStruct((80, NX * NY), BF16)
    slope_y, curve_y, feats = pl.pallas_call(
        stencil_kernel, out_shape=(lines,) * 2 + (feats_shape,), compiler_params=params()
    )(low, high, fields, slope_x)
    send, rhs, grad, rims = pl.pallas_call(
        closure_kernel,
        out_shape=(tile(count_x, 32, NY), lines, lines, tile(2, ROWS, NY)),
        scratch_shapes=[pltpu.VMEM((16, 128), F32)],
        compiler_params=params(),
    )(got, fields, wets, adj, slope_x, slope_y, curve_x, curve_y, feats, forward, back, outw, outr, right, recip, left)
    second = lax.all_to_all(send, "gx", 0, 0, tiled=True)
    send, final = pl.pallas_call(
        share_kernel,
        out_shape=(tile(count_y, ROWS, NY), tile(ROWS * NX, NY)),
        compiler_params=params(),
    )(second, rims, got, rhs, right, recip)
    third = lax.all_to_all(send, "gy", 0, 0, tiled=True)
    factor = 1.0 / math.sqrt(2 * NX * count_x * NY * count_y)

    def finish(*refs):
        finish_kernel(factor, *refs)

    final, state_grad, closure_grad = pl.pallas_call(
        finish,
        in_specs=[in_vmem] * 4,
        out_shape=(tile(ROWS * NX, NY), tile(ROWS * NX, NY), tile(10, HID)),
        out_specs=(in_hbm,) * 3,
        scratch_shapes=[
            pltpu.VMEM((10, HID), F32),
            pltpu.VMEM((ROWS * NX, NY), F32),
            pltpu.SemaphoreType.DMA((3,)),
        ],
        compiler_params=params(),
    )(third, second, grad, final)
    return (final.reshape(state.shape), state_grad.reshape(state.shape), closure_grad.T)


def solution(mesh):
    return jax.shard_map(
        per_device,
        mesh=mesh,
        in_specs=(
            P(None, None, "gx", "gy"),
            P(None, "gx", "gy"),
            P("gx", "gy"),
            P("gx", "gy"),
            P(),
            P(),
            P(None, None, "gx", "gy"),
        ),
        out_specs=(P(None, None, "gx", "gy"), P(None, None, "gx", "gy"), P()),
        check_vma=False,
    )
```

```python
import math

import jax
import jax.numpy as jnp
from jax import lax
from jax.experimental import pallas as pl
from jax.experimental.pallas import tpu as pltpu
from jax.sharding import PartitionSpec as P

F32 = jnp.float32
BF16 = jnp.bfloat16
DIFFUSE = 2048.0
FEAT = 8
HID = 64
NX = 32
NY = 128
XS = 8
ROWS = 8
RIM = 64


def iota(shape, dim):
    return lax.broadcasted_iota(jnp.int32, shape, dim)


def rows8():
    return iota((ROWS, NY), 0)


def lanes8():
    return iota((ROWS, NY), 1)


def wide(row):
    return jnp.broadcast_to(row, (ROWS, NY))


def by_level(first, second):
    return jnp.where((rows8() & 1) == 0, wide(first), wide(second))


def line(ref, x):
    return ref[pl.ds(x, ROWS, stride=NX), :]


def wet_line(sea_ref, depth_ref, x):
    sea = wide(sea_ref[x : x + 1, :])
    depth = wide(depth_ref[x : x + 1, :])
    return jnp.where(((rows8() & 1) < depth) & (sea > 0), 1.0, 0.0).astype(F32)


def rates8():
    return jnp.where(rows8() < 4, DIFFUSE, 0.5).astype(F32)


def split(values):
    high = values.astype(BF16)
    return high, (values - high.astype(F32)).astype(BF16)


def load_kernel(
    state_hbm,
    diff_hbm,
    sea_hbm,
    depth_hbm,
    cot_hbm,
    fields_ref,
    first_ref,
    last_ref,
    diff_ref,
    sea_ref,
    depth_ref,
    cot_ref,
    state_ref,
    sems,
):
    copies = [
        pltpu.make_async_copy(source, target, sems.at[n])
        for n, (source, target) in enumerate(
            (
                (state_hbm, state_ref),
                (sea_hbm, sea_ref),
                (depth_hbm, depth_ref),
                (diff_hbm, diff_ref),
                (cot_hbm, cot_ref),
            )
        )
    ]
    for copy in copies:
        copy.start()
    copies[0].wait()
    lanes = lanes8()
    first = jnp.zeros((ROWS, NY), F32)
    last = jnp.zeros((ROWS, NY), F32)
    for x in range(NX):
        here = line(state_ref, x)
        fields_ref[x] = here
        first = jnp.where(lanes == x, pltpu.roll(here, x, 1) if x else here, first)
        last = jnp.where(lanes == x, pltpu.roll(here, x + 1, 1), last)
    first_ref[...] = first
    last_ref[...] = last
    for copy in copies[1:]:
        copy.wait()


def factor_kernel(
    fields_ref,
    diff_ref,
    sea_ref,
    depth_ref,
    cot_ref,
    send_ref,
    right_ref,
    recip_ref,
    left_ref,
    wets_ref,
):
    row = rows8()
    wet = [wet_line(sea_ref, depth_ref, x) for x in range(NX)]
    for x in range(NX):
        wets_ref[x] = wet[x]
    rates = rates8()
    bare = [
        by_level(diff_ref[x : x + 1, :], diff_ref[NX + x : NX + x + 1, :]) * wet[x]
        for x in range(NX)
    ]
    cond = [rates * bare[x] * wet[x + 1] for x in range(NX - 1)]
    mass = jnp.ones((ROWS, NY), F32)
    carry = jnp.ones((ROWS, NY), F32)
    mass_back = jnp.ones((ROWS, NY), F32)
    cots = [line(cot_ref, x) for x in range(NX)]
    backs = []
    load = cots[0]
    load_back = cots[NX - 1]
    for i in range(NX - 1):
        recip = 1.0 / (mass + cond[i])
        ratio = cond[i] * recip
        right_ref[i] = ratio
        recip_ref[i] = recip
        mass = 1.0 + mass * ratio
        load = cots[i + 1] + ratio * load
        carry = carry * ratio
        j = NX - 2 - i
        ratio_back = cond[j] / (mass_back + cond[j])
        backs.append(ratio_back)
        mass_back = 1.0 + mass_back * ratio_back
        load_back = cots[j] + ratio_back * load_back
    last_self = 1.0 / mass
    first_self = 1.0 / mass_back
    right_ref[NX - 1] = jnp.zeros((ROWS, NY), F32)
    product = backs[NX - 2]
    for x in range(1, NX):
        left_ref[x] = product
        if x < NX - 1:
            product = product * backs[NX - 2 - x]
    recip_ref[NX - 1] = last_self
    across = carry * last_self
    upper = (row & 2) == 0
    tiles = [
        load_back * first_self,
        load * last_self,
        jnp.where(upper, first_self, across),
        jnp.where(upper, last_self, jnp.where(row < 4, bare[NX - 1], wet[0])),
    ]
    tiles += [fields_ref[0], fields_ref[NX - 1]]
    for n, tile in enumerate(tiles):
        send_ref[ROWS * n : ROWS * (n + 1), :] = tile


def two_port(responses, far_response):
    upper = (rows8() & 2) == 0
    return (
        jnp.where(upper, responses, pltpu.roll(responses, 2, 0)),
        jnp.where(upper, pltpu.roll(responses, 6, 0), responses),
        jnp.where(upper, far_response, pltpu.roll(far_response, 2, 0)),
        by_level(far_response[2:3], far_response[3:4]),
        by_level(far_response[6:7], far_response[7:8]),
    )


def side_by_side(own_ref, other_ref, start, stop):
    own, other = own_ref[start:stop, :], other_ref[start:stop, :]
    core = lax.axis_index("gx") & 1
    return jnp.where(core == 0, own, other), jnp.where(core == 0, other, own)


def middle_face(own_ref, other_ref):
    responses = side_by_side(own_ref, other_ref, 16, 24)
    far = side_by_side(own_ref, other_ref, 24, 32)
    left = two_port(responses[0], far[0])
    right = two_port(responses[1], far[1])
    face = rates8() * left[3] * right[4]
    return left, right, face / (1.0 + face * (left[2] + right[0])), far


def chip_values(left, right, link, first, last):
    flux = link * (last[0] - first[1])
    return first[0] - left[1] * flux, last[1] + right[1] * flux


def own_fluxes(left, right, link, first, last, outer):
    flux = link * (last[0] - first[1] + left[1] * outer[0] - right[1] * outer[1])
    core = lax.axis_index("gx") & 1
    return jnp.where(core == 0, outer[0], flux), jnp.where(core == 0, -flux, outer[1])


def gather_chips(chips_ref, own, before, after, far):
    me = lax.axis_index("gx") >> 1
    count = chips_ref.shape[0]
    chips_ref[me] = own
    chips_ref[(me + count - 1) & (count - 1)] = before
    chips_ref[(me + 1) & (count - 1)] = after
    chips_ref[(me + 2) & (count - 1)] = far


def reduced(chips_ref):
    count = chips_ref.shape[0]
    ports = [two_port(chips_ref[j, 16:24, :], chips_ref[j, 24:32, :]) for j in range(count)]
    face = [rates8() * ports[j][3] * ports[j + 1][4] for j in range(count - 1)]
    return [p[0] for p in ports], [p[1] for p in ports], [p[2] for p in ports], face


def merge_kernel(own_ref, other_ref, up_ref, down_ref, far_ref):
    left, right, link, far = middle_face(own_ref, other_ref)
    values = chip_values(
        left,
        right,
        link,
        side_by_side(own_ref, other_ref, 0, 8),
        side_by_side(own_ref, other_ref, 8, 16),
    )
    row = rows8()
    upper = (row & 2) == 0
    tiles = [
        values[0],
        values[1],
        jnp.where(upper, left[0] - link * left[1] * left[1], link * left[1] * right[1]),
        jnp.where(
            upper, right[2] - link * right[1] * right[1], jnp.where(row < 4, far[1], far[0])
        ),
        jnp.where(upper, link * left[1], link * right[1]),
    ]
    for n, tile in enumerate(tiles):
        for ref in (up_ref, down_ref, far_ref):
            ref[ROWS * n : ROWS * (n + 1), :] = tile
    up_ref[40:48, :] = other_ref[40:48, :]
    down_ref[40:48, :] = other_ref[32:40, :]


def end_fluxes(system, first, last, me):
    first_self, across, last_self, face = system
    count = len(first_self)
    zero = jnp.zeros((ROWS, NY), F32)
    give, value = last_self[0], last[0]
    gives, values, links = [give], [value], [zero]
    for j in range(1, count):
        link = face[j - 1] / (1.0 + face[j - 1] * (give + first_self[j]))
        pull = across[j] * link
        value = last[j] + pull * (value - first[j])
        give = last_self[j] - pull * across[j]
        gives.append(give)
        values.append(value)
        links.append(link)
    back_give, back_value = first_self[count - 1], first[count - 1]
    right_flux = [None] * count
    right_flux[count - 1] = zero
    for j in range(count - 2, -1, -1):
        right_flux[j] = (
            face[j] * (back_value - values[j]) / (1.0 + face[j] * (back_give + gives[j]))
        )
        link = face[j] / (1.0 + face[j] * (back_give + last_self[j]))
        pull = across[j] * link
        back_value = first[j] + pull * (back_value - last[j])
        back_give = first_self[j] - pull * across[j]
    left, right = zero, right_flux[0]
    for j in range(1, count):
        here = links[j] * (values[j - 1] - first[j] - across[j] * right_flux[j])
        left = jnp.where(me == j, here, left)
        right = jnp.where(me == j, right_flux[j], right)
    return left, right


def own_lines(read, right_ref, recip_ref, fluxes, write):
    left, right = fluxes
    load = read(0) + left
    loads = [load]
    for i in range(1, NX):
        load = read(i) + right_ref[i - 1] * load
        loads.append(load)
    value = (loads[NX - 1] + right) * recip_ref[NX - 1]
    write(NX - 1, value)
    for i in range(NX - 2, -1, -1):
        value = right_ref[i] * value + recip_ref[i] * loads[i]
        write(i, value)


def network_kernel(weights_ref, out_ref, forward_ref, back_ref, outw_ref, outr_ref):
    weights = weights_ref[...]
    per_level = []
    for level in range(2):
        spread = iota((16, FEAT + 1), 0) == 2 * iota((16, FEAT + 1), 1) + level
        per_level.append(
            jnp.dot(
                spread.astype(F32),
                weights,
                precision=lax.Precision.HIGHEST,
                preferred_element_type=F32,
            )
        )
    both = jnp.concatenate(per_level, 1)
    high = both.astype(BF16).astype(F32)
    low = both - high
    bias = weights[FEAT : FEAT + 1, :]
    bias = jnp.broadcast_to(jnp.concatenate([bias, bias], 1), (16, 2 * HID))
    bias_high = bias.astype(BF16).astype(F32)
    bias_mid = (bias - bias_high).astype(BF16).astype(F32)
    bias_low = bias - bias_high - bias_mid
    row = iota((16, 2 * HID), 0)
    bias = jnp.where(
        row == 0, bias_high, jnp.where(row == 1, bias_mid, jnp.where(row == 2, bias_low, 0.0))
    )
    stack = jnp.concatenate([high, high, bias, low, low, jnp.zeros((48, 2 * HID), F32)], 0)
    forward_ref[...] = jnp.transpose(stack).astype(BF16)
    out = out_ref[...]
    out = jnp.broadcast_to(jnp.concatenate([out, out], 1), (2 * HID, 2 * HID))
    outw_ref[...] = jnp.transpose(out)
    outr_ref[...] = out[0:48]
    scaled = both * out[0:16]
    turned = jnp.concatenate(split(scaled), 0)
    back_ref[...] = jnp.concatenate([turned, turned], 1)


def pack(features, bias, out):
    blank = jnp.zeros((ROWS, HID), F32)
    row = iota((ROWS, 32), 0)
    ends = [
        jnp.broadcast_to(v, (ROWS, 32))
        for v in (bias[:, 0:32], bias[:, 32:64], out[:, 0:32], out[:, 32:64])
    ]
    tail = jnp.zeros((ROWS, 32), F32)
    for n, end in enumerate(ends):
        tail = jnp.where(row == n, end, tail)
    return jnp.concatenate([features, blank[:, :32], tail], 1)


def adjoint_kernel(
    own_ref,
    other_ref,
    chip_ref,
    before_ref,
    after_ref,
    far_ref,
    cot_ref,
    wets_ref,
    right_ref,
    recip_ref,
    lines_ref,
    adj_ref,
    slope_x,
    curve_x,
    chips_ref,
):
    me = lax.axis_index("gx")
    count = lax.axis_size("gx")
    core = me & 1
    zero = jnp.zeros((ROWS, NY), F32)
    below = jnp.where(core == 0, before_ref[40:48, :], other_ref[40:48, :])
    above = jnp.where(core == 0, other_ref[32:40, :], after_ref[40:48, :])
    below = jnp.where(me > 0, below, zero)
    above = jnp.where(me < count - 1, above, zero)
    for x in range(NX):
        east = lines_ref[x + 1] if x < NX - 1 else above
        west = lines_ref[x - 1] if x else below
        slope_x[x] = 0.5 * (east - west)
        curve_x[x] = east - 2.0 * lines_ref[x] + west
    gather_chips(
        chips_ref, chip_ref[...], before_ref[0:40, :], after_ref[0:40, :], far_ref[...]
    )
    count = chips_ref.shape[0]
    first = [chips_ref[j, 0:8, :] for j in range(count)]
    last = [chips_ref[j, 8:16, :] for j in range(count)]
    outer = end_fluxes(reduced(chips_ref), first, last, me >> 1)
    left, right, link, _ = middle_face(own_ref, other_ref)
    fluxes = own_fluxes(
        left,
        right,
        link,
        side_by_side(own_ref, other_ref, 0, 8),
        side_by_side(own_ref, other_ref, 8, 16),
        outer,
    )

    def keep(x, value):
        adj_ref[x] = wets_ref[x] * value

    own_lines(lambda x: line(cot_ref, x), right_ref, recip_ref, fluxes, keep)


def stencil_kernel(low_ref, high_ref, lines_ref, slope_x, slope_y, curve_y, feats):
    here_y = lax.axis_index("gy")
    lanes = lanes8()
    zero = jnp.zeros((ROWS, NY), F32)
    low = jnp.where(here_y > 0, low_ref[...], zero)
    high = jnp.where(here_y < lax.axis_size("gy") - 1, high_ref[...], zero)
    feats[32:48, :] = jnp.ones((16, NX * NY), BF16)
    for x in range(NX):
        center = lines_ref[x]
        south = jnp.where(
            lanes == 0, pltpu.roll(low, (-x) % NY, 1) if x else low, pltpu.roll(center, 1, 1)
        )
        north = jnp.where(
            lanes == NY - 1, pltpu.roll(high, NY - 1 - x, 1), pltpu.roll(center, NY - 1, 1)
        )
        sy = 0.5 * (north - south)
        slope_y[x] = sy
        curve_y[x] = north - 2.0 * center + south
        part_high, part_low = split(jnp.concatenate([slope_x[x], sy], 0))
        place = slice(x * NY, (x + 1) * NY)
        feats[0:16, place] = part_high
        feats[16:32, place] = part_low
        feats[48:64, place] = part_high
        feats[64:80, place] = part_low


def closure_kernel(
    own_ref,
    lines_ref,
    wets,
    adj,
    slope_x,
    slope_y,
    curve_x,
    curve_y,
    feats,
    forward_ref,
    back_ref,
    outw_ref,
    outr_ref,
    right_ref,
    recip_ref,
    left_ref,
    send_ref,
    rhs_ref,
    grad_ref,
    rims_ref,
    pairs_ref,
):
    here_y = lax.axis_index("gy")
    total_y = NY * lax.axis_size("gy")
    lanes = lanes8()
    row = rows8()
    places = (here_y * NY + lanes).astype(F32)
    turn = 0.3 * (0.5 + 0.5 * places / total_y)
    moment = row < 4
    outw = outw_ref[...]
    sharp, keepers, to_feats = [], [], []
    sums = jnp.zeros((48, 256), F32)
    out_sums = jnp.zeros((2 * HID, NY), F32)
    load = load_back = jnp.zeros((ROWS, NY), F32)
    for x in range(NX):
        if x % XS == 0:
            place = slice(x * NY, (x + XS) * NY)
            hidden = jnp.tanh(
                jnp.dot(forward_ref[:, 0:80], feats[:, place], preferred_element_type=F32)
            )
        unit = hidden[:, (x % XS) * NY : (x % XS + 1) * NY]
        weighed = unit * outw
        mixed = by_level(
            jnp.sum(weighed[:HID], 0, keepdims=True), jnp.sum(weighed[HID:], 0, keepdims=True)
        )
        gate = 1.0 / (1.0 + jnp.exp(-mixed))
        nu = jnp.where(moment, 0.24 * gate, 0.0)
        center = lines_ref[x]
        sx, sy, cx, cy = slope_x[x], slope_y[x], curve_x[x], curve_y[x]
        u = by_level(center[0:1], center[1:2])
        v = by_level(center[2:3], center[3:4])
        speed_u = jnp.sqrt(u * u + 0.01)
        speed_v = jnp.sqrt(v * v + 0.01)
        upwind = u * sx + v * sy - 0.5 * (speed_u * cx + speed_v * cy)
        twist = jnp.where(
            row < 2, pltpu.roll(center, 6, 0), jnp.where(moment, -pltpu.roll(center, 2, 0), 0.0)
        )
        explicit = wets[x] * (center - 0.3 * upwind + nu * (cx + cy) + turn * twist)
        rhs_ref[x] = explicit
        load = explicit + right_ref[x - 1] * load if x else explicit
        load_back = load_back + left_ref[x] * explicit if x else explicit
        g = adj[x]
        to_gate = jnp.where(moment, g * (cx + cy) * (0.24 * gate * (1.0 - gate)), 0.0)
        to_gate = to_gate + pltpu.roll(to_gate, 6, 0)
        gate_level = jnp.concatenate(
            [jnp.broadcast_to(to_gate[0:1], (HID, NY)), jnp.broadcast_to(to_gate[1:2], (HID, NY))],
            0,
        )
        pulled = unit * gate_level
        out_sums = out_sums + pulled
        sharp.append(gate_level - unit * pulled)
        along_u = g * (-0.3 * sx + 0.15 * (u / speed_u) * cx)
        along_v = g * (-0.3 * sy + 0.15 * (v / speed_v) * cy)
        along_u = along_u + pltpu.roll(along_u, 4, 0)
        along_u = along_u + pltpu.roll(along_u, 2, 0)
        along_v = along_v + pltpu.roll(along_v, 4, 0)
        along_v = along_v + pltpu.roll(along_v, 2, 0)
        untwist = jnp.where(
            row < 2, along_u - turn * pltpu.roll(g, 6, 0), along_v + turn * pltpu.roll(g, 2, 0)
        )
        bend_x = g * (0.15 * speed_u + nu)
        bend_y = g * (0.15 * speed_v + nu)
        middle = g + jnp.where(moment, untwist, 0.0) - 2.0 * (bend_x + bend_y)
        keepers.append((-0.3 * u * g, -0.3 * v * g, bend_x, bend_y, middle))
        if x % XS == XS - 1:
            stacked = jnp.concatenate(split(jnp.concatenate(sharp, 1)), 0)
            sharp = []
            back = jnp.dot(back_ref[...], stacked, preferred_element_type=F32)
            to_feats.append(back[0:16] + back[16:32])
            sums = sums + lax.dot_general(
                feats[0:48, place], stacked, (((1,), (1,)), ((), ())), preferred_element_type=F32
            )

    first_own = load_back * jnp.where(
        (row & 2) == 0, own_ref[16:24, :], pltpu.roll(own_ref[16:24, :], 2, 0)
    )
    last_own = load * recip_ref[NX - 1]

    rim_north = jnp.zeros((ROWS, NY), F32)
    rim_south = jnp.zeros((ROWS, NY), F32)
    to_east, to_west, kept = [], [], []
    for x in range(NX):
        to_sx, to_sy, bend_x, bend_y, middle = keepers[x]
        mine = to_feats[x // XS][:, (x % XS) * NY : (x % XS + 1) * NY]
        half_x = 0.5 * (to_sx + mine[0:8])
        half_y = 0.5 * (to_sy + mine[8:16])
        to_north = bend_y + half_y
        to_south = bend_y - half_y
        rim_north = jnp.where(lanes == RIM + x, pltpu.roll(to_north, RIM + x + 1, 1), rim_north)
        rim_south = jnp.where(lanes == RIM + x, pltpu.roll(to_south, RIM + x, 1), rim_south)
        to_east.append(bend_x + half_x)
        to_west.append(bend_x - half_x)
        kept.append(
            middle
            + jnp.where(lanes == 0, 0.0, pltpu.roll(to_north, 1, 1))
            + jnp.where(lanes == NY - 1, 0.0, pltpu.roll(to_south, NY - 1, 1))
        )
    for x in range(NX):
        total = kept[x]
        if x:
            total = total + to_east[x - 1]
        if x < NX - 1:
            total = total + to_west[x + 1]
        grad_ref[x] = total
    rims_ref[0] = rim_north
    rims_ref[1] = rim_south
    to_last = to_east[NX - 1]
    to_first = to_west[0]

    sums = (sums[:, 0:128] + sums[:, 128:256]) * outr_ref[...]
    pairs_ref[...] = sums[0:16] + sums[16:32]
    features = pairs_ref[pl.ds(0, 8, stride=2), :] + pltpu.roll(
        pairs_ref[pl.ds(1, 8, stride=2), :], HID, 1
    )
    bias = sums[32:40] + pltpu.roll(sums[32:40], HID, 1)
    out_total = jnp.sum(jnp.transpose(out_sums[0:HID] + out_sums[HID:]), 0, keepdims=True)
    packed = pack(features[:, 0:HID], bias[0:1, 0:HID], out_total)
    me = lax.axis_index("gx")
    for j in range(send_ref.shape[0]):
        send_ref[j, 0:8, :] = first_own
        send_ref[j, 8:16, :] = last_own
        send_ref[j, 16:24, :] = packed
        send_ref[j, 24:32, :] = jnp.where(j > me, to_last, to_first)


def share_kernel(
    own_ref,
    other_ref,
    chips_ref,
    second_ref,
    rims_ref,
    rhs_ref,
    right_ref,
    recip_ref,
    send_ref,
    final_ref,
    sides_ref,
):
    me_y = lax.axis_index("gy")
    me = lax.axis_index("gx")
    blocks = second_ref.shape[0]
    lanes = lanes8()
    zero = jnp.zeros((ROWS, NY), F32)
    total = second_ref[0, 16:24, :]
    for j in range(1, blocks):
        total = total + second_ref[j, 16:24, :]
    rim = (lanes >= RIM) & (lanes < RIM + NX)
    upward = jnp.where(rim, rims_ref[0], total)
    downward = jnp.where(rim, rims_ref[1], total)
    for j in range(send_ref.shape[0]):
        send_ref[j] = jnp.where(j > me_y, upward, downward)
    below = second_ref[jnp.maximum(me - 1, 0), 24:32, :]
    above = second_ref[jnp.minimum(me + 1, blocks - 1), 24:32, :]
    sides_ref[0] = jnp.where(me > 0, below, zero)
    sides_ref[1] = jnp.where(me < blocks - 1, above, zero)
    upper = (rows8() & 2) == 0
    first, last = [], []
    for j in range(chips_ref.shape[0]):
        pulls = chips_ref[j, 32:40, :]
        gap = second_ref[2 * j, 8:16, :] - second_ref[2 * j + 1, 0:8, :]
        left_pull = jnp.where(upper, pulls, pltpu.roll(pulls, 2, 0))
        right_pull = jnp.where(upper, pltpu.roll(pulls, 6, 0), pulls)
        first.append(second_ref[2 * j, 0:8, :] - left_pull * gap)
        last.append(second_ref[2 * j + 1, 8:16, :] + right_pull * gap)
    outer = end_fluxes(reduced(chips_ref), first, last, me >> 1)
    left, right, link, _ = middle_face(own_ref, other_ref)
    pair = me & (blocks - 2)
    fluxes = own_fluxes(
        left,
        right,
        link,
        (second_ref[pair, 0:8, :], second_ref[pair + 1, 0:8, :]),
        (second_ref[pair, 8:16, :], second_ref[pair + 1, 8:16, :]),
        outer,
    )

    def keep(x, value):
        final_ref[pl.ds(x, ROWS, stride=NX), :] = value

    own_lines(lambda x: rhs_ref[x], right_ref, recip_ref, fluxes, keep)


def finish_kernel(
    factor,
    third_ref,
    sides_ref,
    grad_ref,
    final_ref,
    final_hbm,
    out_hbm,
    closure_hbm,
    closure_ref,
    out_ref,
    sems,
):
    copies = [pltpu.make_async_copy(final_ref, final_hbm, sems.at[0])]
    copies[0].start()
    me_y = lax.axis_index("gy")
    count_y = third_ref.shape[0]
    lanes = lanes8()
    zero = jnp.zeros((ROWS, NY), F32)
    parts = [third_ref[j] for j in range(count_y)]
    while len(parts) > 1:
        parts = [a + b for a, b in zip(parts[::2], parts[1::2])]
    total = parts[0] * factor
    closure_ref[0:8, :] = total[:, 0:HID]
    for n in range(2):
        closure_ref[8 + n : 9 + n, :] = jnp.concatenate(
            [total[2 * n : 2 * n + 1, 96:], total[2 * n + 1 : 2 * n + 2, 96:]], 1
        )
    copies.append(pltpu.make_async_copy(closure_ref, closure_hbm, sems.at[1]))
    copies[1].start()
    south = jnp.where(me_y > 0, third_ref[jnp.maximum(me_y - 1, 0)], zero)
    north = jnp.where(me_y < count_y - 1, third_ref[jnp.minimum(me_y + 1, count_y - 1)], zero)
    for x in range(NX):
        value = grad_ref[x]
        if x == 0:
            value = value + sides_ref[0]
        if x == NX - 1:
            value = value + sides_ref[1]
        value = value + jnp.where(lanes == 0, pltpu.roll(south, NY - RIM - x, 1), 0.0)
        value = value + jnp.where(lanes == NY - 1, pltpu.roll(north, NY - 1 - RIM - x, 1), 0.0)
        out_ref[pl.ds(x, ROWS, stride=NX), :] = value
    copies.append(pltpu.make_async_copy(out_ref, out_hbm, sems.at[2]))
    copies[2].start()
    for copy in copies:
        copy.wait()


def tile(*shape):
    return jax.ShapeDtypeStruct(shape, F32)


def along_x(up, down, far):
    count = lax.axis_size("gx")
    return tuple(
        lax.ppermute(values, "gx", [(i, (i + shift) % count) for i in range(count)])
        for values, shift in ((up, 2), (down, count - 2), (far, 4))
    )


def keep_in_hbm(values):
    return pltpu.with_memory_space_constraint(values, pltpu.HBM)


def params():
    return pltpu.CompilerParams(vmem_limit_bytes=40 * 1024 * 1024)


def per_device(state, diffusivity, sea_mask, depth_index, closure_in, closure_out, cotangent):
    count_x = lax.axis_size("gx")
    count_y = lax.axis_size("gy")
    lines = tile(NX, ROWS, NY)
    in_hbm = pl.BlockSpec(memory_space=pltpu.HBM)
    in_vmem = pl.BlockSpec(memory_space=pltpu.VMEM)
    ints = jax.ShapeDtypeStruct((NX, NY), jnp.int32)
    fields, first, last, diff, sea, depth, cot = pl.pallas_call(
        load_kernel,
        in_specs=[in_hbm] * 5,
        out_shape=(
            lines,
            tile(ROWS, NY),
            tile(ROWS, NY),
            tile(2 * NX, NY),
            ints,
            ints,
            tile(ROWS * NX, NY),
        ),
        scratch_shapes=[pltpu.VMEM((ROWS * NX, NY), F32), pltpu.SemaphoreType.DMA((5,))],
        compiler_params=params(),
    )(
        keep_in_hbm(state.reshape(ROWS * NX, NY)),
        keep_in_hbm(diffusivity.reshape(2 * NX, NY)),
        keep_in_hbm(sea_mask),
        keep_in_hbm(depth_index),
        keep_in_hbm(cotangent.reshape(ROWS * NX, NY)),
    )
    own, right, recip, left, wets = pl.pallas_call(
        factor_kernel,
        out_shape=(tile(48, NY),) + (lines,) * 4,
        compiler_params=params(),
    )(fields, diff, sea, depth, cot)
    other = lax.ppermute(own, "gx", [(i, i ^ 1) for i in range(count_x)])
    up, down, chip = pl.pallas_call(
        merge_kernel,
        out_shape=(tile(48, NY), tile(48, NY), tile(40, NY)),
        compiler_params=params(),
    )(own, other)
    before, after, far = along_x(up, down, chip)
    low = lax.ppermute(last, "gy", [(i, (i + 1) % count_y) for i in range(count_y)])
    high = lax.ppermute(first, "gy", [((i + 1) % count_y, i) for i in range(count_y)])
    forward, back, outw, outr = pl.pallas_call(
        network_kernel,
        out_shape=(
            jax.ShapeDtypeStruct((2 * HID, 128), BF16),
            jax.ShapeDtypeStruct((32, 256), BF16),
            tile(2 * HID, 128),
            tile(48, 128),
        ),
        compiler_params=params(),
    )(closure_in.T, closure_out.reshape(1, HID))
    chips_x = count_x // 2
    adj, slope_x, curve_x, chips = pl.pallas_call(
        adjoint_kernel,
        out_shape=(lines,) * 3 + (tile(chips_x, 40, NY),),
        compiler_params=params(),
    )(own, other, chip, before, after, far, cot, wets, right, recip, fields)
    feats_shape = jax.ShapeDtypeStruct((80, NX * NY), BF16)
    slope_y, curve_y, feats = pl.pallas_call(
        stencil_kernel, out_shape=(lines,) * 2 + (feats_shape,), compiler_params=params()
    )(low, high, fields, slope_x)
    send, rhs, grad, rims = pl.pallas_call(
        closure_kernel,
        out_shape=(tile(count_x, 32, NY), lines, lines, tile(2, ROWS, NY)),
        scratch_shapes=[pltpu.VMEM((16, 128), F32)],
        compiler_params=params(),
    )(own, fields, wets, adj, slope_x, slope_y, curve_x, curve_y, feats, forward, back, outw, outr, right, recip, left)
    second = lax.all_to_all(send, "gx", 0, 0, tiled=True)
    send, final, sides = pl.pallas_call(
        share_kernel,
        out_shape=(tile(count_y, ROWS, NY), tile(ROWS * NX, NY), tile(2, ROWS, NY)),
        compiler_params=params(),
    )(own, other, chips, second, rims, rhs, right, recip)
    third = lax.all_to_all(send, "gy", 0, 0, tiled=True)
    factor = 1.0 / math.sqrt(2 * NX * count_x * NY * count_y)

    def finish(*refs):
        finish_kernel(factor, *refs)

    final, state_grad, closure_grad = pl.pallas_call(
        finish,
        in_specs=[in_vmem] * 4,
        out_shape=(tile(ROWS * NX, NY), tile(ROWS * NX, NY), tile(10, HID)),
        out_specs=(in_hbm,) * 3,
        scratch_shapes=[
            pltpu.VMEM((10, HID), F32),
            pltpu.VMEM((ROWS * NX, NY), F32),
            pltpu.SemaphoreType.DMA((3,)),
        ],
        compiler_params=params(),
    )(third, sides, grad, final)
    return (final.reshape(state.shape), state_grad.reshape(state.shape), closure_grad.T)


def solution(mesh):
    return jax.shard_map(
        per_device,
        mesh=mesh,
        in_specs=(
            P(None, None, "gx", "gy"),
            P(None, "gx", "gy"),
            P("gx", "gy"),
            P("gx", "gy"),
            P(),
            P(),
            P(None, None, "gx", "gy"),
        ),
        out_specs=(P(None, None, "gx", "gy"), P(None, None, "gx", "gy"), P()),
        check_vma=False,
    )
```

```python
import math

import jax
import jax.numpy as jnp
from jax import lax
from jax.experimental import pallas as pl
from jax.experimental.pallas import tpu as pltpu
from jax.sharding import PartitionSpec as P

F32 = jnp.float32
BF16 = jnp.bfloat16
DIFFUSE = 2048.0
FEAT = 8
HID = 64
NX = 32
NY = 128
XS = 4
ROWS = 8
RIM = 64


def iota(shape, dim):
    return lax.broadcasted_iota(jnp.int32, shape, dim)


def rows8():
    return iota((ROWS, NY), 0)


def lanes8():
    return iota((ROWS, NY), 1)


def wide(row):
    return jnp.broadcast_to(row, (ROWS, NY))


def by_level(first, second):
    return jnp.where((rows8() & 1) == 0, wide(first), wide(second))


def line(ref, x):
    return ref[pl.ds(x, ROWS, stride=NX), :]


def wet_line(sea_ref, depth_ref, x):
    sea = wide(sea_ref[x : x + 1, :])
    depth = wide(depth_ref[x : x + 1, :])
    return jnp.where(((rows8() & 1) < depth) & (sea > 0), 1.0, 0.0).astype(F32)


def rates8():
    return jnp.where(rows8() < 4, DIFFUSE, 0.5).astype(F32)


def split(values):
    high = values.astype(BF16)
    return high, (values - high.astype(F32)).astype(BF16)


def load_kernel(
    state_hbm,
    diff_hbm,
    sea_hbm,
    depth_hbm,
    cot_hbm,
    fields_ref,
    first_ref,
    last_ref,
    diff_ref,
    sea_ref,
    depth_ref,
    cot_ref,
    state_ref,
    sems,
):
    copies = [
        pltpu.make_async_copy(source, target, sems.at[n])
        for n, (source, target) in enumerate(
            (
                (state_hbm, state_ref),
                (sea_hbm, sea_ref),
                (depth_hbm, depth_ref),
                (diff_hbm, diff_ref),
                (cot_hbm, cot_ref),
            )
        )
    ]
    for copy in copies:
        copy.start()
    copies[0].wait()
    lanes = lanes8()
    first = jnp.zeros((ROWS, NY), F32)
    last = jnp.zeros((ROWS, NY), F32)
    for x in range(NX):
        here = line(state_ref, x)
        fields_ref[x] = here
        first = jnp.where(lanes == x, pltpu.roll(here, x, 1) if x else here, first)
        last = jnp.where(lanes == x, pltpu.roll(here, x + 1, 1), last)
    first_ref[...] = first
    last_ref[...] = last
    for copy in copies[1:]:
        copy.wait()


def factor_kernel(
    fields_ref,
    diff_ref,
    sea_ref,
    depth_ref,
    cot_ref,
    send_ref,
    right_ref,
    recip_ref,
    left_ref,
    wets_ref,
):
    row = rows8()
    wet = [wet_line(sea_ref, depth_ref, x) for x in range(NX)]
    for x in range(NX):
        wets_ref[x] = wet[x]
    rates = rates8()
    bare = [
        by_level(diff_ref[x : x + 1, :], diff_ref[NX + x : NX + x + 1, :]) * wet[x]
        for x in range(NX)
    ]
    cond = [rates * bare[x] * wet[x + 1] for x in range(NX - 1)]
    mass = jnp.ones((ROWS, NY), F32)
    carry = jnp.ones((ROWS, NY), F32)
    mass_back = jnp.ones((ROWS, NY), F32)
    cots = [line(cot_ref, x) for x in range(NX)]
    backs = []
    load = cots[0]
    load_back = cots[NX - 1]
    for i in range(NX - 1):
        recip = 1.0 / (mass + cond[i])
        ratio = cond[i] * recip
        right_ref[i] = ratio
        recip_ref[i] = recip
        mass = 1.0 + mass * ratio
        load = cots[i + 1] + ratio * load
        carry = carry * ratio
        j = NX - 2 - i
        ratio_back = cond[j] / (mass_back + cond[j])
        backs.append(ratio_back)
        mass_back = 1.0 + mass_back * ratio_back
        load_back = cots[j] + ratio_back * load_back
    last_self = 1.0 / mass
    first_self = 1.0 / mass_back
    right_ref[NX - 1] = jnp.zeros((ROWS, NY), F32)
    product = backs[NX - 2]
    for x in range(1, NX):
        left_ref[x] = product
        if x < NX - 1:
            product = product * backs[NX - 2 - x]
    recip_ref[NX - 1] = last_self
    across = carry * last_self
    upper = (row & 2) == 0
    tiles = [
        load_back * first_self,
        load * last_self,
        jnp.where(upper, first_self, across),
        jnp.where(upper, last_self, jnp.where(row < 4, bare[NX - 1], wet[0])),
    ]
    tiles += [fields_ref[0], fields_ref[NX - 1]]
    for n, tile in enumerate(tiles):
        send_ref[ROWS * n : ROWS * (n + 1), :] = tile


def two_port(responses, far_response):
    upper = (rows8() & 2) == 0
    return (
        jnp.where(upper, responses, pltpu.roll(responses, 2, 0)),
        jnp.where(upper, pltpu.roll(responses, 6, 0), responses),
        jnp.where(upper, far_response, pltpu.roll(far_response, 2, 0)),
        by_level(far_response[2:3], far_response[3:4]),
        by_level(far_response[6:7], far_response[7:8]),
    )


def side_by_side(own_ref, other_ref, start, stop):
    own, other = own_ref[start:stop, :], other_ref[start:stop, :]
    core = lax.axis_index("gx") & 1
    return jnp.where(core == 0, own, other), jnp.where(core == 0, other, own)


def middle_face(own_ref, other_ref):
    responses = side_by_side(own_ref, other_ref, 16, 24)
    far = side_by_side(own_ref, other_ref, 24, 32)
    left = two_port(responses[0], far[0])
    right = two_port(responses[1], far[1])
    face = rates8() * left[3] * right[4]
    return left, right, face / (1.0 + face * (left[2] + right[0])), far


def chip_values(left, right, link, first, last):
    flux = link * (last[0] - first[1])
    return first[0] - left[1] * flux, last[1] + right[1] * flux


def own_fluxes(left, right, link, first, last, outer):
    flux = link * (last[0] - first[1] + left[1] * outer[0] - right[1] * outer[1])
    core = lax.axis_index("gx") & 1
    return jnp.where(core == 0, outer[0], flux), jnp.where(core == 0, -flux, outer[1])


def gather_chips(chips_ref, own, before, after, far):
    me = lax.axis_index("gx") >> 1
    count = chips_ref.shape[0]
    chips_ref[me] = own
    chips_ref[(me + count - 1) & (count - 1)] = before
    chips_ref[(me + 1) & (count - 1)] = after
    chips_ref[(me + 2) & (count - 1)] = far


def reduced(chips_ref):
    count = chips_ref.shape[0]
    ports = [two_port(chips_ref[j, 16:24, :], chips_ref[j, 24:32, :]) for j in range(count)]
    face = [rates8() * ports[j][3] * ports[j + 1][4] for j in range(count - 1)]
    return [p[0] for p in ports], [p[1] for p in ports], [p[2] for p in ports], face


def merge_kernel(own_ref, other_ref, up_ref, down_ref, far_ref):
    left, right, link, far = middle_face(own_ref, other_ref)
    values = chip_values(
        left,
        right,
        link,
        side_by_side(own_ref, other_ref, 0, 8),
        side_by_side(own_ref, other_ref, 8, 16),
    )
    row = rows8()
    upper = (row & 2) == 0
    tiles = [
        values[0],
        values[1],
        jnp.where(upper, left[0] - link * left[1] * left[1], link * left[1] * right[1]),
        jnp.where(
            upper, right[2] - link * right[1] * right[1], jnp.where(row < 4, far[1], far[0])
        ),
        jnp.where(upper, link * left[1], link * right[1]),
    ]
    for n, tile in enumerate(tiles):
        for ref in (up_ref, down_ref, far_ref):
            ref[ROWS * n : ROWS * (n + 1), :] = tile
    up_ref[40:48, :] = other_ref[40:48, :]
    down_ref[40:48, :] = other_ref[32:40, :]


def end_fluxes(system, first, last, me):
    first_self, across, last_self, face = system
    count = len(first_self)
    zero = jnp.zeros((ROWS, NY), F32)
    give, value = last_self[0], last[0]
    gives, values, links = [give], [value], [zero]
    for j in range(1, count):
        link = face[j - 1] / (1.0 + face[j - 1] * (give + first_self[j]))
        pull = across[j] * link
        value = last[j] + pull * (value - first[j])
        give = last_self[j] - pull * across[j]
        gives.append(give)
        values.append(value)
        links.append(link)
    back_give, back_value = first_self[count - 1], first[count - 1]
    right_flux = [None] * count
    right_flux[count - 1] = zero
    for j in range(count - 2, -1, -1):
        right_flux[j] = (
            face[j] * (back_value - values[j]) / (1.0 + face[j] * (back_give + gives[j]))
        )
        link = face[j] / (1.0 + face[j] * (back_give + last_self[j]))
        pull = across[j] * link
        back_value = first[j] + pull * (back_value - last[j])
        back_give = first_self[j] - pull * across[j]
    left, right = zero, right_flux[0]
    for j in range(1, count):
        here = links[j] * (values[j - 1] - first[j] - across[j] * right_flux[j])
        left = jnp.where(me == j, here, left)
        right = jnp.where(me == j, right_flux[j], right)
    return left, right


def own_lines(read, right_ref, recip_ref, fluxes, write):
    left, right = fluxes
    load = read(0) + left
    loads = [load]
    for i in range(1, NX):
        load = read(i) + right_ref[i - 1] * load
        loads.append(load)
    value = (loads[NX - 1] + right) * recip_ref[NX - 1]
    write(NX - 1, value)
    for i in range(NX - 2, -1, -1):
        value = right_ref[i] * value + recip_ref[i] * loads[i]
        write(i, value)


def network_kernel(weights_ref, out_ref, forward_ref, back_ref, outw_ref, outr_ref):
    weights = weights_ref[...]
    per_level = []
    for level in range(2):
        spread = iota((16, FEAT + 1), 0) == 2 * iota((16, FEAT + 1), 1) + level
        per_level.append(
            jnp.dot(
                spread.astype(F32),
                weights,
                precision=lax.Precision.HIGHEST,
                preferred_element_type=F32,
            )
        )
    both = jnp.concatenate(per_level, 1)
    high = both.astype(BF16).astype(F32)
    low = both - high
    bias = weights[FEAT : FEAT + 1, :]
    bias = jnp.broadcast_to(jnp.concatenate([bias, bias], 1), (16, 2 * HID))
    bias_high = bias.astype(BF16).astype(F32)
    bias_mid = (bias - bias_high).astype(BF16).astype(F32)
    bias_low = bias - bias_high - bias_mid
    row = iota((16, 2 * HID), 0)
    bias = jnp.where(
        row == 0, bias_high, jnp.where(row == 1, bias_mid, jnp.where(row == 2, bias_low, 0.0))
    )
    stack = jnp.concatenate([high, high, bias, low, low, jnp.zeros((48, 2 * HID), F32)], 0)
    forward_ref[...] = jnp.transpose(stack).astype(BF16)
    out = out_ref[...]
    out = jnp.broadcast_to(jnp.concatenate([out, out], 1), (2 * HID, 2 * HID))
    outw_ref[...] = jnp.transpose(out)
    outr_ref[...] = out[0:48]
    scaled = both * out[0:16]
    turned = jnp.concatenate(split(scaled), 0)
    back_ref[...] = jnp.concatenate([turned, turned], 1)


def pack(features, bias, out):
    blank = jnp.zeros((ROWS, HID), F32)
    row = iota((ROWS, 32), 0)
    ends = [
        jnp.broadcast_to(v, (ROWS, 32))
        for v in (bias[:, 0:32], bias[:, 32:64], out[:, 0:32], out[:, 32:64])
    ]
    tail = jnp.zeros((ROWS, 32), F32)
    for n, end in enumerate(ends):
        tail = jnp.where(row == n, end, tail)
    return jnp.concatenate([features, blank[:, :32], tail], 1)


def adjoint_kernel(
    own_ref,
    other_ref,
    chip_ref,
    before_ref,
    after_ref,
    far_ref,
    cot_ref,
    wets_ref,
    right_ref,
    recip_ref,
    lines_ref,
    adj_ref,
    slope_x,
    curve_x,
    chips_ref,
):
    me = lax.axis_index("gx")
    count = lax.axis_size("gx")
    core = me & 1
    zero = jnp.zeros((ROWS, NY), F32)
    below = jnp.where(core == 0, before_ref[40:48, :], other_ref[40:48, :])
    above = jnp.where(core == 0, other_ref[32:40, :], after_ref[40:48, :])
    below = jnp.where(me > 0, below, zero)
    above = jnp.where(me < count - 1, above, zero)
    for x in range(NX):
        east = lines_ref[x + 1] if x < NX - 1 else above
        west = lines_ref[x - 1] if x else below
        slope_x[x] = 0.5 * (east - west)
        curve_x[x] = east - 2.0 * lines_ref[x] + west
    gather_chips(
        chips_ref, chip_ref[...], before_ref[0:40, :], after_ref[0:40, :], far_ref[...]
    )
    count = chips_ref.shape[0]
    first = [chips_ref[j, 0:8, :] for j in range(count)]
    last = [chips_ref[j, 8:16, :] for j in range(count)]
    outer = end_fluxes(reduced(chips_ref), first, last, me >> 1)
    left, right, link, _ = middle_face(own_ref, other_ref)
    fluxes = own_fluxes(
        left,
        right,
        link,
        side_by_side(own_ref, other_ref, 0, 8),
        side_by_side(own_ref, other_ref, 8, 16),
        outer,
    )

    def keep(x, value):
        adj_ref[x] = wets_ref[x] * value

    own_lines(lambda x: line(cot_ref, x), right_ref, recip_ref, fluxes, keep)


def stencil_kernel(low_ref, high_ref, lines_ref, slope_x, slope_y, curve_y, feats):
    here_y = lax.axis_index("gy")
    lanes = lanes8()
    zero = jnp.zeros((ROWS, NY), F32)
    low = jnp.where(here_y > 0, low_ref[...], zero)
    high = jnp.where(here_y < lax.axis_size("gy") - 1, high_ref[...], zero)
    feats[32:48, :] = jnp.ones((16, NX * NY), BF16)
    for x in range(NX):
        center = lines_ref[x]
        south = jnp.where(
            lanes == 0, pltpu.roll(low, (-x) % NY, 1) if x else low, pltpu.roll(center, 1, 1)
        )
        north = jnp.where(
            lanes == NY - 1, pltpu.roll(high, NY - 1 - x, 1), pltpu.roll(center, NY - 1, 1)
        )
        sy = 0.5 * (north - south)
        slope_y[x] = sy
        curve_y[x] = north - 2.0 * center + south
        part_high, part_low = split(jnp.concatenate([slope_x[x], sy], 0))
        place = slice(x * NY, (x + 1) * NY)
        feats[0:16, place] = part_high
        feats[16:32, place] = part_low
        feats[48:64, place] = part_high
        feats[64:80, place] = part_low


def closure_kernel(
    own_ref,
    lines_ref,
    wets,
    adj,
    slope_x,
    slope_y,
    curve_x,
    curve_y,
    feats,
    forward_ref,
    back_ref,
    outw_ref,
    outr_ref,
    right_ref,
    recip_ref,
    left_ref,
    send_ref,
    rhs_ref,
    grad_ref,
    rims_ref,
    pairs_ref,
):
    here_y = lax.axis_index("gy")
    total_y = NY * lax.axis_size("gy")
    lanes = lanes8()
    row = rows8()
    places = (here_y * NY + lanes).astype(F32)
    turn = 0.3 * (0.5 + 0.5 * places / total_y)
    moment = row < 4
    outw = outw_ref[...]
    sharp, keepers = [], []
    waiting, partial_sums = [], []
    rim_north = [jnp.zeros((ROWS, NY), F32)]
    rim_south = [jnp.zeros((ROWS, NY), F32)]
    to_east, to_west, kept = [], [], []

    def ahead(x):
        return jnp.dot(
            forward_ref[:, 0:80],
            feats[:, x * NY : (x + XS) * NY],
            preferred_element_type=F32,
        )

    def finish(x):
        stacked = waiting.pop()
        back = jnp.dot(back_ref[...], stacked, preferred_element_type=F32)
        back = back[0:16] + back[16:32]
        partial_sums.append(
            lax.dot_general(
                feats[0:48, x * NY : (x + XS) * NY],
                stacked,
                (((1,), (1,)), ((), ())),
                preferred_element_type=F32,
            )
        )

        for i in range(XS):
            lane = RIM + x + i
            to_sx, to_sy, bend_x, bend_y, middle = keepers[x + i]
            mine = back[:, i * NY : (i + 1) * NY]
            half_x = 0.5 * (to_sx + mine[0:8])
            half_y = 0.5 * (to_sy + mine[8:16])
            to_north = bend_y + half_y
            to_south = bend_y - half_y
            rim_north[0] = jnp.where(lanes == lane, pltpu.roll(to_north, lane + 1, 1), rim_north[0])
            rim_south[0] = jnp.where(lanes == lane, pltpu.roll(to_south, lane, 1), rim_south[0])
            to_east.append(bend_x + half_x)
            to_west.append(bend_x - half_x)
            kept.append(
                middle
                + jnp.where(lanes == 0, 0.0, pltpu.roll(to_north, 1, 1))
                + jnp.where(lanes == NY - 1, 0.0, pltpu.roll(to_south, NY - 1, 1))
            )
            done = x + i - 1
            if done >= 0:
                total = kept[done] + to_west[done + 1]
                grad_ref[done] = total + to_east[done - 1] if done else total

    before = ahead(0)
    out_sums = jnp.zeros((2 * HID, NY), F32)
    load = load_back = jnp.zeros((ROWS, NY), F32)
    for x in range(NX):
        if x % XS == 0:
            hidden = jnp.tanh(before)
            if x + XS < NX:
                before = ahead(x + XS)
            if x:
                finish(x - XS)
        unit = hidden[:, (x % XS) * NY : (x % XS + 1) * NY]
        weighed = unit * outw
        mixed = by_level(
            jnp.sum(weighed[:HID], 0, keepdims=True), jnp.sum(weighed[HID:], 0, keepdims=True)
        )
        gate = 1.0 / (1.0 + jnp.exp(-mixed))
        nu = jnp.where(moment, 0.24 * gate, 0.0)
        center = lines_ref[x]
        sx, sy, cx, cy = slope_x[x], slope_y[x], curve_x[x], curve_y[x]
        u = by_level(center[0:1], center[1:2])
        v = by_level(center[2:3], center[3:4])
        speed_u = jnp.sqrt(u * u + 0.01)
        speed_v = jnp.sqrt(v * v + 0.01)
        upwind = u * sx + v * sy - 0.5 * (speed_u * cx + speed_v * cy)
        twist = jnp.where(
            row < 2, pltpu.roll(center, 6, 0), jnp.where(moment, -pltpu.roll(center, 2, 0), 0.0)
        )
        explicit = wets[x] * (center - 0.3 * upwind + nu * (cx + cy) + turn * twist)
        rhs_ref[x] = explicit
        load = explicit + right_ref[x - 1] * load if x else explicit
        load_back = load_back + left_ref[x] * explicit if x else explicit
        g = adj[x]
        to_gate = jnp.where(moment, g * (cx + cy) * (0.24 * gate * (1.0 - gate)), 0.0)
        to_gate = to_gate + pltpu.roll(to_gate, 6, 0)
        gate_level = jnp.concatenate(
            [jnp.broadcast_to(to_gate[0:1], (HID, NY)), jnp.broadcast_to(to_gate[1:2], (HID, NY))],
            0,
        )
        pulled = unit * gate_level
        out_sums = out_sums + pulled
        sharp.append(gate_level - unit * pulled)
        along_u = g * (-0.3 * sx + 0.15 * (u / speed_u) * cx)
        along_v = g * (-0.3 * sy + 0.15 * (v / speed_v) * cy)
        along_u = along_u + pltpu.roll(along_u, 4, 0)
        along_u = along_u + pltpu.roll(along_u, 2, 0)
        along_v = along_v + pltpu.roll(along_v, 4, 0)
        along_v = along_v + pltpu.roll(along_v, 2, 0)
        untwist = jnp.where(
            row < 2, along_u - turn * pltpu.roll(g, 6, 0), along_v + turn * pltpu.roll(g, 2, 0)
        )
        bend_x = g * (0.15 * speed_u + nu)
        bend_y = g * (0.15 * speed_v + nu)
        middle = g + jnp.where(moment, untwist, 0.0) - 2.0 * (bend_x + bend_y)
        keepers.append((-0.3 * u * g, -0.3 * v * g, bend_x, bend_y, middle))
        if x % XS == XS - 1:
            waiting.append(jnp.concatenate(split(jnp.concatenate(sharp, 1)), 0))
            sharp = []
    finish(NX - XS)
    grad_ref[NX - 1] = kept[NX - 1] + to_east[NX - 2]
    sums = sum(partial_sums)

    first_own = load_back * jnp.where(
        (row & 2) == 0, own_ref[16:24, :], pltpu.roll(own_ref[16:24, :], 2, 0)
    )
    last_own = load * recip_ref[NX - 1]

    rims_ref[0] = rim_north[0]
    rims_ref[1] = rim_south[0]
    to_last = to_east[NX - 1]
    to_first = to_west[0]

    sums = (sums[:, 0:128] + sums[:, 128:256]) * outr_ref[...]
    pairs_ref[...] = sums[0:16] + sums[16:32]
    features = pairs_ref[pl.ds(0, 8, stride=2), :] + pltpu.roll(
        pairs_ref[pl.ds(1, 8, stride=2), :], HID, 1
    )
    bias = sums[32:40] + pltpu.roll(sums[32:40], HID, 1)
    out_total = jnp.sum(jnp.transpose(out_sums[0:HID] + out_sums[HID:]), 0, keepdims=True)
    packed = pack(features[:, 0:HID], bias[0:1, 0:HID], out_total)
    me = lax.axis_index("gx")
    for j in range(send_ref.shape[0]):
        send_ref[j, 0:8, :] = first_own
        send_ref[j, 8:16, :] = last_own
        send_ref[j, 16:24, :] = packed
        send_ref[j, 24:32, :] = jnp.where(j > me, to_last, to_first)


def share_kernel(
    own_ref,
    other_ref,
    chips_ref,
    second_ref,
    rims_ref,
    rhs_ref,
    right_ref,
    recip_ref,
    send_ref,
    final_ref,
    sides_ref,
):
    me_y = lax.axis_index("gy")
    me = lax.axis_index("gx")
    blocks = second_ref.shape[0]
    lanes = lanes8()
    zero = jnp.zeros((ROWS, NY), F32)
    total = second_ref[0, 16:24, :]
    for j in range(1, blocks):
        total = total + second_ref[j, 16:24, :]
    rim = (lanes >= RIM) & (lanes < RIM + NX)
    upward = jnp.where(rim, rims_ref[0], total)
    downward = jnp.where(rim, rims_ref[1], total)
    for j in range(send_ref.shape[0]):
        send_ref[j] = jnp.where(j > me_y, upward, downward)
    below = second_ref[jnp.maximum(me - 1, 0), 24:32, :]
    above = second_ref[jnp.minimum(me + 1, blocks - 1), 24:32, :]
    sides_ref[0] = jnp.where(me > 0, below, zero)
    sides_ref[1] = jnp.where(me < blocks - 1, above, zero)
    upper = (rows8() & 2) == 0
    first, last = [], []
    for j in range(chips_ref.shape[0]):
        pulls = chips_ref[j, 32:40, :]
        gap = second_ref[2 * j, 8:16, :] - second_ref[2 * j + 1, 0:8, :]
        left_pull = jnp.where(upper, pulls, pltpu.roll(pulls, 2, 0))
        right_pull = jnp.where(upper, pltpu.roll(pulls, 6, 0), pulls)
        first.append(second_ref[2 * j, 0:8, :] - left_pull * gap)
        last.append(second_ref[2 * j + 1, 8:16, :] + right_pull * gap)
    outer = end_fluxes(reduced(chips_ref), first, last, me >> 1)
    left, right, link, _ = middle_face(own_ref, other_ref)
    pair = me & (blocks - 2)
    fluxes = own_fluxes(
        left,
        right,
        link,
        (second_ref[pair, 0:8, :], second_ref[pair + 1, 0:8, :]),
        (second_ref[pair, 8:16, :], second_ref[pair + 1, 8:16, :]),
        outer,
    )

    def keep(x, value):
        final_ref[pl.ds(x, ROWS, stride=NX), :] = value

    own_lines(lambda x: rhs_ref[x], right_ref, recip_ref, fluxes, keep)


def finish_kernel(
    factor,
    third_ref,
    sides_ref,
    grad_ref,
    final_ref,
    final_hbm,
    out_hbm,
    closure_hbm,
    closure_ref,
    out_ref,
    sems,
):
    copies = [pltpu.make_async_copy(final_ref, final_hbm, sems.at[0])]
    copies[0].start()
    me_y = lax.axis_index("gy")
    count_y = third_ref.shape[0]
    lanes = lanes8()
    zero = jnp.zeros((ROWS, NY), F32)
    parts = [third_ref[j] for j in range(count_y)]
    while len(parts) > 1:
        parts = [a + b for a, b in zip(parts[::2], parts[1::2])]
    total = parts[0] * factor
    closure_ref[0:8, :] = total[:, 0:HID]
    for n in range(2):
        closure_ref[8 + n : 9 + n, :] = jnp.concatenate(
            [total[2 * n : 2 * n + 1, 96:], total[2 * n + 1 : 2 * n + 2, 96:]], 1
        )
    copies.append(pltpu.make_async_copy(closure_ref, closure_hbm, sems.at[1]))
    copies[1].start()
    south = jnp.where(me_y > 0, third_ref[jnp.maximum(me_y - 1, 0)], zero)
    north = jnp.where(me_y < count_y - 1, third_ref[jnp.minimum(me_y + 1, count_y - 1)], zero)
    for x in range(NX):
        value = grad_ref[x]
        if x == 0:
            value = value + sides_ref[0]
        if x == NX - 1:
            value = value + sides_ref[1]
        value = value + jnp.where(lanes == 0, pltpu.roll(south, NY - RIM - x, 1), 0.0)
        value = value + jnp.where(lanes == NY - 1, pltpu.roll(north, NY - 1 - RIM - x, 1), 0.0)
        out_ref[pl.ds(x, ROWS, stride=NX), :] = value
    copies.append(pltpu.make_async_copy(out_ref, out_hbm, sems.at[2]))
    copies[2].start()
    for copy in copies:
        copy.wait()


def tile(*shape):
    return jax.ShapeDtypeStruct(shape, F32)


def along_x(up, down, far):
    count = lax.axis_size("gx")
    return tuple(
        lax.ppermute(values, "gx", [(i, (i + shift) % count) for i in range(count)])
        for values, shift in ((up, 2), (down, count - 2), (far, 4))
    )


def keep_in_hbm(values):
    return pltpu.with_memory_space_constraint(values, pltpu.HBM)


def params():
    return pltpu.CompilerParams(vmem_limit_bytes=40 * 1024 * 1024)


def per_device(state, diffusivity, sea_mask, depth_index, closure_in, closure_out, cotangent):
    count_x = lax.axis_size("gx")
    count_y = lax.axis_size("gy")
    lines = tile(NX, ROWS, NY)
    in_hbm = pl.BlockSpec(memory_space=pltpu.HBM)
    in_vmem = pl.BlockSpec(memory_space=pltpu.VMEM)
    ints = jax.ShapeDtypeStruct((NX, NY), jnp.int32)
    fields, first, last, diff, sea, depth, cot = pl.pallas_call(
        load_kernel,
        in_specs=[in_hbm] * 5,
        out_shape=(
            lines,
            tile(ROWS, NY),
            tile(ROWS, NY),
            tile(2 * NX, NY),
            ints,
            ints,
            tile(ROWS * NX, NY),
        ),
        scratch_shapes=[pltpu.VMEM((ROWS * NX, NY), F32), pltpu.SemaphoreType.DMA((5,))],
        compiler_params=params(),
    )(
        keep_in_hbm(state.reshape(ROWS * NX, NY)),
        keep_in_hbm(diffusivity.reshape(2 * NX, NY)),
        keep_in_hbm(sea_mask),
        keep_in_hbm(depth_index),
        keep_in_hbm(cotangent.reshape(ROWS * NX, NY)),
    )
    own, right, recip, left, wets = pl.pallas_call(
        factor_kernel,
        out_shape=(tile(48, NY),) + (lines,) * 4,
        compiler_params=params(),
    )(fields, diff, sea, depth, cot)
    other = lax.ppermute(own, "gx", [(i, i ^ 1) for i in range(count_x)])
    up, down, chip = pl.pallas_call(
        merge_kernel,
        out_shape=(tile(48, NY), tile(48, NY), tile(40, NY)),
        compiler_params=params(),
    )(own, other)
    before, after, far = along_x(up, down, chip)
    low = lax.ppermute(last, "gy", [(i, (i + 1) % count_y) for i in range(count_y)])
    high = lax.ppermute(first, "gy", [((i + 1) % count_y, i) for i in range(count_y)])
    forward, back, outw, outr = pl.pallas_call(
        network_kernel,
        out_shape=(
            jax.ShapeDtypeStruct((2 * HID, 128), BF16),
            jax.ShapeDtypeStruct((32, 256), BF16),
            tile(2 * HID, 128),
            tile(48, 128),
        ),
        compiler_params=params(),
    )(closure_in.T, closure_out.reshape(1, HID))
    chips_x = count_x // 2
    adj, slope_x, curve_x, chips = pl.pallas_call(
        adjoint_kernel,
        out_shape=(lines,) * 3 + (tile(chips_x, 40, NY),),
        compiler_params=params(),
    )(own, other, chip, before, after, far, cot, wets, right, recip, fields)
    feats_shape = jax.ShapeDtypeStruct((80, NX * NY), BF16)
    slope_y, curve_y, feats = pl.pallas_call(
        stencil_kernel, out_shape=(lines,) * 2 + (feats_shape,), compiler_params=params()
    )(low, high, fields, slope_x)
    send, rhs, grad, rims = pl.pallas_call(
        closure_kernel,
        out_shape=(tile(count_x, 32, NY), lines, lines, tile(2, ROWS, NY)),
        scratch_shapes=[pltpu.VMEM((16, 128), F32)],
        compiler_params=params(),
    )(own, fields, wets, adj, slope_x, slope_y, curve_x, curve_y, feats, forward, back, outw, outr, right, recip, left)
    second = lax.all_to_all(send, "gx", 0, 0, tiled=True)
    send, final, sides = pl.pallas_call(
        share_kernel,
        out_shape=(tile(count_y, ROWS, NY), tile(ROWS * NX, NY), tile(2, ROWS, NY)),
        compiler_params=params(),
    )(own, other, chips, second, rims, rhs, right, recip)
    third = lax.all_to_all(send, "gy", 0, 0, tiled=True)
    factor = 1.0 / math.sqrt(2 * NX * count_x * NY * count_y)

    def finish(*refs):
        finish_kernel(factor, *refs)

    final, state_grad, closure_grad = pl.pallas_call(
        finish,
        in_specs=[in_vmem] * 4,
        out_shape=(tile(ROWS * NX, NY), tile(ROWS * NX, NY), tile(10, HID)),
        out_specs=(in_hbm,) * 3,
        scratch_shapes=[
            pltpu.VMEM((10, HID), F32),
            pltpu.VMEM((ROWS * NX, NY), F32),
            pltpu.SemaphoreType.DMA((3,)),
        ],
        compiler_params=params(),
    )(third, sides, grad, final)
    return (final.reshape(state.shape), state_grad.reshape(state.shape), closure_grad.T)


def solution(mesh):
    return jax.shard_map(
        per_device,
        mesh=mesh,
        in_specs=(
            P(None, None, "gx", "gy"),
            P(None, "gx", "gy"),
            P("gx", "gy"),
            P("gx", "gy"),
            P(),
            P(),
            P(None, None, "gx", "gy"),
        ),
        out_specs=(P(None, None, "gx", "gy"), P(None, None, "gx", "gy"), P()),
        check_vma=False,
    )
```

```python
import math

import jax
import jax.numpy as jnp
from jax import lax
from jax.experimental import pallas as pl
from jax.experimental.pallas import tpu as pltpu
from jax.sharding import PartitionSpec as P

F32 = jnp.float32
BF16 = jnp.bfloat16
DIFFUSE = 2048.0
FEAT = 8
HID = 64
NX = 32
NY = 128
XS = 4
ROWS = 8
RIM = 64


def iota(shape, dim):
    return lax.broadcasted_iota(jnp.int32, shape, dim)


def rows8():
    return iota((ROWS, NY), 0)


def lanes8():
    return iota((ROWS, NY), 1)


def wide(row):
    return jnp.broadcast_to(row, (ROWS, NY))


def by_level(first, second):
    return jnp.where((rows8() & 1) == 0, wide(first), wide(second))


def line(ref, x):
    return ref[pl.ds(x, ROWS, stride=NX), :]


def wet_line(sea_ref, depth_ref, x):
    sea = wide(sea_ref[x : x + 1, :])
    depth = wide(depth_ref[x : x + 1, :])
    return jnp.where(((rows8() & 1) < depth) & (sea > 0), 1.0, 0.0).astype(F32)


def rates8():
    return jnp.where(rows8() < 4, DIFFUSE, 0.5).astype(F32)


def split(values):
    high = values.astype(BF16)
    return high, (values - high.astype(F32)).astype(BF16)


def load_kernel(
    state_hbm,
    diff_hbm,
    sea_hbm,
    depth_hbm,
    cot_hbm,
    fields_ref,
    first_ref,
    last_ref,
    diff_ref,
    sea_ref,
    depth_ref,
    cot_ref,
    state_ref,
    sems,
):
    copies = [
        pltpu.make_async_copy(source, target, sems.at[n])
        for n, (source, target) in enumerate(
            (
                (state_hbm, state_ref),
                (sea_hbm, sea_ref),
                (depth_hbm, depth_ref),
                (diff_hbm, diff_ref),
                (cot_hbm, cot_ref),
            )
        )
    ]
    for copy in copies:
        copy.start()
    copies[0].wait()
    lanes = lanes8()
    first = jnp.zeros((ROWS, NY), F32)
    last = jnp.zeros((ROWS, NY), F32)
    for x in range(NX):
        here = line(state_ref, x)
        fields_ref[x] = here
        first = jnp.where(lanes == x, pltpu.roll(here, x, 1) if x else here, first)
        last = jnp.where(lanes == x, pltpu.roll(here, x + 1, 1), last)
    first_ref[...] = first
    last_ref[...] = last
    for copy in copies[1:]:
        copy.wait()


def factor_kernel(
    fields_ref,
    diff_ref,
    sea_ref,
    depth_ref,
    cot_ref,
    send_ref,
    right_ref,
    recip_ref,
    left_ref,
    wets_ref,
):
    row = rows8()
    wet = [wet_line(sea_ref, depth_ref, x) for x in range(NX)]
    for x in range(NX):
        wets_ref[x] = wet[x]
    rates = rates8()
    bare = [
        by_level(diff_ref[x : x + 1, :], diff_ref[NX + x : NX + x + 1, :]) * wet[x]
        for x in range(NX)
    ]
    cond = [rates * bare[x] * wet[x + 1] for x in range(NX - 1)]
    mass = jnp.ones((ROWS, NY), F32)
    carry = jnp.ones((ROWS, NY), F32)
    mass_back = jnp.ones((ROWS, NY), F32)
    cots = [line(cot_ref, x) for x in range(NX)]
    backs = []
    load = cots[0]
    load_back = cots[NX - 1]
    for i in range(NX - 1):
        recip = 1.0 / (mass + cond[i])
        ratio = cond[i] * recip
        right_ref[i] = ratio
        recip_ref[i] = recip
        mass = 1.0 + mass * ratio
        load = cots[i + 1] + ratio * load
        carry = carry * ratio
        j = NX - 2 - i
        ratio_back = cond[j] / (mass_back + cond[j])
        backs.append(ratio_back)
        mass_back = 1.0 + mass_back * ratio_back
        load_back = cots[j] + ratio_back * load_back
    last_self = 1.0 / mass
    first_self = 1.0 / mass_back
    right_ref[NX - 1] = jnp.zeros((ROWS, NY), F32)
    product = backs[NX - 2]
    for x in range(1, NX):
        left_ref[x] = product
        if x < NX - 1:
            product = product * backs[NX - 2 - x]
    recip_ref[NX - 1] = last_self
    across = carry * last_self
    upper = (row & 2) == 0
    tiles = [
        load_back * first_self,
        load * last_self,
        jnp.where(upper, first_self, across),
        jnp.where(upper, last_self, jnp.where(row < 4, bare[NX - 1], wet[0])),
    ]
    tiles += [fields_ref[0], fields_ref[NX - 1]]
    for n, tile in enumerate(tiles):
        send_ref[ROWS * n : ROWS * (n + 1), :] = tile


def two_port(responses, far_response):
    upper = (rows8() & 2) == 0
    return (
        jnp.where(upper, responses, pltpu.roll(responses, 2, 0)),
        jnp.where(upper, pltpu.roll(responses, 6, 0), responses),
        jnp.where(upper, far_response, pltpu.roll(far_response, 2, 0)),
        by_level(far_response[2:3], far_response[3:4]),
        by_level(far_response[6:7], far_response[7:8]),
    )


def side_by_side(own_ref, other_ref, start, stop):
    own, other = own_ref[start:stop, :], other_ref[start:stop, :]
    core = lax.axis_index("gx") & 1
    return jnp.where(core == 0, own, other), jnp.where(core == 0, other, own)


def middle_face(own_ref, other_ref):
    responses = side_by_side(own_ref, other_ref, 16, 24)
    far = side_by_side(own_ref, other_ref, 24, 32)
    left = two_port(responses[0], far[0])
    right = two_port(responses[1], far[1])
    face = rates8() * left[3] * right[4]
    return left, right, face / (1.0 + face * (left[2] + right[0])), far


def chip_values(left, right, link, first, last):
    flux = link * (last[0] - first[1])
    return first[0] - left[1] * flux, last[1] + right[1] * flux


def own_fluxes(left, right, link, first, last, outer):
    flux = link * (last[0] - first[1] + left[1] * outer[0] - right[1] * outer[1])
    core = lax.axis_index("gx") & 1
    return jnp.where(core == 0, outer[0], flux), jnp.where(core == 0, -flux, outer[1])


def gather_chips(chips_ref, own, before, after, far):
    me = lax.axis_index("gx") >> 1
    count = chips_ref.shape[0]
    chips_ref[me] = own
    chips_ref[(me + count - 1) & (count - 1)] = before
    chips_ref[(me + 1) & (count - 1)] = after
    chips_ref[(me + 2) & (count - 1)] = far


def reduced(chips_ref):
    count = chips_ref.shape[0]
    ports = [two_port(chips_ref[j, 16:24, :], chips_ref[j, 24:32, :]) for j in range(count)]
    face = [rates8() * ports[j][3] * ports[j + 1][4] for j in range(count - 1)]
    return [p[0] for p in ports], [p[1] for p in ports], [p[2] for p in ports], face


def merge_kernel(own_ref, other_ref, up_ref, down_ref, far_ref):
    left, right, link, far = middle_face(own_ref, other_ref)
    values = chip_values(
        left,
        right,
        link,
        side_by_side(own_ref, other_ref, 0, 8),
        side_by_side(own_ref, other_ref, 8, 16),
    )
    row = rows8()
    upper = (row & 2) == 0
    tiles = [
        values[0],
        values[1],
        jnp.where(upper, left[0] - link * left[1] * left[1], link * left[1] * right[1]),
        jnp.where(
            upper, right[2] - link * right[1] * right[1], jnp.where(row < 4, far[1], far[0])
        ),
        jnp.where(upper, link * left[1], link * right[1]),
    ]
    for n, tile in enumerate(tiles):
        for ref in (up_ref, down_ref, far_ref):
            ref[ROWS * n : ROWS * (n + 1), :] = tile
    up_ref[40:48, :] = other_ref[40:48, :]
    down_ref[40:48, :] = other_ref[32:40, :]


def end_fluxes(system, first, last, me):
    first_self, across, last_self, face = system
    count = len(first_self)
    zero = jnp.zeros((ROWS, NY), F32)
    give, value = last_self[0], last[0]
    gives, values, links = [give], [value], [zero]
    for j in range(1, count):
        link = face[j - 1] / (1.0 + face[j - 1] * (give + first_self[j]))
        pull = across[j] * link
        value = last[j] + pull * (value - first[j])
        give = last_self[j] - pull * across[j]
        gives.append(give)
        values.append(value)
        links.append(link)
    back_give, back_value = first_self[count - 1], first[count - 1]
    right_flux = [None] * count
    right_flux[count - 1] = zero
    for j in range(count - 2, -1, -1):
        right_flux[j] = (
            face[j] * (back_value - values[j]) / (1.0 + face[j] * (back_give + gives[j]))
        )
        link = face[j] / (1.0 + face[j] * (back_give + last_self[j]))
        pull = across[j] * link
        back_value = first[j] + pull * (back_value - last[j])
        back_give = first_self[j] - pull * across[j]
    left, right = zero, right_flux[0]
    for j in range(1, count):
        here = links[j] * (values[j - 1] - first[j] - across[j] * right_flux[j])
        left = jnp.where(me == j, here, left)
        right = jnp.where(me == j, right_flux[j], right)
    return left, right


def own_lines(read, right_ref, recip_ref, fluxes, write):
    left, right = fluxes
    load = read(0) + left
    loads = [load]
    for i in range(1, NX):
        load = read(i) + right_ref[i - 1] * load
        loads.append(load)
    value = (loads[NX - 1] + right) * recip_ref[NX - 1]
    write(NX - 1, value)
    for i in range(NX - 2, -1, -1):
        value = right_ref[i] * value + recip_ref[i] * loads[i]
        write(i, value)


def network_kernel(weights_ref, out_ref, forward_ref, back_ref, outw_ref, outr_ref):
    weights = weights_ref[...]
    per_level = []
    for level in range(2):
        spread = iota((16, FEAT + 1), 0) == 2 * iota((16, FEAT + 1), 1) + level
        per_level.append(
            jnp.dot(
                spread.astype(F32),
                weights,
                precision=lax.Precision.HIGHEST,
                preferred_element_type=F32,
            )
        )
    both = jnp.concatenate(per_level, 1)
    high = both.astype(BF16).astype(F32)
    low = both - high
    bias = weights[FEAT : FEAT + 1, :]
    bias = jnp.broadcast_to(jnp.concatenate([bias, bias], 1), (16, 2 * HID))
    bias_high = bias.astype(BF16).astype(F32)
    bias_mid = (bias - bias_high).astype(BF16).astype(F32)
    bias_low = bias - bias_high - bias_mid
    row = iota((16, 2 * HID), 0)
    bias = jnp.where(
        row == 0, bias_high, jnp.where(row == 1, bias_mid, jnp.where(row == 2, bias_low, 0.0))
    )
    stack = jnp.concatenate([high, high, bias, low, low, jnp.zeros((48, 2 * HID), F32)], 0)
    forward_ref[...] = jnp.transpose(stack).astype(BF16)
    out = out_ref[...]
    out = jnp.broadcast_to(jnp.concatenate([out, out], 1), (2 * HID, 2 * HID))
    outw_ref[...] = jnp.transpose(out)
    outr_ref[...] = out[0:48]
    scaled = both * out[0:16]
    turned = jnp.concatenate(split(scaled), 0)
    back_ref[...] = jnp.concatenate([turned, turned], 1)


def pack(features, bias, out):
    blank = jnp.zeros((ROWS, HID), F32)
    row = iota((ROWS, 32), 0)
    ends = [
        jnp.broadcast_to(v, (ROWS, 32))
        for v in (bias[:, 0:32], bias[:, 32:64], out[:, 0:32], out[:, 32:64])
    ]
    tail = jnp.zeros((ROWS, 32), F32)
    for n, end in enumerate(ends):
        tail = jnp.where(row == n, end, tail)
    return jnp.concatenate([features, blank[:, :32], tail], 1)


def adjoint_kernel(
    own_ref,
    other_ref,
    chip_ref,
    before_ref,
    after_ref,
    far_ref,
    cot_ref,
    wets_ref,
    right_ref,
    recip_ref,
    lines_ref,
    adj_ref,
    slope_x,
    curve_x,
    chips_ref,
):
    me = lax.axis_index("gx")
    count = lax.axis_size("gx")
    core = me & 1
    zero = jnp.zeros((ROWS, NY), F32)
    below = jnp.where(core == 0, before_ref[40:48, :], other_ref[40:48, :])
    above = jnp.where(core == 0, other_ref[32:40, :], after_ref[40:48, :])
    below = jnp.where(me > 0, below, zero)
    above = jnp.where(me < count - 1, above, zero)
    for x in range(NX):
        east = lines_ref[x + 1] if x < NX - 1 else above
        west = lines_ref[x - 1] if x else below
        slope_x[x] = 0.5 * (east - west)
        curve_x[x] = east - 2.0 * lines_ref[x] + west
    gather_chips(
        chips_ref, chip_ref[...], before_ref[0:40, :], after_ref[0:40, :], far_ref[...]
    )
    count = chips_ref.shape[0]
    first = [chips_ref[j, 0:8, :] for j in range(count)]
    last = [chips_ref[j, 8:16, :] for j in range(count)]
    outer = end_fluxes(reduced(chips_ref), first, last, me >> 1)
    left, right, link, _ = middle_face(own_ref, other_ref)
    fluxes = own_fluxes(
        left,
        right,
        link,
        side_by_side(own_ref, other_ref, 0, 8),
        side_by_side(own_ref, other_ref, 8, 16),
        outer,
    )

    def keep(x, value):
        adj_ref[x] = wets_ref[x] * value

    own_lines(lambda x: line(cot_ref, x), right_ref, recip_ref, fluxes, keep)


def stencil_kernel(low_ref, high_ref, lines_ref, slope_x, slope_y, curve_y, feats):
    here_y = lax.axis_index("gy")
    lanes = lanes8()
    zero = jnp.zeros((ROWS, NY), F32)
    low = jnp.where(here_y > 0, low_ref[...], zero)
    high = jnp.where(here_y < lax.axis_size("gy") - 1, high_ref[...], zero)
    feats[32:48, :] = jnp.ones((16, NX * NY), BF16)
    for x in range(NX):
        center = lines_ref[x]
        south = jnp.where(
            lanes == 0, pltpu.roll(low, (-x) % NY, 1) if x else low, pltpu.roll(center, 1, 1)
        )
        north = jnp.where(
            lanes == NY - 1, pltpu.roll(high, NY - 1 - x, 1), pltpu.roll(center, NY - 1, 1)
        )
        sy = 0.5 * (north - south)
        slope_y[x] = sy
        curve_y[x] = north - 2.0 * center + south
        part_high, part_low = split(jnp.concatenate([slope_x[x], sy], 0))
        place = slice(x * NY, (x + 1) * NY)
        feats[0:16, place] = part_high
        feats[16:32, place] = part_low
        feats[48:64, place] = part_high
        feats[64:80, place] = part_low


def closure_kernel(
    own_ref,
    lines_ref,
    wets,
    adj,
    slope_x,
    slope_y,
    curve_x,
    curve_y,
    feats,
    forward_ref,
    back_ref,
    outw_ref,
    outr_ref,
    right_ref,
    recip_ref,
    left_ref,
    send_ref,
    rhs_ref,
    grad_ref,
    rims_ref,
    pairs_ref,
):
    here_y = lax.axis_index("gy")
    total_y = NY * lax.axis_size("gy")
    lanes = lanes8()
    row = rows8()
    places = (here_y * NY + lanes).astype(F32)
    turn = 0.3 * (0.5 + 0.5 * places / total_y)
    moment = row < 4
    outw = outw_ref[...]
    sharp, keepers = [], []
    waiting, partial_sums = [], []
    rim_north = [jnp.zeros((ROWS, NY), F32)]
    rim_south = [jnp.zeros((ROWS, NY), F32)]
    to_east, to_west, kept = [], [], []

    def ahead(x):
        return jnp.dot(
            forward_ref[:, 0:80],
            feats[:, x * NY : (x + XS) * NY],
            preferred_element_type=F32,
        )

    def finish(x):
        stacked = waiting.pop()
        back = jnp.dot(back_ref[...], stacked, preferred_element_type=F32)
        back = back[0:16] + back[16:32]
        partial_sums.append(
            lax.dot_general(
                feats[0:48, x * NY : (x + XS) * NY],
                stacked,
                (((1,), (1,)), ((), ())),
                preferred_element_type=F32,
            )
        )

        for i in range(XS):
            lane = RIM + x + i
            to_sx, to_sy, bend_x, bend_y, middle = keepers[x + i]
            mine = back[:, i * NY : (i + 1) * NY]
            half_x = 0.5 * (to_sx + mine[0:8])
            half_y = 0.5 * (to_sy + mine[8:16])
            to_north = bend_y + half_y
            to_south = bend_y - half_y
            rim_north[0] = jnp.where(lanes == lane, pltpu.roll(to_north, lane + 1, 1), rim_north[0])
            rim_south[0] = jnp.where(lanes == lane, pltpu.roll(to_south, lane, 1), rim_south[0])
            to_east.append(bend_x + half_x)
            to_west.append(bend_x - half_x)
            kept.append(
                middle
                + jnp.where(lanes == 0, 0.0, pltpu.roll(to_north, 1, 1))
                + jnp.where(lanes == NY - 1, 0.0, pltpu.roll(to_south, NY - 1, 1))
            )
            done = x + i - 1
            if done >= 0:
                total = kept[done] + to_west[done + 1]
                grad_ref[done] = total + to_east[done - 1] if done else total

    before = ahead(0)
    out_sums = jnp.zeros((2 * HID, NY), F32)
    load = load_back = jnp.zeros((ROWS, NY), F32)
    for x in range(NX):
        if x % XS == 0:
            hidden = jnp.tanh(before)
            if x + XS < NX:
                before = ahead(x + XS)
            if x:
                finish(x - XS)
        unit = hidden[:, (x % XS) * NY : (x % XS + 1) * NY]
        weighed = unit * outw
        mixed = by_level(
            jnp.sum(weighed[:HID], 0, keepdims=True), jnp.sum(weighed[HID:], 0, keepdims=True)
        )
        gate = 1.0 / (1.0 + jnp.exp(-mixed))
        nu = jnp.where(moment, 0.24 * gate, 0.0)
        center = lines_ref[x]
        sx, sy, cx, cy = slope_x[x], slope_y[x], curve_x[x], curve_y[x]
        u = by_level(center[0:1], center[1:2])
        v = by_level(center[2:3], center[3:4])
        speed_u = jnp.sqrt(u * u + 0.01)
        speed_v = jnp.sqrt(v * v + 0.01)
        upwind = u * sx + v * sy - 0.5 * (speed_u * cx + speed_v * cy)
        twist = jnp.where(
            row < 2, pltpu.roll(center, 6, 0), jnp.where(moment, -pltpu.roll(center, 2, 0), 0.0)
        )
        explicit = wets[x] * (center - 0.3 * upwind + nu * (cx + cy) + turn * twist)
        rhs_ref[x] = explicit
        load = explicit + right_ref[x - 1] * load if x else explicit
        load_back = load_back + left_ref[x] * explicit if x else explicit
        g = adj[x]
        to_gate = jnp.where(moment, g * (cx + cy) * (0.24 * gate * (1.0 - gate)), 0.0)
        to_gate = to_gate + pltpu.roll(to_gate, 6, 0)
        gate_level = jnp.concatenate(
            [jnp.broadcast_to(to_gate[0:1], (HID, NY)), jnp.broadcast_to(to_gate[1:2], (HID, NY))],
            0,
        )
        pulled = unit * gate_level
        out_sums = out_sums + pulled
        sharp.append(gate_level - unit * pulled)
        along_u = g * (-0.3 * sx + 0.15 * (u / speed_u) * cx)
        along_v = g * (-0.3 * sy + 0.15 * (v / speed_v) * cy)
        along_u = along_u + pltpu.roll(along_u, 4, 0)
        along_u = along_u + pltpu.roll(along_u, 2, 0)
        along_v = along_v + pltpu.roll(along_v, 4, 0)
        along_v = along_v + pltpu.roll(along_v, 2, 0)
        untwist = jnp.where(
            row < 2, along_u - turn * pltpu.roll(g, 6, 0), along_v + turn * pltpu.roll(g, 2, 0)
        )
        bend_x = g * (0.15 * speed_u + nu)
        bend_y = g * (0.15 * speed_v + nu)
        middle = g + jnp.where(moment, untwist, 0.0) - 2.0 * (bend_x + bend_y)
        keepers.append((-0.3 * u * g, -0.3 * v * g, bend_x, bend_y, middle))
        if x % XS == XS - 1:
            waiting.append(jnp.concatenate(split(jnp.concatenate(sharp, 1)), 0))
            sharp = []
    finish(NX - XS)
    grad_ref[NX - 1] = kept[NX - 1] + to_east[NX - 2]
    sums = sum(partial_sums)

    first_own = load_back * jnp.where(
        (row & 2) == 0, own_ref[16:24, :], pltpu.roll(own_ref[16:24, :], 2, 0)
    )
    last_own = load * recip_ref[NX - 1]

    rims_ref[0] = rim_north[0]
    rims_ref[1] = rim_south[0]
    to_last = to_east[NX - 1]
    to_first = to_west[0]

    sums = (sums[:, 0:128] + sums[:, 128:256]) * outr_ref[...]
    pairs_ref[...] = sums[0:16] + sums[16:32]
    features = pairs_ref[pl.ds(0, 8, stride=2), :] + pltpu.roll(
        pairs_ref[pl.ds(1, 8, stride=2), :], HID, 1
    )
    bias = sums[32:40] + pltpu.roll(sums[32:40], HID, 1)
    out_total = jnp.sum(jnp.transpose(out_sums[0:HID] + out_sums[HID:]), 0, keepdims=True)
    packed = pack(features[:, 0:HID], bias[0:1, 0:HID], out_total)
    me = lax.axis_index("gx")
    for j in range(send_ref.shape[0]):
        send_ref[j, 0:8, :] = first_own
        send_ref[j, 8:16, :] = last_own
        send_ref[j, 16:24, :] = packed
        send_ref[j, 24:32, :] = jnp.where(j > me, to_last, to_first)


def share_kernel(
    own_ref,
    other_ref,
    chips_ref,
    second_ref,
    rims_ref,
    rhs_ref,
    right_ref,
    recip_ref,
    send_ref,
    final_ref,
    sides_ref,
):
    me_y = lax.axis_index("gy")
    me = lax.axis_index("gx")
    blocks = second_ref.shape[0]
    lanes = lanes8()
    zero = jnp.zeros((ROWS, NY), F32)
    total = second_ref[0, 16:24, :]
    for j in range(1, blocks):
        total = total + second_ref[j, 16:24, :]
    rim = (lanes >= RIM) & (lanes < RIM + NX)
    upward = jnp.where(rim, rims_ref[0], total)
    downward = jnp.where(rim, rims_ref[1], total)
    for j in range(send_ref.shape[0]):
        send_ref[j] = jnp.where(j > me_y, upward, downward)
    below = second_ref[jnp.maximum(me - 1, 0), 24:32, :]
    above = second_ref[jnp.minimum(me + 1, blocks - 1), 24:32, :]
    sides_ref[0] = jnp.where(me > 0, below, zero)
    sides_ref[1] = jnp.where(me < blocks - 1, above, zero)
    upper = (rows8() & 2) == 0
    first, last = [], []
    for j in range(chips_ref.shape[0]):
        pulls = chips_ref[j, 32:40, :]
        gap = second_ref[2 * j, 8:16, :] - second_ref[2 * j + 1, 0:8, :]
        left_pull = jnp.where(upper, pulls, pltpu.roll(pulls, 2, 0))
        right_pull = jnp.where(upper, pltpu.roll(pulls, 6, 0), pulls)
        first.append(second_ref[2 * j, 0:8, :] - left_pull * gap)
        last.append(second_ref[2 * j + 1, 8:16, :] + right_pull * gap)
    outer = end_fluxes(reduced(chips_ref), first, last, me >> 1)
    left, right, link, _ = middle_face(own_ref, other_ref)
    pair = me & (blocks - 2)
    fluxes = own_fluxes(
        left,
        right,
        link,
        (second_ref[pair, 0:8, :], second_ref[pair + 1, 0:8, :]),
        (second_ref[pair, 8:16, :], second_ref[pair + 1, 8:16, :]),
        outer,
    )

    def keep(x, value):
        final_ref[pl.ds(x, ROWS, stride=NX), :] = value

    own_lines(lambda x: rhs_ref[x], right_ref, recip_ref, fluxes, keep)


def finish_kernel(
    factor,
    third_ref,
    sides_ref,
    grad_ref,
    final_ref,
    final_hbm,
    out_hbm,
    closure_hbm,
    closure_ref,
    out_ref,
    sems,
):
    copies = [pltpu.make_async_copy(final_ref, final_hbm, sems.at[0])]
    copies[0].start()
    me_y = lax.axis_index("gy")
    count_y = third_ref.shape[0]
    lanes = lanes8()
    zero = jnp.zeros((ROWS, NY), F32)
    south = jnp.where(me_y > 0, third_ref[jnp.maximum(me_y - 1, 0)], zero)
    north = jnp.where(me_y < count_y - 1, third_ref[jnp.minimum(me_y + 1, count_y - 1)], zero)
    for x in range(NX):
        value = grad_ref[x]
        if x == 0:
            value = value + sides_ref[0]
        if x == NX - 1:
            value = value + sides_ref[1]
        value = value + jnp.where(lanes == 0, pltpu.roll(south, NY - RIM - x, 1), 0.0)
        value = value + jnp.where(lanes == NY - 1, pltpu.roll(north, NY - 1 - RIM - x, 1), 0.0)
        out_ref[pl.ds(x, ROWS, stride=NX), :] = value
    copies.append(pltpu.make_async_copy(out_ref, out_hbm, sems.at[2]))
    copies[1].start()
    parts = [third_ref[j] for j in range(count_y)]
    while len(parts) > 1:
        parts = [a + b for a, b in zip(parts[::2], parts[1::2])]
    total = parts[0] * factor
    closure_ref[0:8, :] = total[:, 0:HID]
    for n in range(2):
        closure_ref[8 + n : 9 + n, :] = jnp.concatenate(
            [total[2 * n : 2 * n + 1, 96:], total[2 * n + 1 : 2 * n + 2, 96:]], 1
        )
    copies.append(pltpu.make_async_copy(closure_ref, closure_hbm, sems.at[1]))
    copies[2].start()
    for copy in copies:
        copy.wait()


def tile(*shape):
    return jax.ShapeDtypeStruct(shape, F32)


def along_x(up, down, far):
    count = lax.axis_size("gx")
    return tuple(
        lax.ppermute(values, "gx", [(i, (i + shift) % count) for i in range(count)])
        for values, shift in ((up, 2), (down, count - 2), (far, 4))
    )


def keep_in_hbm(values):
    return pltpu.with_memory_space_constraint(values, pltpu.HBM)


def params():
    return pltpu.CompilerParams(vmem_limit_bytes=40 * 1024 * 1024)


def per_device(state, diffusivity, sea_mask, depth_index, closure_in, closure_out, cotangent):
    count_x = lax.axis_size("gx")
    count_y = lax.axis_size("gy")
    lines = tile(NX, ROWS, NY)
    in_hbm = pl.BlockSpec(memory_space=pltpu.HBM)
    in_vmem = pl.BlockSpec(memory_space=pltpu.VMEM)
    ints = jax.ShapeDtypeStruct((NX, NY), jnp.int32)
    fields, first, last, diff, sea, depth, cot = pl.pallas_call(
        load_kernel,
        in_specs=[in_hbm] * 5,
        out_shape=(
            lines,
            tile(ROWS, NY),
            tile(ROWS, NY),
            tile(2 * NX, NY),
            ints,
            ints,
            tile(ROWS * NX, NY),
        ),
        scratch_shapes=[pltpu.VMEM((ROWS * NX, NY), F32), pltpu.SemaphoreType.DMA((5,))],
        compiler_params=params(),
    )(
        keep_in_hbm(state.reshape(ROWS * NX, NY)),
        keep_in_hbm(diffusivity.reshape(2 * NX, NY)),
        keep_in_hbm(sea_mask),
        keep_in_hbm(depth_index),
        keep_in_hbm(cotangent.reshape(ROWS * NX, NY)),
    )
    own, right, recip, left, wets = pl.pallas_call(
        factor_kernel,
        out_shape=(tile(48, NY),) + (lines,) * 4,
        compiler_params=params(),
    )(fields, diff, sea, depth, cot)
    other = lax.ppermute(own, "gx", [(i, i ^ 1) for i in range(count_x)])
    up, down, chip = pl.pallas_call(
        merge_kernel,
        out_shape=(tile(48, NY), tile(48, NY), tile(40, NY)),
        compiler_params=params(),
    )(own, other)
    before, after, far = along_x(up, down, chip)
    low = lax.ppermute(last, "gy", [(i, (i + 1) % count_y) for i in range(count_y)])
    high = lax.ppermute(first, "gy", [((i + 1) % count_y, i) for i in range(count_y)])
    forward, back, outw, outr = pl.pallas_call(
        network_kernel,
        out_shape=(
            jax.ShapeDtypeStruct((2 * HID, 128), BF16),
            jax.ShapeDtypeStruct((32, 256), BF16),
            tile(2 * HID, 128),
            tile(48, 128),
        ),
        compiler_params=params(),
    )(closure_in.T, closure_out.reshape(1, HID))
    chips_x = count_x // 2
    adj, slope_x, curve_x, chips = pl.pallas_call(
        adjoint_kernel,
        out_shape=(lines,) * 3 + (tile(chips_x, 40, NY),),
        compiler_params=params(),
    )(own, other, chip, before, after, far, cot, wets, right, recip, fields)
    feats_shape = jax.ShapeDtypeStruct((80, NX * NY), BF16)
    slope_y, curve_y, feats = pl.pallas_call(
        stencil_kernel, out_shape=(lines,) * 2 + (feats_shape,), compiler_params=params()
    )(low, high, fields, slope_x)
    send, rhs, grad, rims = pl.pallas_call(
        closure_kernel,
        out_shape=(tile(count_x, 32, NY), lines, lines, tile(2, ROWS, NY)),
        scratch_shapes=[pltpu.VMEM((16, 128), F32)],
        compiler_params=params(),
    )(own, fields, wets, adj, slope_x, slope_y, curve_x, curve_y, feats, forward, back, outw, outr, right, recip, left)
    second = lax.all_to_all(send, "gx", 0, 0, tiled=True)
    send, final, sides = pl.pallas_call(
        share_kernel,
        out_shape=(tile(count_y, ROWS, NY), tile(ROWS * NX, NY), tile(2, ROWS, NY)),
        compiler_params=params(),
    )(own, other, chips, second, rims, rhs, right, recip)
    third = lax.all_to_all(send, "gy", 0, 0, tiled=True)
    factor = 1.0 / math.sqrt(2 * NX * count_x * NY * count_y)

    def finish(*refs):
        finish_kernel(factor, *refs)

    final, state_grad, closure_grad = pl.pallas_call(
        finish,
        in_specs=[in_vmem] * 4,
        out_shape=(tile(ROWS * NX, NY), tile(ROWS * NX, NY), tile(10, HID)),
        out_specs=(in_hbm,) * 3,
        scratch_shapes=[
            pltpu.VMEM((10, HID), F32),
            pltpu.VMEM((ROWS * NX, NY), F32),
            pltpu.SemaphoreType.DMA((3,)),
        ],
        compiler_params=params(),
    )(third, sides, grad, final)
    return (final.reshape(state.shape), state_grad.reshape(state.shape), closure_grad.T)


def solution(mesh):
    return jax.shard_map(
        per_device,
        mesh=mesh,
        in_specs=(
            P(None, None, "gx", "gy"),
            P(None, "gx", "gy"),
            P("gx", "gy"),
            P("gx", "gy"),
            P(),
            P(),
            P(None, None, "gx", "gy"),
        ),
        out_specs=(P(None, None, "gx", "gy"), P(None, None, "gx", "gy"), P()),
        check_vma=False,
    )
```
